32 devices in a mesh: dp: 8 (over z, y), mp: 4 (over x, core).
Axes of the slice: x: 2, y: 2, z: 4, core: 2. Of those that a mesh axis runs over, the one named last changes fastest.
Arguments:
- tokens: bfloat16 [17408, 1024], P(('dp', 'mp')), may hold values from -6 to 6
- caption_len: int32 [8, 2], P('dp'), may hold values from 5 to 64, as said below
- row_offset: int32 [8], P('dp'), may hold values from 0 to 118, as said below
- wqkv: bfloat16 [1024, 3, 1024], P(None, None, 'mp'), may hold values from -0.1875 to 0.1875
- qv_bias: bfloat16 [2, 1024], P(None, 'mp'), may hold values from -1.796875 to 1.796875
- wout: bfloat16 [1024, 1024], P('mp'), may hold values from -0.75 to 0.75
- out_bias: bfloat16 [1024], replicated, may hold values from -0.29882812 to 0.29882812
- w1: bfloat16 [1024, 4096], P(None, 'mp'), may hold values from -0.1875 to 0.1875
- b1: bfloat16 [4096], P('mp'), may hold values from -1.796875 to 1.796875
- w2: bfloat16 [4096, 1024], P('mp'), may hold values from -0.09375 to 0.09375
- b2: bfloat16 [1024], replicated, may hold values from -0.59765625 to 0.59765625
- ln_gain: bfloat16 [4, 1024], replicated, may hold values from 0.5 to 1.5
- ln_bias: bfloat16 [4, 1024], replicated, may hold values from -0.59765625 to 0.59765625
- cotangent: bfloat16 [17408, 1024], P(('dp', 'mp')), may hold values from -6 to 6
Outputs:
- mixed: bfloat16 [17408, 1024], P(('dp', 'mp'))
- tokens_grad: bfloat16 [17408, 1024], P(('dp', 'mp'))
- wqkv_grad: float32 [1024, 3, 1024], P(None, None, 'mp')
- qv_bias_grad: float32 [2, 1024], P(None, 'mp')
- wout_grad: float32 [1024, 1024], P('mp')
- out_bias_grad: float32 [1024], replicated
- w1_grad: float32 [1024, 4096], P(None, 'mp')
- b1_grad: float32 [4096], P('mp')
- w2_grad: float32 [4096, 1024], P('mp')
- b2_grad: float32 [1024], replicated
- ln_gain_grad: float32 [4, 1024], replicated
- ln_bias_grad: float32 [4, 1024], replicated
The draws below stay inside these ranges and needn't reach their ends.
Inputs may be any that keep to these rules, and one draw needn't show every extreme that they name: `caption_len`: the largest caption length 64 occurs in every draw. A row's items start at row_offset and follow one another without gaps; the last ends at or before position 2176.
All inputs are finite; a program needn't handle non-finite values.
Results may differ from the reference program's by a relative error of at most 0.019.
Values may be sent and summed in bfloat16 or wider, within the bound.
A program may use at most 192 MiB of HBM per device.

```python
import jax
import jax.numpy as jnp
from jax import lax

D = 1024
HEADS = 16
HEAD = 64
FF = 4096
IMG = 1024
CAP_MIN = 5
CAP_MAX = 64
ITEMS = 2
ROW_LEN = 2176
ROWS = 8
TOKENS = 17408


def caption_table(key):
    picks = jax.random.randint(jax.random.fold_in(key, 11), (ROWS, ITEMS), CAP_MIN, CAP_MAX + 1)
    picks = picks.at[ROWS - 1].set(CAP_MIN)
    picks = picks.at[0, 0].set(CAP_MAX)
    return picks.astype(jnp.int32)


def draw_caption_len(key, part):
    return caption_table(key)


def draw_row_offset(key, part):
    captions = caption_table(key)
    slack = ROW_LEN - ITEMS * IMG - jnp.sum(captions, axis=1)
    drawn_values = jax.random.randint(jax.random.fold_in(key, 23), (ROWS,), 0, 1 << 20)
    offset = drawn_values % (slack + 1)
    offset = offset.at[ROWS - 1].set(slack[ROWS - 1])
    return offset.astype(jnp.int32)


def steps_of(own_key, dims, pieces, least, largest):
    factor_of = 1.0
    for axis_at, shards_of in pieces:
        heights = jax.random.uniform(jax.random.fold_in(jax.random.fold_in(own_key, 6), axis_at), (shards_of,), jnp.float32, least / len(pieces), largest / len(pieces))
        factor_of = factor_of * jnp.repeat(jnp.exp(heights), dims[axis_at] // shards_of).reshape((-1,) + (1,) * (len(dims) - 1 - axis_at))
    return factor_of


def gaussian(key, extent, deviation, reach, pieces=(), held_as=jnp.bfloat16):
    entries = deviation * jax.random.normal(key, extent, jnp.float32)
    if pieces:
        entries = entries * steps_of(key, extent, pieces, -0.22, 0.18)
    return jnp.clip(entries, -reach, reach).astype(held_as)


def setup_inputs(seed: int = 0) -> dict:
    keys = jax.random.split(jax.random.key(seed), 15)
    tokens = gaussian(keys[0], (TOKENS, D), 1.0, 6.0, ((0, 32),))
    caption_len = draw_caption_len(jax.random.fold_in(keys[14], 71), 0)
    row_offset = draw_row_offset(jax.random.fold_in(keys[14], 71), 0)
    wqkv = gaussian(keys[3], (D, 3, D), D ** -0.5, 0.1875, ((2, 4),))
    qv_bias = gaussian(keys[4], (2, D), 0.3, 1.796875, ((1, 4),))
    wout = gaussian(keys[5], (D, D), (D // 16) ** -0.5, 0.75, ((0, 4),))
    out_bias = gaussian(keys[6], (D,), 0.05, 0.29882812)
    w1 = gaussian(keys[7], (D, FF), D ** -0.5, 0.1875, ((1, 4),))
    b1 = gaussian(keys[8], (FF,), 0.3, 1.796875, ((0, 4),))
    w2 = gaussian(keys[9], (FF, D), FF ** -0.5, 0.09375, ((0, 4),))
    b2 = gaussian(keys[10], (D,), 0.1, 0.59765625)
    ln_gain = jnp.clip(1.0 + 0.1 * jax.random.normal(keys[11], (4, D), jnp.float32), 0.5, 1.5).astype(jnp.bfloat16)
    ln_bias = gaussian(keys[12], (4, D), 0.1, 0.59765625)
    cotangent = gaussian(keys[13], (TOKENS, D), 1.0, 6.0, ((0, 32),))
    return {"tokens": tokens, "caption_len": caption_len, "row_offset": row_offset, "wqkv": wqkv, "qv_bias": qv_bias, "wout": wout, "out_bias": out_bias, "w1": w1, "b1": b1, "w2": w2, "b2": b2, "ln_gain": ln_gain, "ln_bias": ln_bias, "cotangent": cotangent}


@jax.custom_vjp
def low(v):
    return lax.optimization_barrier(v.astype(jnp.bfloat16)).astype(jnp.float32)

@jax.custom_vjp
def low_back(v):
    return v

def low_keep(v):
    return (low(v), None)

def low_pass(kept, grad):
    return (grad,)

def back_keep(v):
    return (v, None)

def back_low(kept, grad):
    return (low(grad),)
low.defvjp(low_keep, low_pass)
low_back.defvjp(back_keep, back_low)
eps_norm = 1e-05
masked_value = -1000000000.0
highest = lax.Precision.HIGHEST

def layer_norm(values, gain, shift):
    center = values - lax.optimization_barrier(jnp.mean(values, axis=-1, keepdims=True))
    spread = lax.optimization_barrier(jnp.mean(center * center, axis=-1, keepdims=True))
    return center * lax.rsqrt(spread + eps_norm) * gain + shift

def gelu_tanh(values):
    return jax.nn.gelu(values, approximate=True)

def segment_ids(item_lengths, offset):
    ends = (offset + jnp.cumsum(item_lengths)).astype(jnp.int32)
    bounds = jnp.concatenate([jnp.reshape(offset, (1,)).astype(jnp.int32), ends])
    place = jnp.arange(ROW_LEN, dtype=jnp.int32)
    return lax.optimization_barrier(jnp.sum((place[:, None] >= bounds[None, :]).astype(jnp.int32), axis=1)).astype(jnp.int32)

def row_forward(row_x, segment, wqkv, qv_bias, wout, out_bias, w1, b1, w2, b2, gains, shifts):
    norm_a = low(layer_norm(row_x, gains[0], shifts[0]))
    proj = jnp.dot(norm_a, wqkv.reshape(D, 3 * D), precision=highest).reshape(ROW_LEN, 3, HEADS, HEAD)
    queries = low(low_back(proj[:, 0] + qv_bias[0].reshape(HEADS, HEAD)))
    keys_low = low(low_back(proj[:, 1]))
    values_low = low(low_back(proj[:, 2] + qv_bias[1].reshape(HEADS, HEAD)))
    place = jnp.arange(ROW_LEN, dtype=jnp.int32)
    qblock = ROW_LEN // 4

    def block(start):
        query_block = lax.dynamic_slice_in_dim(queries, start, qblock, 0)
        logits = jnp.einsum('qhd,khd->hqk', query_block, keys_low, precision=highest) * HEAD ** (-0.5)
        block_rows = start + jnp.arange(qblock, dtype=jnp.int32)
        block_segment = lax.dynamic_slice_in_dim(segment, start, qblock)
        allowed = (block_segment[:, None] == segment[None, :]) & (place[None, :] <= block_rows[:, None])
        scores = low_back(jnp.where(allowed[None], logits, masked_value))
        probs = low(jax.nn.softmax(scores, axis=-1))
        return jnp.einsum('hqk,khd->qhd', probs, values_low, precision=highest)
    starts = (jnp.arange(4, dtype=jnp.int32) * qblock).astype(jnp.int32)
    heads_out = lax.map(jax.checkpoint(block), starts)
    heads_out = low(low_back(heads_out.reshape(ROW_LEN, D)))
    attn = low_back(jnp.dot(heads_out, wout, precision=highest) + out_bias)
    hidden = row_x + layer_norm(attn, gains[1], shifts[1])
    norm_c = low(layer_norm(hidden, gains[2], shifts[2]))
    pre_act = low_back(jnp.dot(norm_c, w1, precision=highest) + b1)
    act_low = low(gelu_tanh(pre_act))
    branch = low_back(jnp.dot(act_low, w2, precision=highest) + b2)
    return hidden + layer_norm(branch, gains[3], shifts[3])

def reference(tokens, caption_len, row_offset, wqkv, qv_bias, wout, out_bias, w1, b1, w2, b2, ln_gain, ln_bias, cotangent):
    weights = tuple((item.astype(jnp.float32) for item in (wqkv, qv_bias, wout, out_bias, w1, b1, w2, b2, ln_gain, ln_bias)))
    inputs_rows = tokens.astype(jnp.float32).reshape(ROWS, ROW_LEN, D)
    grads_rows = cotangent.astype(jnp.float32).reshape(ROWS, ROW_LEN, D)

    def one_row(totals, packed):
        row_in, row_grad, captions, offset = packed
        segment = segment_ids(captions + IMG, offset)

        def forward(row_x, *params):
            return row_forward(row_x, segment, *params)
        output, pullback = jax.vjp(forward, row_in, *weights)
        grads = pullback(row_grad)
        totals = tuple((total_item + grad_item for total_item, grad_item in zip(totals, grads[1:])))
        return (totals, (output.astype(jnp.bfloat16), grads[0].astype(jnp.bfloat16)))
    zeros = tuple((jnp.zeros_like(item) for item in weights))
    totals, (outputs, input_grads) = lax.scan(one_row, zeros, (inputs_rows, grads_rows, caption_len, row_offset))
    return (outputs.reshape(TOKENS, D), input_grads.reshape(TOKENS, D), totals[0], totals[1], totals[2], totals[3], totals[4], totals[5], totals[6], totals[7], totals[8], totals[9])
```

```python
import functools
import jax, jax.numpy as jnp
from jax import lax
from jax.experimental import pallas as pl
from jax.experimental.pallas import tpu as pltpu
from jax.sharding import PartitionSpec as P
HEAD=64; IMG=1024; CAP_MIN=5; LANES=128
F32=jnp.float32; BF=jnp.bfloat16
NT=(((1,),(1,)),((),()))
TN=(((0,),(0,)),((),()))

def plan(seq):
    least=IMG+CAP_MIN
    slack=seq-2*least
    lo=least//LANES*LANES
    hi=-(-(seq-least)//LANES)*LANES
    head_pad=-(-slack//LANES)*LANES
    tail_pad=(2*least)//LANES*LANES
    def cut(a,b,step):
        out=[]
        while a<b:
            out.append((a,min(a+step,b))); a=min(a+step,b)
        return out
    return lo,hi,head_pad,tail_pad,cut

def free_of_mask(k0,k1,q0,q1,seq):
    lo,hi,head_pad,tail_pad,_=plan(seq)
    if k1>q0: return False
    if q1<=lo: return k0>=head_pad
    if q0>=hi: return k0>=hi and q1<=tail_pad
    return False

def seg_start(pos,b0,b1,b2):
    return jnp.where(pos>=b2,b2,jnp.where(pos>=b1,b1,jnp.where(pos>=b0,b0,0)))

def fwd_kernel(bounds,q_ref,k_ref,v_ref,o_ref,lse_ref):
    seq,width=q_ref.shape
    h=pl.program_id(0)
    b0,b1,b2=bounds[0],bounds[1],bounds[2]
    lo,hi,_,_,cut=plan(seq)
    lane=lax.broadcasted_iota(jnp.int32,(1,width),1)
    mine=(lane//HEAD)==h
    blocks=[(a,b,0) for a,b in cut(0,lo,256)]+[(a,b,0) for a,b in cut(lo,hi,256)]+[(a,b,lo) for a,b in cut(hi,seq,256)]
    for a,b,start in blocks:
        n=b-a
        qm=jnp.where(mine,q_ref[a:b,:].astype(F32)*HEAD**-0.5,0.0).astype(BF)
        qpos=a+lax.broadcasted_iota(jnp.int32,(n,1),0)
        first=seg_start(qpos,b0,b1,b2)
        parts=[]
        top=None
        for c,d in cut(start,b,128):
            s=lax.dot_general(qm,k_ref[c:d,:],NT,preferred_element_type=F32)
            if not free_of_mask(c,d,a,b,seq):
                kpos=c+lax.broadcasted_iota(jnp.int32,(n,d-c),1)
                s=jnp.where((kpos>=first)&(kpos<=qpos),s,-1e9)
            parts.append(s)
            top=s if top is None else jnp.maximum(top,s)
        m=jnp.max(top,axis=1,keepdims=True)
        es=[jnp.exp(s-m) for s in parts]
        tot=es[0]
        for e in es[1:]: tot=tot+e
        l=jnp.sum(tot,axis=1,keepdims=True)
        p=jnp.concatenate([e.astype(BF) for e in es],axis=1)
        o=jnp.dot(p,v_ref[start:b,:],preferred_element_type=F32)/l
        o_ref[a:b,:]=jnp.where(mine,o.astype(BF),o_ref[a:b,:])
        lse=m+jnp.log(l)
        lse_ref[0,:,a:b]=jnp.broadcast_to(lse,(n,128)).T[0:8,:]

def bwd_kernel(bounds,q_ref,k_ref,v_ref,o_ref,do_ref,lse_ref,dq_ref,dk_ref,dv_ref,qm_s,dom_s,dqt_s,delta_s):
    seq,width=q_ref.shape
    h=pl.program_id(0)
    b0,b1,b2=bounds[0],bounds[1],bounds[2]
    lo,hi,_,_,cut=plan(seq)
    lane=lax.broadcasted_iota(jnp.int32,(1,width),1)
    mine=(lane//HEAD)==h
    qm_s[...]=jnp.where(mine,q_ref[...].astype(F32)*HEAD**-0.5,0.0).astype(BF)
    dom_s[...]=jnp.where(mine,do_ref[...],jnp.zeros((),BF))
    ones=jnp.ones((8,width),F32)
    for a,b in cut(0,seq,256):
        prod=dom_s[a:b,:].astype(F32)*o_ref[a:b,:].astype(F32)
        delta_s[:,a:b]=lax.dot_general(ones,prod,NT,preferred_element_type=F32,precision=lax.Precision.HIGHEST)
    dqt_s[...]=jnp.zeros_like(dqt_s)
    blocks=[(a,b,hi) for a,b in cut(0,lo,256)]+[(a,b,seq) for a,b in cut(lo,hi,256)]+[(a,b,seq) for a,b in cut(hi,seq,256)]
    for a,b,stop in blocks:
        n=b-a
        kk=k_ref[a:b,:]; vv=v_ref[a:b,:]
        kpos=a+lax.broadcasted_iota(jnp.int32,(n,1),0)
        kh=jnp.where(mine,kk,jnp.zeros((),BF))
        pts=[];dsts=[]
        for c,d in cut(a,stop,128):
            st=lax.dot_general(kk,qm_s[c:d,:],NT,preferred_element_type=F32)
            pt=jnp.exp(st-lse_ref[0,0:1,c:d])
            if not free_of_mask(a,b,c,d,seq):
                qpos=c+lax.broadcasted_iota(jnp.int32,(1,d-c),1)
                first=seg_start(qpos,b0,b1,b2)
                pt=jnp.where((kpos>=first)&(kpos<=qpos),pt,0.0)
            dpt=lax.dot_general(vv,dom_s[c:d,:],NT,preferred_element_type=F32)
            dst=pt*(dpt-delta_s[0:1,c:d])
            pts.append(pt.astype(BF)); dsts.append(dst.astype(BF))
        pt=jnp.concatenate(pts,axis=1); dst=jnp.concatenate(dsts,axis=1)
        dv=jnp.dot(pt,dom_s[a:stop,:],preferred_element_type=F32)
        dk=jnp.dot(dst,qm_s[a:stop,:],preferred_element_type=F32)
        dv_ref[a:b,:]=jnp.where(mine,dv.astype(BF),dv_ref[a:b,:])
        dk_ref[a:b,:]=jnp.where(mine,dk.astype(BF),dk_ref[a:b,:])
        dqt_s[:,a:stop]+=lax.dot_general(kh,dst,TN,preferred_element_type=F32)
    for a,b in cut(0,seq,128):
        dq=(dqt_s[:,a:b]*HEAD**-0.5).T
        dq_ref[a:b,:]=jnp.where(mine,dq.astype(BF),dq_ref[a:b,:])

def attn_fwd(bounds,q,k,v):
    seq,width=q.shape; H=width//HEAD
    full=pl.BlockSpec((seq,width),lambda h:(0,0))
    return pl.pallas_call(fwd_kernel,grid=(H,),
        in_specs=[pl.BlockSpec(memory_space=pltpu.SMEM),full,full,full],
        out_specs=[full,pl.BlockSpec((1,8,seq),lambda h:(h,0,0))],
        out_shape=[jax.ShapeDtypeStruct((seq,width),BF),jax.ShapeDtypeStruct((H,8,seq),F32)],
        compiler_params=pltpu.CompilerParams(vmem_limit_bytes=56<<20),name="attn_fwd")(bounds,q,k,v)

def attn_bwd(bounds,q,k,v,o,do,lse):
    seq,width=q.shape; H=width//HEAD
    full=pl.BlockSpec((seq,width),lambda h:(0,0))
    sh=jax.ShapeDtypeStruct((seq,width),BF)
    return pl.pallas_call(bwd_kernel,grid=(H,),
        in_specs=[pl.BlockSpec(memory_space=pltpu.SMEM),full,full,full,full,full,pl.BlockSpec((1,8,seq),lambda h:(h,0,0))],
        out_specs=[full,full,full],out_shape=[sh,sh,sh],
        scratch_shapes=[pltpu.VMEM((seq,width),BF),pltpu.VMEM((seq,width),BF),pltpu.VMEM((width,seq),F32),pltpu.VMEM((8,seq),F32)],
        compiler_params=pltpu.CompilerParams(vmem_limit_bytes=56<<20),name="attn_bwd")(bounds,q,k,v,o,do,lse)

eps_norm = 1e-05


def layer_norm(values, gain, shift):
    center = values - jnp.mean(values, axis=-1, keepdims=True)
    spread = jnp.mean(center * center, axis=-1, keepdims=True)
    return center * lax.rsqrt(spread + eps_norm) * gain + shift


def gelu_tanh(values):
    return jax.nn.gelu(values, approximate=True)


def swap(values, axis, mask):
    size = lax.axis_size(axis)
    return lax.ppermute(values, axis, [(i, i ^ mask) for i in range(size)])


def masks_of(axis):
    size = lax.axis_size(axis)
    out = []
    step = size // 2
    while step:
        out.append(step)
        step //= 2
    return out


def gather_rel(block, axis):
    have = {0: block}
    for mask in masks_of(axis):
        have.update({j ^ mask: swap(v, axis, mask) for j, v in list(have.items())})
    return jnp.stack([have[j] for j in range(lax.axis_size(axis))])


def scatter_rel(parts, axis):
    have = {j: parts[j] for j in range(parts.shape[0])}
    for mask in reversed(masks_of(axis)):
        got = {j: swap(have[j].astype(BF), axis, mask) for j in have if j & mask}
        have = {j: have[j] + got[j ^ mask].astype(F32) for j in have if not j & mask}
    return have[0]


def reduce_all(values, axis):
    me = lax.axis_index(axis)
    masks = list(reversed(masks_of(axis)))
    rows = values.shape[0]
    for mask in masks:
        rows //= 2
        bit = (me // mask) % 2
        keep = lax.dynamic_slice_in_dim(values, bit * rows, rows, 0)
        send = lax.dynamic_slice_in_dim(values, (1 - bit) * rows, rows, 0)
        values = keep + swap(send.astype(BF), axis, mask).astype(F32)
    low = values.astype(BF)
    for mask in reversed(masks):
        bit = (me // mask) % 2
        got = swap(low, axis, mask)
        both = jnp.concatenate([low, got], axis=0)
        flipped = jnp.concatenate([got, low], axis=0)
        low = jnp.where(bit == 0, both, flipped)
    return low.astype(F32)


def sum_small(values, axes):
    for axis in axes:
        for mask in masks_of(axis):
            values = values + swap(values, axis, mask)
    return values


def shards(
    tokens, caption_len, row_offset, wqkv, qv_bias, wout, out_bias, w1, b1, w2, b2, ln_gain, ln_bias, cotangent,
):
    local_rows, width = tokens.shape
    size = lax.axis_size("mp")
    seq_len = local_rows * size
    head_part = wqkv.shape[2]
    gains = ln_gain.astype(F32)
    shifts = ln_bias.astype(F32)
    me = lax.axis_index("mp")

    def pick(blocks):
        return jnp.concatenate(
            [lax.dynamic_index_in_dim(blocks, me ^ j, 0, keepdims=True) for j in range(size)], axis=0
        )

    first = row_offset[0]
    second = first + caption_len[0, 0] + IMG
    third = second + caption_len[0, 1] + IMG
    bounds = jnp.stack([first, second, third]).astype(jnp.int32)

    def sort(rel):
        return pick(rel).reshape((seq_len,) + rel.shape[2:])

    def rel_of(rows):
        return pick(rows.reshape((size, local_rows) + rows.shape[1:]))

    rows_in = tokens.astype(F32)
    norm_a, pull_a = jax.vjp(layer_norm, rows_in, gains[0], shifts[0])
    attn_full = sort(gather_rel(norm_a.astype(BF), "mp"))
    w_in = wqkv.reshape(width, 3 * head_part)
    projected = jnp.dot(attn_full, w_in, preferred_element_type=F32)
    bias3 = jnp.concatenate([qv_bias[0], jnp.zeros_like(qv_bias[0]), qv_bias[1]]).astype(F32)
    projected = (projected + bias3).astype(BF)
    queries, keys, values = [projected[:, i * head_part:(i + 1) * head_part] for i in range(3)]
    head_low, lse = attn_fwd(bounds, queries, keys, values)
    head_rel = rel_of(head_low)
    attn_out = scatter_rel(jnp.dot(head_rel, wout, preferred_element_type=F32), "mp") + out_bias.astype(F32)
    norm_b, pull_b = jax.vjp(layer_norm, attn_out, gains[1], shifts[1])
    hidden_rows = rows_in + norm_b
    norm_c, pull_c = jax.vjp(layer_norm, hidden_rows, gains[2], shifts[2])
    mlp_rel = gather_rel(norm_c.astype(BF), "mp")
    mlp_full = mlp_rel.reshape(seq_len, width)
    pre_act = jnp.dot(mlp_full, w1, preferred_element_type=F32) + b1.astype(F32)
    activated, gelu_pull = jax.vjp(gelu_tanh, pre_act)
    act_low = activated.astype(BF)
    branch = scatter_rel(
        jnp.dot(act_low, w2, preferred_element_type=F32).reshape(size, local_rows, width), "mp"
    ) + b2.astype(F32)
    norm_d, pull_d = jax.vjp(layer_norm, branch, gains[3], shifts[3])
    mixed = (hidden_rows + norm_d).astype(BF)
    grad_out = cotangent.astype(F32)
    grad_branch, gain_d, shift_d = pull_d(grad_out)
    branch_low = grad_branch.astype(BF)
    b2_part = jnp.sum(branch_low.astype(F32), axis=0)
    branch_full = gather_rel(branch_low, "mp").reshape(seq_len, width)
    w2_grad = jnp.einsum("tf,td->fd", act_low, branch_full, preferred_element_type=F32)
    w2_grad = reduce_all(w2_grad, "dp")
    grad_act = jnp.einsum("td,fd->tf", branch_full, w2, preferred_element_type=F32)
    grad_pre = gelu_pull(grad_act)[0].astype(BF)
    b1_grad = jnp.sum(grad_pre.astype(F32), axis=0)
    w1_grad = jnp.einsum("td,tf->df", mlp_full, grad_pre, preferred_element_type=F32)
    w1_grad = reduce_all(w1_grad, "dp")
    grad_norm_c = scatter_rel(
        jnp.einsum("tf,df->td", grad_pre, w1, preferred_element_type=F32).reshape(size, local_rows, width), "mp"
    )
    grad_hidden_c, gain_c, shift_c = pull_c(grad_norm_c)
    grad_hidden = grad_out + grad_hidden_c
    grad_attn, gain_b, shift_b = pull_b(grad_hidden)
    attn_grad_low = grad_attn.astype(BF)
    out_bias_part = jnp.sum(attn_grad_low.astype(F32), axis=0)
    attn_grad_full = sort(gather_rel(attn_grad_low, "mp"))
    wout_grad = jnp.einsum("tc,td->cd", head_low, attn_grad_full, preferred_element_type=F32)
    wout_grad = reduce_all(wout_grad, "dp")
    grad_heads = jnp.einsum("td,cd->tc", attn_grad_full, wout, preferred_element_type=F32).astype(BF)
    grads = attn_bwd(bounds, queries, keys, values, head_low, grad_heads, lse)
    grad_proj = jnp.concatenate(grads, axis=1)
    part_sums = jnp.sum(grad_proj.astype(F32), axis=0).reshape(3, head_part)
    qv_part = jnp.stack([part_sums[0], part_sums[2]])
    wqkv_grad = jnp.einsum("td,tc->dc", attn_full, grad_proj, preferred_element_type=F32)
    wqkv_grad = reduce_all(wqkv_grad, "dp").reshape(width, 3, head_part)
    grad_rel = rel_of(grad_proj)
    grad_norm_a = scatter_rel(jnp.einsum("jtc,dc->jtd", grad_rel, w_in, preferred_element_type=F32), "mp")
    grad_rows_a, gain_a, shift_a = pull_a(grad_norm_a)
    tokens_grad = (grad_hidden + grad_rows_a).astype(BF)
    own_sums = sum_small(jnp.concatenate([qv_part.reshape(-1), b1_grad]), ("dp",))
    qv_sum = own_sums[: 2 * head_part].reshape(2, head_part)
    b1_sum = own_sums[2 * head_part:]
    stack = jnp.stack(
        [gain_a, gain_b, gain_c, gain_d, shift_a, shift_b, shift_c, shift_d, out_bias_part, b2_part]
    )
    stack = sum_small(stack, ("mp", "dp"))
    return (
        mixed, tokens_grad, wqkv_grad, qv_sum, wout_grad, stack[8], w1_grad, b1_sum, w2_grad, stack[9],
        stack[0:4], stack[4:8],
    )


def solution(mesh):
    rows = P(("dp", "mp"), None)
    placed = (
        rows, P("dp", None), P("dp"), P(None, None, "mp"), P(None, "mp"), P("mp", None), P(), P(None, "mp"),
        P("mp"), P("mp", None), P(), P(), P(), rows,
    )
    return jax.shard_map(
        shards,
        mesh=mesh,
        in_specs=placed,
        out_specs=(
            rows, rows, P(None, None, "mp"), P(None, "mp"), P("mp", None), P(), P(None, "mp"), P("mp"),
            P("mp", None), P(), P(), P(),
        ),
        check_vma=False,
    )
```

```python
import functools
import jax, jax.numpy as jnp
from jax import lax
from jax.experimental import pallas as pl
from jax.experimental.pallas import tpu as pltpu
from jax.sharding import PartitionSpec as P
HEAD=64; IMG=1024; CAP_MIN=5; LANES=128
F32=jnp.float32; BF=jnp.bfloat16
MESH=pl.DeviceIdType.MESH
NT=(((1,),(1,)),((),()))
TN=(((0,),(0,)),((),()))

def plan(seq):
    least=IMG+CAP_MIN
    slack=seq-2*least
    lo=least//LANES*LANES
    hi=-(-(seq-least)//LANES)*LANES
    head_pad=-(-slack//LANES)*LANES
    tail_pad=(2*least)//LANES*LANES
    def cut(a,b,step):
        out=[]
        while a<b:
            out.append((a,min(a+step,b))); a=min(a+step,b)
        return out
    return lo,hi,head_pad,tail_pad,cut

def free_of_mask(k0,k1,q0,q1,seq):
    lo,hi,head_pad,tail_pad,_=plan(seq)
    if k1>q0: return False
    if q1<=lo: return k0>=head_pad
    if q0>=hi: return k0>=hi and q1<=tail_pad
    return False

def seg_start(pos,b0,b1,b2):
    return jnp.where(pos>=b2,b2,jnp.where(pos>=b1,b1,jnp.where(pos>=b0,b0,0)))

def fwd_kernel(bounds,q_ref,k_ref,v_ref,o_ref,lse_ref):
    seq,width=q_ref.shape
    h=pl.program_id(0)
    b0,b1,b2=bounds[0],bounds[1],bounds[2]
    lo,hi,_,_,cut=plan(seq)
    lane=lax.broadcasted_iota(jnp.int32,(1,width),1)
    mine=(lane//HEAD)==h
    blocks=[(a,b,0) for a,b in cut(0,lo,256)]+[(a,b,0) for a,b in cut(lo,hi,256)]+[(a,b,lo) for a,b in cut(hi,seq,256)]
    for a,b,start in blocks:
        n=b-a
        qm=jnp.where(mine,q_ref[a:b,:].astype(F32)*HEAD**-0.5,0.0).astype(BF)
        qpos=a+lax.broadcasted_iota(jnp.int32,(n,1),0)
        first=seg_start(qpos,b0,b1,b2)
        parts=[]
        top=None
        for c,d in cut(start,b,128):
            s=lax.dot_general(qm,k_ref[c:d,:],NT,preferred_element_type=F32)
            if not free_of_mask(c,d,a,b,seq):
                kpos=c+lax.broadcasted_iota(jnp.int32,(n,d-c),1)
                s=jnp.where((kpos>=first)&(kpos<=qpos),s,-1e9)
            parts.append(s)
            top=s if top is None else jnp.maximum(top,s)
        m=jnp.max(top,axis=1,keepdims=True)
        es=[jnp.exp(s-m) for s in parts]
        tot=es[0]
        for e in es[1:]: tot=tot+e
        l=jnp.sum(tot,axis=1,keepdims=True)
        p=jnp.concatenate([e.astype(BF) for e in es],axis=1)
        o=jnp.dot(p,v_ref[start:b,:],preferred_element_type=F32)/l
        o_ref[a:b,:]=jnp.where(mine,o.astype(BF),o_ref[a:b,:])
        lse=m+jnp.log(l)
        lse_ref[0,:,a:b]=jnp.broadcast_to(lse,(n,128)).T[0:8,:]

def bwd_kernel(bounds,q_ref,k_ref,v_ref,o_ref,do_ref,lse_ref,dq_ref,dk_ref,dv_ref,qm_s,dom_s,dqt_s,delta_s):
    seq,width=q_ref.shape
    h=pl.program_id(0)
    b0,b1,b2=bounds[0],bounds[1],bounds[2]
    lo,hi,_,_,cut=plan(seq)
    lane=lax.broadcasted_iota(jnp.int32,(1,width),1)
    mine=(lane//HEAD)==h
    qm_s[...]=jnp.where(mine,q_ref[...].astype(F32)*HEAD**-0.5,0.0).astype(BF)
    dom_s[...]=jnp.where(mine,do_ref[...],jnp.zeros((),BF))
    ones=jnp.ones((8,width),F32)
    for a,b in cut(0,seq,256):
        prod=dom_s[a:b,:].astype(F32)*o_ref[a:b,:].astype(F32)
        delta_s[:,a:b]=lax.dot_general(ones,prod,NT,preferred_element_type=F32,precision=lax.Precision.HIGHEST)
    dqt_s[...]=jnp.zeros_like(dqt_s)
    blocks=[(a,b,hi) for a,b in cut(0,lo,256)]+[(a,b,seq) for a,b in cut(lo,hi,256)]+[(a,b,seq) for a,b in cut(hi,seq,256)]
    for a,b,stop in blocks:
        n=b-a
        kk=k_ref[a:b,:]; vv=v_ref[a:b,:]
        kpos=a+lax.broadcasted_iota(jnp.int32,(n,1),0)
        kh=jnp.where(mine,kk,jnp.zeros((),BF))
        pts=[];dsts=[]
        for c,d in cut(a,stop,128):
            st=lax.dot_general(kk,qm_s[c:d,:],NT,preferred_element_type=F32)
            pt=jnp.exp(st-lse_ref[0,0:1,c:d])
            if not free_of_mask(a,b,c,d,seq):
                qpos=c+lax.broadcasted_iota(jnp.int32,(1,d-c),1)
                first=seg_start(qpos,b0,b1,b2)
                pt=jnp.where((kpos>=first)&(kpos<=qpos),pt,0.0)
            dpt=lax.dot_general(vv,dom_s[c:d,:],NT,preferred_element_type=F32)
            dst=pt*(dpt-delta_s[0:1,c:d])
            pts.append(pt.astype(BF)); dsts.append(dst.astype(BF))
        pt=jnp.concatenate(pts,axis=1); dst=jnp.concatenate(dsts,axis=1)
        dv=jnp.dot(pt,dom_s[a:stop,:],preferred_element_type=F32)
        dk=jnp.dot(dst,qm_s[a:stop,:],preferred_element_type=F32)
        dv_ref[a:b,:]=jnp.where(mine,dv.astype(BF),dv_ref[a:b,:])
        dk_ref[a:b,:]=jnp.where(mine,dk.astype(BF),dk_ref[a:b,:])
        dqt_s[:,a:stop]+=lax.dot_general(kh,dst,TN,preferred_element_type=F32)
    for a,b in cut(0,seq,128):
        dq=(dqt_s[:,a:b]*HEAD**-0.5).T
        dq_ref[a:b,:]=jnp.where(mine,dq.astype(BF),dq_ref[a:b,:])

def attn_fwd(bounds,q,k,v):
    seq,width=q.shape; H=width//HEAD
    full=pl.BlockSpec((seq,width),lambda h:(0,0))
    return pl.pallas_call(fwd_kernel,grid=(H,),
        in_specs=[pl.BlockSpec(memory_space=pltpu.SMEM),full,full,full],
        out_specs=[full,pl.BlockSpec((1,8,seq),lambda h:(h,0,0))],
        out_shape=[jax.ShapeDtypeStruct((seq,width),BF),jax.ShapeDtypeStruct((H,8,seq),F32)],
        compiler_params=pltpu.CompilerParams(vmem_limit_bytes=56<<20),name="attn_fwd")(bounds,q,k,v)

def attn_bwd(bounds,q,k,v,o,do,lse):
    seq,width=q.shape; H=width//HEAD
    full=pl.BlockSpec((seq,width),lambda h:(0,0))
    sh=jax.ShapeDtypeStruct((seq,width),BF)
    return pl.pallas_call(bwd_kernel,grid=(H,),
        in_specs=[pl.BlockSpec(memory_space=pltpu.SMEM),full,full,full,full,full,pl.BlockSpec((1,8,seq),lambda h:(h,0,0))],
        out_specs=[full,full,full],out_shape=[sh,sh,sh],
        scratch_shapes=[pltpu.VMEM((seq,width),BF),pltpu.VMEM((seq,width),BF),pltpu.VMEM((width,seq),F32),pltpu.VMEM((8,seq),F32)],
        compiler_params=pltpu.CompilerParams(vmem_limit_bytes=56<<20),name="attn_bwd")(bounds,q,k,v,o,do,lse)

eps_norm = 1e-05


def layer_norm(values, gain, shift):
    center = values - jnp.mean(values, axis=-1, keepdims=True)
    spread = jnp.mean(center * center, axis=-1, keepdims=True)
    return center * lax.rsqrt(spread + eps_norm) * gain + shift


def gelu_tanh(values):
    return jax.nn.gelu(values, approximate=True)


def swap(values, axis, mask):
    size = lax.axis_size(axis)
    return lax.ppermute(values, axis, [(i, i ^ mask) for i in range(size)])


def masks_of(axis):
    size = lax.axis_size(axis)
    out = []
    step = size // 2
    while step:
        out.append(step)
        step //= 2
    return out


def gather_rel(block, axis):
    have = {0: block}
    for mask in masks_of(axis):
        have.update({j ^ mask: swap(v, axis, mask) for j, v in list(have.items())})
    return jnp.stack([have[j] for j in range(lax.axis_size(axis))])


def scatter_rel(parts, axis):
    have = {j: parts[j] for j in range(parts.shape[0])}
    for mask in reversed(masks_of(axis)):
        got = {j: swap(have[j].astype(BF), axis, mask) for j in have if j & mask}
        have = {j: have[j] + got[j ^ mask].astype(F32) for j in have if not j & mask}
    return have[0]


def reduce_all(values, axis):
    me = lax.axis_index(axis)
    masks = list(reversed(masks_of(axis)))
    rows = values.shape[0]
    for mask in masks:
        rows //= 2
        bit = (me // mask) % 2
        keep = lax.dynamic_slice_in_dim(values, bit * rows, rows, 0)
        send = lax.dynamic_slice_in_dim(values, (1 - bit) * rows, rows, 0)
        values = keep + swap(send.astype(BF), axis, mask).astype(F32)
    low = values.astype(BF)
    for mask in reversed(masks):
        bit = (me // mask) % 2
        got = swap(low, axis, mask)
        both = jnp.concatenate([low, got], axis=0)
        flipped = jnp.concatenate([got, low], axis=0)
        low = jnp.where(bit == 0, both, flipped)
    return low.astype(F32)


def sum_small(values, axes):
    for axis in axes:
        for mask in masks_of(axis):
            values = values + swap(values, axis, mask)
    return values


SLOT = {1: 0, 3: 1, 2: 2, 0: 3}
TILE = 256


def spans_of(rows):
    units = rows // 16
    sizes = [16 * (units // 4 + (1 if i < units % 4 else 0)) for i in range(4)]
    edges = [sum(sizes[:i]) for i in range(5)]
    return [(edges[i], edges[i + 1]) for i in range(4)]


def fold8(values):
    rows, cols = values.shape
    return jnp.sum(values.reshape(rows // 8, 8, cols), axis=0)


def norm_stats(values):
    center = values - jnp.mean(values, axis=-1, keepdims=True)
    inv = lax.rsqrt(jnp.mean(center * center, axis=-1, keepdims=True) + eps_norm)
    return center * inv, inv


def norm_pull(upstream, gain, unit, inv):
    scaled = upstream * gain
    first = jnp.mean(scaled, axis=-1, keepdims=True)
    second = jnp.mean(scaled * unit, axis=-1, keepdims=True)
    return (scaled - first - unit * second) * inv


def mid_kernel(
    heads, tokens, cot, wout, w1, w2, b1, vec,
    mixed, ghid, ghead, w2g, w1g, wog, sums, b1sum,
    hs, mlp, act, dgel, brn, gpre, u1, u2, hid, r1, r2, pbuf, cs, cr, xs, xr, acc, b1acc, stage,
    send, recv, local_sem,
):
    local, width = tokens.shape
    hidden_units = w1.shape[1]
    spans = spans_of(local)
    count = len(spans)
    dp, me = lax.axis_index("dp"), lax.axis_index("mp")
    mx, mc = me // 2, me % 2
    peer_core = (dp, mx * 2 + 1 - mc)
    peer_x = (dp, (1 - mx) * 2 + mc)
    owner = {0: me, 1: mx * 2 + 1 - mc, 2: (1 - mx) * 2 + mc, 3: (1 - mx) * 2 + 1 - mc}

    barrier = pltpu.get_barrier_semaphore()
    for peer in (peer_core, peer_x):
        pl.semaphore_signal(barrier, inc=1, device_id=peer, device_id_type=MESH)
    pl.semaphore_wait(barrier, 2)

    def remote(src, dst, phase, kind, c, device):
        i = (phase * 5 + kind) * count + c
        return pltpu.make_async_remote_copy(
            src_ref=src, dst_ref=dst, send_sem=send.at[i], recv_sem=recv.at[i], device_id=device, device_id_type=MESH
        )

    def core_copy(phase, c):
        lo, hi = spans[c]
        rows = pl.ds(2 * lo, 2 * (hi - lo))
        return remote(cs.at[rows], cr.at[rows], phase, 0, c, peer_core)

    def x_copy(phase, c):
        lo, hi = spans[c]
        rows = pl.ds(lo, hi - lo)
        return remote(xs.at[rows], xr.at[rows], phase, 1, c, peer_x)

    def block(c, j):
        lo, hi = spans[c]
        return pl.ds(4 * lo + SLOT[j] * (hi - lo), hi - lo)

    def gather_copies(full, phase, c):
        own = full.at[block(c, 0)]
        return (
            remote(own, full.at[block(c, 2)], phase, 2, c, peer_x),
            remote(own, full.at[block(c, 1)], phase, 3, c, peer_core),
            remote(full.at[block(c, 2)], full.at[block(c, 3)], phase, 4, c, peer_core),
        )

    def tiles(c):
        lo, hi = spans[c]
        step = next(t for t in (48, 64, 32, 16) if (hi - lo) % t == 0)
        return (hi - lo) // step, step

    def start_gather(full, phase, c):
        first, second, _ = gather_copies(full, phase, c)
        first.start()
        second.start()

    def forward(full, phase, c):
        first, second, third = gather_copies(full, phase, c)
        first.wait_recv()
        third.start()
        second.wait_recv()
        third.wait_recv()

    def partial_products(lhs, rhs, turned, phase, c, half, wide=TILE):
        lo, hi = spans[c]
        r = hi - lo
        rows = pl.ds(4 * lo + half * 2 * r, 2 * r)
        out = pl.ds(2 * lo, 2 * r)

        def body(n, carry):
            cols = pl.ds(pl.multiple_of(n * wide, wide), wide)
            if turned:
                part = lax.dot_general(lhs[rows, :], rhs[cols, :], NT, preferred_element_type=F32)
            else:
                part = jnp.dot(lhs[rows, :], rhs[:, cols], preferred_element_type=F32)
            if half == 0:
                cs[out, cols] = part.astype(BF)
            else:
                pbuf[out, cols] = part
            return carry

        lax.fori_loop(0, width // wide, body, 0)

    def pass_on(phase, c):
        lo, hi = spans[c]
        r = hi - lo
        core_copy(phase, c).wait_recv()
        if phase:
            x_copy(phase - 1, c).wait_send()
        xs[lo:hi, :] = (pbuf[2 * lo:2 * lo + r, :] + cr[2 * lo + r:2 * lo + 2 * r, :].astype(F32)).astype(BF)
        x_copy(phase, c).start()

    def own_total(c, i, step):
        lo, hi = spans[c]
        r = hi - lo
        kept = pl.ds(pl.multiple_of(2 * lo + r + i * step, 16), step)
        near = pl.ds(pl.multiple_of(2 * lo + i * step, 16), step)
        far = pl.ds(pl.multiple_of(lo + i * step, 16), step)
        return far, pbuf[kept, :] + cr[near, :].astype(F32) + xr[far, :].astype(F32)

    def row(i):
        return vec[i:i + 1, :]

    acc[...] = jnp.zeros_like(acc)
    b1acc[...] = jnp.zeros_like(b1acc)

    def add(i, values):
        acc[8 * i:8 * i + 8, :] += fold8(values)

    def project(c):
        lo, hi = spans[c]
        for j in (1, 3, 2, 0):
            start = pl.multiple_of(owner[j] * local + lo, 16)
            hs[block(c, j), :] = heads[pl.ds(start, hi - lo), :]
        partial_products(hs, wout, False, 0, c, 0)
        core_copy(0, c).start()
        partial_products(hs, wout, False, 0, c, 1)

    project(0)
    for c in range(count):
        if c + 1 < count:
            project(c + 1)
        pass_on(0, c)

    for c in range(count):
        x_copy(0, c).wait_recv()
        lo, hi = spans[c]
        trips, step = tiles(c)

        def norms(i, carry):
            rows, total = own_total(c, i, step)
            unit, inv = norm_stats(total + row(0))
            u1[rows, :] = unit
            r1[rows, :] = jnp.broadcast_to(inv, (step, LANES))
            hidden = tokens[rows, :].astype(F32) + unit * row(2) + row(3)
            hid[rows, :] = hidden
            unit, inv = norm_stats(hidden)
            u2[rows, :] = unit
            r2[rows, :] = jnp.broadcast_to(inv, (step, LANES))
            dst = pl.ds(pl.multiple_of(4 * lo + SLOT[0] * (hi - lo) + i * step, 16), step)
            mlp[dst, :] = (unit * row(4) + row(5)).astype(BF)
            return carry

        lax.fori_loop(0, trips, norms, 0)
        start_gather(mlp, 0, c)

    for c in range(count):
        lo, hi = spans[c]
        r = hi - lo
        forward(mlp, 0, c)
        core_copy(0, c).wait_send()
        for half in range(2):
            rows = pl.ds(4 * lo + half * 2 * r, 2 * r)

            def units(n, carry):
                cols = pl.ds(pl.multiple_of(n * TILE, TILE), TILE)
                pre = jnp.dot(mlp[rows, :], w1[:, cols], preferred_element_type=F32) + b1[:, cols]
                square = pre * pre
                inner = (0.7978845608028654 * pre) * (1.0 + 0.044715 * square)
                tanh = jnp.tanh(inner)
                plus = 0.5 * (1.0 + tanh)
                act[rows, cols] = (pre * plus).astype(BF)
                slope = plus + (0.5 * pre) * (1.0 - tanh * tanh) * (
                    0.7978845608028654 * (1.0 + (3 * 0.044715) * square)
                )
                dgel[rows, cols] = slope.astype(BF)
                return carry

            lax.fori_loop(0, hidden_units // TILE, units, 0)
            partial_products(act, w2, False, 1, c, half)
            if half == 0:
                core_copy(1, c).start()
        pass_on(1, c)

    for c in range(count):
        x_copy(1, c).wait_recv()
        lo, hi = spans[c]
        trips, step = tiles(c)

        def last(i, carry):
            rows, total = own_total(c, i, step)
            unit, inv = norm_stats(total + row(1))
            mixed[rows, :] = (hid[rows, :] + unit * row(6) + row(7)).astype(BF)
            grad = cot[rows, :].astype(F32)
            add(2, grad * unit)
            add(5, grad)
            low = norm_pull(grad, row(6), unit, inv).astype(BF)
            add(7, low.astype(F32))
            dst = pl.ds(pl.multiple_of(4 * lo + SLOT[0] * (hi - lo) + i * step, 16), step)
            brn[dst, :] = low
            return carry

        lax.fori_loop(0, trips, last, 0)
        start_gather(brn, 1, c)

    for c in range(count):
        lo, hi = spans[c]
        r = hi - lo
        forward(brn, 1, c)
        core_copy(1, c).wait_send()
        for half in range(2):
            rows = pl.ds(4 * lo + half * 2 * r, 2 * r)

            def slopes(n, carry):
                cols = pl.ds(pl.multiple_of(n * TILE, TILE), TILE)
                grad = lax.dot_general(brn[rows, :], w2[cols, :], NT, preferred_element_type=F32)
                low = (grad * dgel[rows, cols].astype(F32)).astype(BF)
                gpre[rows, cols] = low
                b1acc[:, cols] += fold8(low.astype(F32))
                return carry

            lax.fori_loop(0, hidden_units // TILE, slopes, 0)
            partial_products(gpre, w1, True, 2, c, half)
            if half == 0:
                core_copy(2, c).start()
        pass_on(2, c)

    def weight_grad(lhs, rhs, dst, first_slot):
        trips = lhs.shape[1] // TILE

        def out(n, slot):
            return pltpu.make_async_copy(
                stage.at[slot], dst.at[pl.ds(n * TILE, TILE)], local_sem.at[first_slot + n]
            )

        for n in range(trips):
            if n >= 2:
                out(n - 2, n % 2).wait()
            stage[n % 2] = lax.dot_general(
                lhs[:, n * TILE:(n + 1) * TILE], rhs[...], TN, preferred_element_type=F32
            )
            out(n, n % 2).start()
        for n in range(max(0, trips - 2), trips):
            out(n, n % 2).wait()

    weight_grad(act, brn, w2g, 0)

    for c in range(count):
        x_copy(2, c).wait_recv()
        lo, hi = spans[c]
        trips, step = tiles(c)

        def pulls(i, carry):
            rows, total = own_total(c, i, step)
            unit = u2[rows, :]
            add(1, total * unit)
            add(4, total)
            grad = cot[rows, :].astype(F32) + norm_pull(total, row(4), unit, r2[rows, 0:1])
            ghid[rows, :] = grad
            unit = u1[rows, :]
            add(0, grad * unit)
            add(3, grad)
            low = norm_pull(grad, row(2), unit, r1[rows, 0:1]).astype(BF)
            add(6, low.astype(F32))
            dst = pl.ds(pl.multiple_of(4 * lo + SLOT[0] * (hi - lo) + i * step, 16), step)
            dgel[dst, :] = low
            return carry

        lax.fori_loop(0, trips, pulls, 0)
        start_gather(dgel, 2, c)

    weight_grad(mlp, gpre, w1g, width // TILE)

    for c in range(count):
        lo, hi = spans[c]
        forward(dgel, 2, c)
        for j in (1, 3, 2, 0):
            start = pl.multiple_of(owner[j] * local + lo, 16)
            ghead[pl.ds(start, hi - lo), :] = lax.dot_general(
                dgel[block(c, j), :], wout[...], NT, preferred_element_type=F32
            ).astype(BF)
    weight_grad(hs, dgel, wog, 2 * (width // TILE))

    for i in range(8):
        sums[i:i + 1, :] = jnp.sum(acc[8 * i:8 * i + 8, :], axis=0, keepdims=True)
    b1sum[...] = jnp.sum(b1acc[...], axis=0, keepdims=True)

    for c in range(count):
        core_copy(2, c).wait_send()
        x_copy(2, c).wait_send()
        for phase, full in ((0, mlp), (1, brn), (2, dgel)):
            for copy in gather_copies(full, phase, c):
                copy.wait_send()


def middle(heads, tokens, cot, wout, w1, w2, b1, vec):
    seq, part = heads.shape
    local, width = tokens.shape
    units = w1.shape[1]
    vmem = pl.BlockSpec(memory_space=pltpu.VMEM)
    any_spec = pl.BlockSpec(memory_space=pl.ANY)
    shape = jax.ShapeDtypeStruct
    copies = 15 * 4
    return pl.pallas_call(
        mid_kernel,
        in_specs=[vmem] * 8,
        out_specs=[vmem, vmem, vmem, any_spec, any_spec, any_spec, vmem, vmem],
        out_shape=[
            shape((local, width), BF), shape((local, width), F32), shape((seq, part), BF),
            shape((units, width), F32), shape((width, units), F32), shape((part, width), F32),
            shape((8, width), F32), shape((1, units), F32),
        ],
        scratch_shapes=[
            pltpu.VMEM((seq, part), BF), pltpu.VMEM((seq, width), BF), pltpu.VMEM((seq, units), BF),
            pltpu.VMEM((seq, units), BF), pltpu.VMEM((seq, width), BF), pltpu.VMEM((seq, units), BF),
            pltpu.VMEM((local, width), F32), pltpu.VMEM((local, width), F32), pltpu.VMEM((local, width), F32),
            pltpu.VMEM((local, LANES), F32), pltpu.VMEM((local, LANES), F32),
            pltpu.VMEM((2 * local, width), F32), pltpu.VMEM((2 * local, width), BF),
            pltpu.VMEM((2 * local, width), BF), pltpu.VMEM((local, width), BF), pltpu.VMEM((local, width), BF),
            pltpu.VMEM((64, width), F32), pltpu.VMEM((8, units), F32), pltpu.VMEM((2, TILE, width), F32),
            pltpu.SemaphoreType.DMA((copies,)), pltpu.SemaphoreType.DMA((copies,)), pltpu.SemaphoreType.DMA((16,)),
        ],
        compiler_params=pltpu.CompilerParams(collective_id=0, has_side_effects=True, vmem_limit_bytes=63 << 20),
        cost_estimate=pl.CostEstimate(
            flops=14 * seq * width * units, bytes_accessed=40 << 20, transcendentals=seq * units
        ),
        name="middle",
    )(heads, tokens, cot, wout, w1, w2, b1, vec)


def middle_by_ops(head_low, rows_in, cotangent, wout, out_bias, w1, b1, w2, b2, gains, shifts, rel_of, sort):
    local_rows, width = rows_in.shape
    size = lax.axis_size("mp")
    seq_len, head_part = head_low.shape
    head_rel = rel_of(head_low)
    grad_out_all = cotangent.astype(F32)
    state = []
    for lo, hi in [(0, local_rows)]:
        rows = hi - lo
        total = size * rows
        attn_out = scatter_rel(
            jnp.dot(head_rel[:, lo:hi], wout, preferred_element_type=F32), "mp"
        ) + out_bias.astype(F32)
        norm_b, pull_b = jax.vjp(layer_norm, attn_out, gains[1], shifts[1])
        hidden_rows = rows_in[lo:hi] + norm_b
        norm_c, pull_c = jax.vjp(layer_norm, hidden_rows, gains[2], shifts[2])
        mlp_full = gather_rel(norm_c.astype(BF), "mp").reshape(total, width)
        pre_act = jnp.dot(mlp_full, w1, preferred_element_type=F32) + b1.astype(F32)
        activated, gelu_pull = jax.vjp(gelu_tanh, pre_act)
        act_low = activated.astype(BF)
        branch = scatter_rel(
            jnp.dot(act_low, w2, preferred_element_type=F32).reshape(size, rows, width), "mp"
        ) + b2.astype(F32)
        norm_d, pull_d = jax.vjp(layer_norm, branch, gains[3], shifts[3])
        mixed = (hidden_rows + norm_d).astype(BF)
        grad_out = grad_out_all[lo:hi]
        grad_branch, gain_d, shift_d = pull_d(grad_out)
        branch_low = grad_branch.astype(BF)
        b2_part = jnp.sum(branch_low.astype(F32), axis=0)
        branch_full = gather_rel(branch_low, "mp").reshape(total, width)
        grad_act = jnp.einsum("td,fd->tf", branch_full, w2, preferred_element_type=F32)
        grad_pre = gelu_pull(grad_act)[0].astype(BF)
        b1_part = jnp.sum(grad_pre.astype(F32), axis=0)
        grad_norm_c = scatter_rel(
            jnp.einsum("tf,df->td", grad_pre, w1, preferred_element_type=F32).reshape(size, rows, width), "mp"
        )
        grad_hidden_c, gain_c, shift_c = pull_c(grad_norm_c)
        grad_hidden = grad_out + grad_hidden_c
        grad_attn, gain_b, shift_b = pull_b(grad_hidden)
        attn_grad_low = grad_attn.astype(BF)
        out_bias_part = jnp.sum(attn_grad_low.astype(F32), axis=0)
        attn_grad_rel = gather_rel(attn_grad_low, "mp")
        state.append(dict(
            mixed=mixed, act=act_low, branch=branch_full, mlp=mlp_full, pre=grad_pre, hidden=grad_hidden,
            attn=attn_grad_rel, heads=head_rel[:, lo:hi].reshape(total, head_part),
            gh=jnp.einsum("jtd,cd->jtc", attn_grad_rel, wout, preferred_element_type=F32).astype(BF),
            sums=jnp.stack([gain_b, gain_c, gain_d, shift_b, shift_c, shift_d, out_bias_part, b2_part]),
            b1=b1_part,
        ))

    def joined(name, axis=0):
        return jnp.concatenate([s[name] for s in state], axis=axis)

    w2_grad = jnp.einsum("tf,td->fd", joined("act"), joined("branch"), preferred_element_type=F32)
    w1_grad = jnp.einsum("td,tf->df", joined("mlp"), joined("pre"), preferred_element_type=F32)
    attn_grad_full = joined("attn", 1).reshape(seq_len, width)
    wout_grad = jnp.einsum(
        "tc,td->cd", head_rel.reshape(seq_len, head_part), attn_grad_full, preferred_element_type=F32
    )
    grad_heads = sort(joined("gh", 1))
    mixed, grad_hidden = joined("mixed"), joined("hidden")
    mid_sums = sum(s["sums"] for s in state)
    b1_grad = sum(s["b1"] for s in state)
    return mixed, grad_hidden, grad_heads, w2_grad, w1_grad, wout_grad, mid_sums, b1_grad


def shards(
    tokens, caption_len, row_offset, wqkv, qv_bias, wout, out_bias, w1, b1, w2, b2, ln_gain, ln_bias, cotangent,
):
    local_rows, width = tokens.shape
    size = lax.axis_size("mp")
    seq_len = local_rows * size
    head_part = wqkv.shape[2]
    gains = ln_gain.astype(F32)
    shifts = ln_bias.astype(F32)
    me = lax.axis_index("mp")

    def pick(blocks):
        return jnp.concatenate(
            [lax.dynamic_index_in_dim(blocks, me ^ j, 0, keepdims=True) for j in range(size)], axis=0
        )

    first = row_offset[0]
    second = first + caption_len[0, 0] + IMG
    third = second + caption_len[0, 1] + IMG
    bounds = jnp.stack([first, second, third]).astype(jnp.int32)

    def sort(rel):
        return pick(rel).reshape((seq_len,) + rel.shape[2:])

    def rel_of(rows):
        return pick(rows.reshape((size, local_rows) + rows.shape[1:]))

    rows_in = tokens.astype(F32)
    norm_a, pull_a = jax.vjp(layer_norm, rows_in, gains[0], shifts[0])
    attn_full = sort(gather_rel(norm_a.astype(BF), "mp"))
    w_in = wqkv.reshape(width, 3 * head_part)
    projected = jnp.dot(attn_full, w_in, preferred_element_type=F32)
    bias3 = jnp.concatenate([qv_bias[0], jnp.zeros_like(qv_bias[0]), qv_bias[1]]).astype(F32)
    projected = (projected + bias3).astype(BF)
    queries, keys, values = [projected[:, i * head_part:(i + 1) * head_part] for i in range(3)]
    head_low, lse = attn_fwd(bounds, queries, keys, values)
    if size == 4 and local_rows % 16 == 0 and w1.shape[1] % TILE == 0 and head_part % TILE == 0:
        vec = jnp.stack(
            [out_bias.astype(F32), b2.astype(F32), gains[1], shifts[1], gains[2], shifts[2], gains[3], shifts[3]]
        )
        mixed, grad_hidden, grad_heads, w2_grad, w1_grad, wout_grad, mid_sums, b1_grad = middle(
            head_low, tokens, cotangent, wout, w1, w2, b1.astype(F32)[None], vec
        )
        b1_grad = b1_grad[0]
    else:
        mixed, grad_hidden, grad_heads, w2_grad, w1_grad, wout_grad, mid_sums, b1_grad = middle_by_ops(
            head_low, rows_in, cotangent, wout, out_bias, w1, b1, w2, b2, gains, shifts, rel_of, sort
        )
    w2_grad = reduce_all(w2_grad, "dp")
    w1_grad = reduce_all(w1_grad, "dp")
    wout_grad = reduce_all(wout_grad, "dp")
    grads = attn_bwd(bounds, queries, keys, values, head_low, grad_heads, lse)
    grad_proj = jnp.concatenate(grads, axis=1)
    part_sums = jnp.sum(grad_proj.astype(F32), axis=0).reshape(3, head_part)
    qv_part = jnp.stack([part_sums[0], part_sums[2]])
    wqkv_grad = jnp.einsum("td,tc->dc", attn_full, grad_proj, preferred_element_type=F32)
    wqkv_grad = reduce_all(wqkv_grad, "dp").reshape(width, 3, head_part)
    grad_rel = rel_of(grad_proj)
    grad_norm_a = scatter_rel(jnp.einsum("jtc,dc->jtd", grad_rel, w_in, preferred_element_type=F32), "mp")
    grad_rows_a, gain_a, shift_a = pull_a(grad_norm_a)
    tokens_grad = (grad_hidden + grad_rows_a).astype(BF)
    own_sums = sum_small(jnp.concatenate([qv_part.reshape(-1), b1_grad]), ("dp",))
    qv_sum = own_sums[: 2 * head_part].reshape(2, head_part)
    b1_sum = own_sums[2 * head_part:]
    stack = jnp.concatenate([gain_a[None], mid_sums[0:3], shift_a[None], mid_sums[3:8]])
    stack = sum_small(stack, ("mp", "dp"))
    return (
        mixed, tokens_grad, wqkv_grad, qv_sum, wout_grad, stack[8], w1_grad, b1_sum, w2_grad, stack[9],
        stack[0:4], stack[4:8],
    )


def solution(mesh):
    rows = P(("dp", "mp"), None)
    placed = (
        rows, P("dp", None), P("dp"), P(None, None, "mp"), P(None, "mp"), P("mp", None), P(), P(None, "mp"),
        P("mp"), P("mp", None), P(), P(), P(), rows,
    )
    return jax.shard_map(
        shards,
        mesh=mesh,
        in_specs=placed,
        out_specs=(
            rows, rows, P(None, None, "mp"), P(None, "mp"), P("mp", None), P(), P(None, "mp"), P("mp"),
            P("mp", None), P(), P(), P(),
        ),
        check_vma=False,
    )
```

```python
import functools
import jax, jax.numpy as jnp
from jax import lax
from jax.experimental import pallas as pl
from jax.experimental.pallas import tpu as pltpu
from jax.sharding import PartitionSpec as P
HEAD=64; IMG=1024; CAP_MIN=5; LANES=128
F32=jnp.float32; BF=jnp.bfloat16
MESH=pl.DeviceIdType.MESH
NT=(((1,),(1,)),((),()))
TN=(((0,),(0,)),((),()))

def plan(seq):
    least=IMG+CAP_MIN
    slack=seq-2*least
    lo=least//LANES*LANES
    hi=-(-(seq-least)//LANES)*LANES
    head_pad=-(-slack//LANES)*LANES
    tail_pad=(2*least)//LANES*LANES
    def cut(a,b,step):
        out=[]
        while a<b:
            out.append((a,min(a+step,b))); a=min(a+step,b)
        return out
    return lo,hi,head_pad,tail_pad,cut

def free_of_mask(k0,k1,q0,q1,seq):
    lo,hi,head_pad,tail_pad,_=plan(seq)
    if k1>q0: return False
    if q1<=lo: return k0>=head_pad
    if q0>=hi: return k0>=hi and q1<=tail_pad
    return False

def seg_start(pos,b0,b1,b2):
    return jnp.where(pos>=b2,b2,jnp.where(pos>=b1,b1,jnp.where(pos>=b0,b0,0)))

def fwd_kernel(bounds,q_ref,k_ref,v_ref,o_ref,lse_ref):
    seq,width=q_ref.shape
    h=pl.program_id(0)
    b0,b1,b2=bounds[0],bounds[1],bounds[2]
    lo,hi,_,_,cut=plan(seq)
    lane=lax.broadcasted_iota(jnp.int32,(1,width),1)
    mine=(lane//HEAD)==h
    blocks=[(a,b,0) for a,b in cut(0,lo,256)]+[(a,b,0) for a,b in cut(lo,hi,256)]+[(a,b,lo) for a,b in cut(hi,seq,256)]
    for a,b,start in blocks:
        n=b-a
        qm=jnp.where(mine,q_ref[a:b,:].astype(F32)*HEAD**-0.5,0.0).astype(BF)
        qpos=a+lax.broadcasted_iota(jnp.int32,(n,1),0)
        first=seg_start(qpos,b0,b1,b2)
        parts=[]
        top=None
        for c,d in cut(start,b,128):
            s=lax.dot_general(qm,k_ref[c:d,:],NT,preferred_element_type=F32)
            if not free_of_mask(c,d,a,b,seq):
                kpos=c+lax.broadcasted_iota(jnp.int32,(n,d-c),1)
                s=jnp.where((kpos>=first)&(kpos<=qpos),s,-1e9)
            parts.append(s)
            top=s if top is None else jnp.maximum(top,s)
        m=jnp.max(top,axis=1,keepdims=True)
        es=[jnp.exp(s-m) for s in parts]
        tot=es[0]
        for e in es[1:]: tot=tot+e
        l=jnp.sum(tot,axis=1,keepdims=True)
        p=jnp.concatenate([e.astype(BF) for e in es],axis=1)
        o=jnp.dot(p,v_ref[start:b,:],preferred_element_type=F32)/l
        o_ref[a:b,:]=jnp.where(mine,o.astype(BF),o_ref[a:b,:])
        lse=m+jnp.log(l)
        lse_ref[0,:,a:b]=jnp.broadcast_to(lse,(n,128)).T[0:8,:]

def bwd_kernel(bounds,q_ref,k_ref,v_ref,o_ref,do_ref,lse_ref,dq_ref,dk_ref,dv_ref,qm_s,dom_s,dqt_s,delta_s):
    seq,width=q_ref.shape
    h=pl.program_id(0)
    b0,b1,b2=bounds[0],bounds[1],bounds[2]
    lo,hi,_,_,cut=plan(seq)
    lane=lax.broadcasted_iota(jnp.int32,(1,width),1)
    mine=(lane//HEAD)==h
    qm_s[...]=jnp.where(mine,q_ref[...].astype(F32)*HEAD**-0.5,0.0).astype(BF)
    dom_s[...]=jnp.where(mine,do_ref[...],jnp.zeros((),BF))
    ones=jnp.ones((8,width),F32)
    for a,b in cut(0,seq,256):
        prod=dom_s[a:b,:].astype(F32)*o_ref[a:b,:].astype(F32)
        delta_s[:,a:b]=lax.dot_general(ones,prod,NT,preferred_element_type=F32,precision=lax.Precision.HIGHEST)
    dqt_s[...]=jnp.zeros_like(dqt_s)
    blocks=[(a,b,hi) for a,b in cut(0,lo,256)]+[(a,b,seq) for a,b in cut(lo,hi,256)]+[(a,b,seq) for a,b in cut(hi,seq,256)]
    for a,b,stop in blocks:
        n=b-a
        kk=k_ref[a:b,:]; vv=v_ref[a:b,:]
        kpos=a+lax.broadcasted_iota(jnp.int32,(n,1),0)
        kh=jnp.where(mine,kk,jnp.zeros((),BF))
        pts=[];dsts=[]
        for c,d in cut(a,stop,128):
            st=lax.dot_general(kk,qm_s[c:d,:],NT,preferred_element_type=F32)
            pt=jnp.exp(st-lse_ref[0,0:1,c:d])
            if not free_of_mask(a,b,c,d,seq):
                qpos=c+lax.broadcasted_iota(jnp.int32,(1,d-c),1)
                first=seg_start(qpos,b0,b1,b2)
                pt=jnp.where((kpos>=first)&(kpos<=qpos),pt,0.0)
            dpt=lax.dot_general(vv,dom_s[c:d,:],NT,preferred_element_type=F32)
            dst=pt*(dpt-delta_s[0:1,c:d])
            pts.append(pt.astype(BF)); dsts.append(dst.astype(BF))
        pt=jnp.concatenate(pts,axis=1); dst=jnp.concatenate(dsts,axis=1)
        dv=jnp.dot(pt,dom_s[a:stop,:],preferred_element_type=F32)
        dk=jnp.dot(dst,qm_s[a:stop,:],preferred_element_type=F32)
        dv_ref[a:b,:]=jnp.where(mine,dv.astype(BF),dv_ref[a:b,:])
        dk_ref[a:b,:]=jnp.where(mine,dk.astype(BF),dk_ref[a:b,:])
        dqt_s[:,a:stop]+=lax.dot_general(kh,dst,TN,preferred_element_type=F32)
    for a,b in cut(0,seq,128):
        dq=(dqt_s[:,a:b]*HEAD**-0.5).T
        dq_ref[a:b,:]=jnp.where(mine,dq.astype(BF),dq_ref[a:b,:])

def attn_fwd(bounds,q,k,v):
    seq,width=q.shape; H=width//HEAD
    full=pl.BlockSpec((seq,width),lambda h:(0,0))
    return pl.pallas_call(fwd_kernel,grid=(H,),
        in_specs=[pl.BlockSpec(memory_space=pltpu.SMEM),full,full,full],
        out_specs=[full,pl.BlockSpec((1,8,seq),lambda h:(h,0,0))],
        out_shape=[jax.ShapeDtypeStruct((seq,width),BF),jax.ShapeDtypeStruct((H,8,seq),F32)],
        compiler_params=pltpu.CompilerParams(vmem_limit_bytes=56<<20),name="attn_fwd")(bounds,q,k,v)

def attn_bwd(bounds,q,k,v,o,do,lse):
    seq,width=q.shape; H=width//HEAD
    full=pl.BlockSpec((seq,width),lambda h:(0,0))
    sh=jax.ShapeDtypeStruct((seq,width),BF)
    return pl.pallas_call(bwd_kernel,grid=(H,),
        in_specs=[pl.BlockSpec(memory_space=pltpu.SMEM),full,full,full,full,full,pl.BlockSpec((1,8,seq),lambda h:(h,0,0))],
        out_specs=[full,full,full],out_shape=[sh,sh,sh],
        scratch_shapes=[pltpu.VMEM((seq,width),BF),pltpu.VMEM((seq,width),BF),pltpu.VMEM((width,seq),F32),pltpu.VMEM((8,seq),F32)],
        compiler_params=pltpu.CompilerParams(vmem_limit_bytes=56<<20),name="attn_bwd")(bounds,q,k,v,o,do,lse)

eps_norm = 1e-05


def layer_norm(values, gain, shift):
    center = values - jnp.mean(values, axis=-1, keepdims=True)
    spread = jnp.mean(center * center, axis=-1, keepdims=True)
    return center * lax.rsqrt(spread + eps_norm) * gain + shift


def gelu_tanh(values):
    return jax.nn.gelu(values, approximate=True)


def swap(values, axis, mask):
    size = lax.axis_size(axis)
    return lax.ppermute(values, axis, [(i, i ^ mask) for i in range(size)])


def masks_of(axis):
    size = lax.axis_size(axis)
    out = []
    step = size // 2
    while step:
        out.append(step)
        step //= 2
    return out


def gather_rel(block, axis):
    have = {0: block}
    for mask in masks_of(axis):
        have.update({j ^ mask: swap(v, axis, mask) for j, v in list(have.items())})
    return jnp.stack([have[j] for j in range(lax.axis_size(axis))])


def scatter_rel(parts, axis):
    have = {j: parts[j] for j in range(parts.shape[0])}
    for mask in reversed(masks_of(axis)):
        got = {j: swap(have[j].astype(BF), axis, mask) for j in have if j & mask}
        have = {j: have[j] + got[j ^ mask].astype(F32) for j in have if not j & mask}
    return have[0]


def reduce_all(values, axis):
    me = lax.axis_index(axis)
    masks = list(reversed(masks_of(axis)))
    rows = values.shape[0]
    for mask in masks:
        rows //= 2
        bit = (me // mask) % 2
        keep = lax.dynamic_slice_in_dim(values, bit * rows, rows, 0)
        send = lax.dynamic_slice_in_dim(values, (1 - bit) * rows, rows, 0)
        values = keep + swap(send.astype(BF), axis, mask).astype(F32)
    low = values.astype(BF)
    for mask in reversed(masks):
        bit = (me // mask) % 2
        got = swap(low, axis, mask)
        both = jnp.concatenate([low, got], axis=0)
        flipped = jnp.concatenate([got, low], axis=0)
        low = jnp.where(bit == 0, both, flipped)
    return low.astype(F32)


def sum_small(values, axes):
    for axis in axes:
        for mask in masks_of(axis):
            values = values + swap(values, axis, mask)
    return values


SLOT = {1: 0, 3: 1, 2: 2, 0: 3}
TILE = 256


def spans_of(rows):
    units = rows // 16
    sizes = [16 * (units // 4 + (1 if i < units % 4 else 0)) for i in range(4)]
    edges = [sum(sizes[:i]) for i in range(5)]
    return [(edges[i], edges[i + 1]) for i in range(4)]


def fold8(values):
    rows, cols = values.shape
    return jnp.sum(values.reshape(rows // 8, 8, cols), axis=0)


def norm_stats(values):
    center = values - jnp.mean(values, axis=-1, keepdims=True)
    inv = lax.rsqrt(jnp.mean(center * center, axis=-1, keepdims=True) + eps_norm)
    return center * inv, inv


def norm_pull(upstream, gain, unit, inv):
    scaled = upstream * gain
    first = jnp.mean(scaled, axis=-1, keepdims=True)
    second = jnp.mean(scaled * unit, axis=-1, keepdims=True)
    return (scaled - first - unit * second) * inv


def dp_place():
    dp, me = lax.axis_index("dp"), lax.axis_index("mp")
    y, low, high = dp % 2, dp // 2 % 2, dp // 4
    return (y, low, high), (
        (dp + 1 - 2 * y, me), (dp + 2 * (1 - 2 * low), me), (dp + 4 * (1 - 2 * high), me)
    )


def by_rows(count, body):
    step = next(t for t in (64, 48, 32, 16) if count % t == 0)

    def trip(i, carry):
        body(pl.multiple_of(i * step, 16), step)
        return carry

    lax.fori_loop(0, count // step, trip, 0)


class Reduction:
    def __init__(self, rows, work, held, sbuf, rbuf, full, send, recv, base):
        self.rows, self.work, self.held, self.full = rows, work, held, full
        self.sbuf, self.rbuf, self.send, self.recv, self.base = sbuf, rbuf, send, recv, base
        self.bits, self.peers = dp_place()
        off = [0]
        for k in range(3):
            off.append(off[-1] + self.bits[k] * (rows >> (k + 1)))
        self.off = off

    def copy(self, i):
        if i < 3:
            src, dst, peer = self.sbuf[i], self.rbuf[i], self.peers[i]
        else:
            k = 5 - i
            part = self.full.at[pl.ds(pl.multiple_of(self.off[k + 1], 16), self.rows >> (k + 1))]
            src, dst, peer = part, part, self.peers[k]
        return pltpu.make_async_remote_copy(
            src_ref=src, dst_ref=dst, send_sem=self.send.at[self.base + i], recv_sem=self.recv.at[self.base + i],
            device_id=peer, device_id_type=MESH,
        )

    def at(self, offset, i, step):
        return pl.ds(pl.multiple_of(offset + i - (self.off[1] if self.held else 0), 16), step)

    def reduce(self, k, fresh=False):
        n = self.rows >> (k + 1)
        bit = self.bits[k]
        give, keep = self.off[k] + (1 - bit) * n, self.off[k] + bit * n
        if not fresh:
            self.copy(k - 1).wait_recv()

        def out(i, step):
            rows = pl.ds(i, step)
            value = self.work[self.at(give, i, step), :]
            if not fresh:
                value = value + self.rbuf[k - 1][pl.ds(pl.multiple_of((1 - bit) * n + i, 16), step), :].astype(F32)
            self.sbuf[k][rows, :] = value.astype(BF)

        def stay(i, step):
            rows = self.at(keep, i, step)
            self.work[rows, :] += self.rbuf[k - 1][pl.ds(pl.multiple_of(bit * n + i, 16), step), :].astype(F32)

        by_rows(n, out)
        self.copy(k).start()
        if not fresh:
            by_rows(n, stay)

    def settle(self, dst, at):
        n = self.rows >> 3
        self.copy(2).wait_recv()

        def body(i, step):
            value = self.work[self.at(self.off[3], i, step), :] + self.rbuf[2][pl.ds(i, step), :].astype(F32)
            dst[pl.ds(pl.multiple_of(at + i, 16), step), :] = value.astype(BF)

        by_rows(n, body)

    def gather(self, i):
        if i > 3:
            self.copy(i - 1).wait_recv()
        self.copy(i).start()

    def finish(self, first=0):
        if self.full is not None:
            self.copy(5).wait_recv()
        for i in range(first, 6 if self.full is not None else 3):
            self.copy(i).wait_send()


def mid_kernel(
    heads, tokens, cot, wout, w1, w2, b1, vec,
    mixed, ghid, ghead, w2e, w1h, wog, sums, b1sum,
    hs, mlp, act, dgel, brn, gpre, u1, u2, hid, r1, r2, pbuf, cs, cr, xs, xr, acc, b1acc,
    s2y, r2y, r2z, r2w, r1y, send, recv, dsend, drecv,
):
    local, width = tokens.shape
    hidden_units = w1.shape[1]
    spans = spans_of(local)
    count = len(spans)
    dp, me = lax.axis_index("dp"), lax.axis_index("mp")
    mx, mc = me // 2, me % 2
    peer_core = (dp, mx * 2 + 1 - mc)
    peer_x = (dp, (1 - mx) * 2 + mc)
    owner = {0: me, 1: mx * 2 + 1 - mc, 2: (1 - mx) * 2 + mc, 3: (1 - mx) * 2 + 1 - mc}

    barrier = pltpu.get_barrier_semaphore()
    bits, dp_peers = dp_place()
    for peer in (peer_core, peer_x) + dp_peers:
        pl.semaphore_signal(barrier, inc=1, device_id=peer, device_id_type=MESH)
    pl.semaphore_wait(barrier, 5)

    def remote(src, dst, phase, kind, c, device):
        i = (phase * 5 + kind) * count + c
        return pltpu.make_async_remote_copy(
            src_ref=src, dst_ref=dst, send_sem=send.at[i], recv_sem=recv.at[i], device_id=device, device_id_type=MESH
        )

    def core_copy(phase, c):
        lo, hi = spans[c]
        rows = pl.ds(2 * lo, 2 * (hi - lo))
        return remote(cs.at[rows], cr.at[rows], phase, 0, c, peer_core)

    def x_copy(phase, c):
        lo, hi = spans[c]
        rows = pl.ds(lo, hi - lo)
        return remote(xs.at[rows], xr.at[rows], phase, 1, c, peer_x)

    def block(c, j):
        lo, hi = spans[c]
        return pl.ds(4 * lo + SLOT[j] * (hi - lo), hi - lo)

    def gather_copies(full, phase, c):
        own = full.at[block(c, 0)]
        return (
            remote(own, full.at[block(c, 2)], phase, 2, c, peer_x),
            remote(own, full.at[block(c, 1)], phase, 3, c, peer_core),
            remote(full.at[block(c, 2)], full.at[block(c, 3)], phase, 4, c, peer_core),
        )

    def tiles(c):
        lo, hi = spans[c]
        step = next(t for t in (48, 64, 32, 16) if (hi - lo) % t == 0)
        return (hi - lo) // step, step

    def start_gather(full, phase, c):
        first, second, _ = gather_copies(full, phase, c)
        first.start()
        second.start()

    def forward(full, phase, c):
        first, second, third = gather_copies(full, phase, c)
        first.wait_recv()
        third.start()
        second.wait_recv()
        third.wait_recv()

    def partial_products(lhs, rhs, turned, phase, c, half, wide=TILE):
        lo, hi = spans[c]
        r = hi - lo
        rows = pl.ds(4 * lo + half * 2 * r, 2 * r)
        out = pl.ds(2 * lo, 2 * r)

        def body(n, carry):
            cols = pl.ds(pl.multiple_of(n * wide, wide), wide)
            if turned:
                part = lax.dot_general(lhs[rows, :], rhs[cols, :], NT, preferred_element_type=F32)
            else:
                part = jnp.dot(lhs[rows, :], rhs[:, cols], preferred_element_type=F32)
            if half == 0:
                cs[out, cols] = part.astype(BF)
            else:
                pbuf[out, cols] = part
            return carry

        lax.fori_loop(0, width // wide, body, 0)

    def pass_on(phase, c):
        lo, hi = spans[c]
        r = hi - lo
        core_copy(phase, c).wait_recv()
        if phase:
            x_copy(phase - 1, c).wait_send()
        xs[lo:hi, :] = (pbuf[2 * lo:2 * lo + r, :] + cr[2 * lo + r:2 * lo + 2 * r, :].astype(F32)).astype(BF)
        x_copy(phase, c).start()

    def own_total(c, i, step):
        lo, hi = spans[c]
        r = hi - lo
        kept = pl.ds(pl.multiple_of(2 * lo + r + i * step, 16), step)
        near = pl.ds(pl.multiple_of(2 * lo + i * step, 16), step)
        far = pl.ds(pl.multiple_of(lo + i * step, 16), step)
        return far, pbuf[kept, :] + cr[near, :].astype(F32) + xr[far, :].astype(F32)

    def row(i):
        return vec[i:i + 1, :]

    acc[...] = jnp.zeros_like(acc)
    b1acc[...] = jnp.zeros_like(b1acc)

    def add(i, values):
        acc[8 * i:8 * i + 8, :] += fold8(values)

    def project(c):
        lo, hi = spans[c]
        for j in (1, 3, 2, 0):
            start = pl.multiple_of(owner[j] * local + lo, 16)
            hs[block(c, j), :] = heads[pl.ds(start, hi - lo), :]
        partial_products(hs, wout, False, 0, c, 0)
        core_copy(0, c).start()
        partial_products(hs, wout, False, 0, c, 1)

    project(0)
    for c in range(count):
        if c + 1 < count:
            project(c + 1)
        pass_on(0, c)

    for c in range(count):
        x_copy(0, c).wait_recv()
        lo, hi = spans[c]
        trips, step = tiles(c)

        def norms(i, carry):
            rows, total = own_total(c, i, step)
            unit, inv = norm_stats(total + row(0))
            u1[rows, :] = unit
            r1[rows, :] = jnp.broadcast_to(inv, (step, LANES))
            hidden = tokens[rows, :].astype(F32) + unit * row(2) + row(3)
            hid[rows, :] = hidden
            unit, inv = norm_stats(hidden)
            u2[rows, :] = unit
            r2[rows, :] = jnp.broadcast_to(inv, (step, LANES))
            dst = pl.ds(pl.multiple_of(4 * lo + SLOT[0] * (hi - lo) + i * step, 16), step)
            mlp[dst, :] = (unit * row(4) + row(5)).astype(BF)
            return carry

        lax.fori_loop(0, trips, norms, 0)
        start_gather(mlp, 0, c)

    for c in range(count):
        lo, hi = spans[c]
        r = hi - lo
        forward(mlp, 0, c)
        core_copy(0, c).wait_send()
        for half in range(2):
            rows = pl.ds(4 * lo + half * 2 * r, 2 * r)

            def units(n, carry):
                cols = pl.ds(pl.multiple_of(n * TILE, TILE), TILE)
                pre = jnp.dot(mlp[rows, :], w1[:, cols], preferred_element_type=F32) + b1[:, cols]
                square = pre * pre
                inner = (0.7978845608028654 * pre) * (1.0 + 0.044715 * square)
                tanh = jnp.tanh(inner)
                plus = 0.5 * (1.0 + tanh)
                act[rows, cols] = (pre * plus).astype(BF)
                slope = plus + (0.5 * pre) * (1.0 - tanh * tanh) * (
                    0.7978845608028654 * (1.0 + (3 * 0.044715) * square)
                )
                dgel[rows, cols] = slope.astype(BF)
                return carry

            lax.fori_loop(0, hidden_units // TILE, units, 0)
            partial_products(act, w2, False, 1, c, half)
            if half == 0:
                core_copy(1, c).start()
        pass_on(1, c)

    for c in range(count):
        x_copy(1, c).wait_recv()
        lo, hi = spans[c]
        trips, step = tiles(c)

        def last(i, carry):
            rows, total = own_total(c, i, step)
            unit, inv = norm_stats(total + row(1))
            mixed[rows, :] = (hid[rows, :] + unit * row(6) + row(7)).astype(BF)
            grad = cot[rows, :].astype(F32)
            add(2, grad * unit)
            add(5, grad)
            low = norm_pull(grad, row(6), unit, inv).astype(BF)
            add(7, low.astype(F32))
            dst = pl.ds(pl.multiple_of(4 * lo + SLOT[0] * (hi - lo) + i * step, 16), step)
            brn[dst, :] = low
            return carry

        lax.fori_loop(0, trips, last, 0)
        start_gather(brn, 1, c)

    for c in range(count):
        lo, hi = spans[c]
        r = hi - lo
        forward(brn, 1, c)
        core_copy(1, c).wait_send()
        for half in range(2):
            rows = pl.ds(4 * lo + half * 2 * r, 2 * r)

            def slopes(n, carry):
                cols = pl.ds(pl.multiple_of(n * TILE, TILE), TILE)
                grad = lax.dot_general(brn[rows, :], w2[cols, :], NT, preferred_element_type=F32)
                low = (grad * dgel[rows, cols].astype(F32)).astype(BF)
                gpre[rows, cols] = low
                b1acc[:, cols] += fold8(low.astype(F32))
                return carry

            lax.fori_loop(0, hidden_units // TILE, slopes, 0)
            partial_products(gpre, w1, True, 2, c, half)
            if half == 0:
                core_copy(2, c).start()
        pass_on(2, c)

    half_rows = hidden_units // 2
    sum2 = Reduction(
        hidden_units, hid, True, (s2y, act.at[512:768], act.at[768:896]), (r2y, r2z, r2w), None, dsend, drecv, 0
    )
    sum1 = Reduction(width, w1h, True, (act.at[0:512],), (r1y,), None, dsend, drecv, 3)

    def weight_grad(lhs, rhs, half, dst):
        for n in range(half_rows // TILE):
            cols = pl.ds(pl.multiple_of(half * half_rows + n * TILE, TILE), TILE)
            part = lax.dot_general(lhs[:, cols], rhs[...], TN, preferred_element_type=F32)
            dst[n * TILE:(n + 1) * TILE, :] = part.astype(dst.dtype)

    weight_grad(act, brn, 1 - bits[0], s2y)
    sum2.copy(0).start()
    weight_grad(act, brn, bits[0], hid)
    weight_grad(mlp, gpre, 1 - bits[0], act)
    sum1.copy(0).start()
    weight_grad(mlp, gpre, bits[0], w1h)

    for c in range(count):
        x_copy(2, c).wait_recv()
        lo, hi = spans[c]
        trips, step = tiles(c)

        def pulls(i, carry):
            rows, total = own_total(c, i, step)
            unit = u2[rows, :]
            add(1, total * unit)
            add(4, total)
            grad = cot[rows, :].astype(F32) + norm_pull(total, row(4), unit, r2[rows, 0:1])
            ghid[rows, :] = grad
            unit = u1[rows, :]
            add(0, grad * unit)
            add(3, grad)
            low = norm_pull(grad, row(2), unit, r1[rows, 0:1]).astype(BF)
            add(6, low.astype(F32))
            dst = pl.ds(pl.multiple_of(4 * lo + SLOT[0] * (hi - lo) + i * step, 16), step)
            dgel[dst, :] = low
            return carry

        lax.fori_loop(0, trips, pulls, 0)
        start_gather(dgel, 2, c)

    sum2.reduce(1)
    for c in range(count):
        lo, hi = spans[c]
        forward(dgel, 2, c)
        for j in (1, 3, 2, 0):
            start = pl.multiple_of(owner[j] * local + lo, 16)
            ghead[pl.ds(start, hi - lo), :] = lax.dot_general(
                dgel[block(c, j), :], wout[...], NT, preferred_element_type=F32
            ).astype(BF)
        if c == 1:
            sum2.reduce(2)
    wog[...] = lax.dot_general(hs[...], dgel[...], TN, preferred_element_type=F32)
    sum2.settle(w2e, 0)
    sum1.copy(0).wait_recv()

    def add_half(i, step):
        w1h[pl.ds(i, step), :] += r1y[pl.ds(i, step), :].astype(F32)

    by_rows(half_rows, add_half)
    sum2.finish()
    sum1.copy(0).wait_send()

    for i in range(8):
        sums[i:i + 1, :] = jnp.sum(acc[8 * i:8 * i + 8, :], axis=0, keepdims=True)
    b1sum[...] = jnp.sum(b1acc[...], axis=0, keepdims=True)

    for c in range(count):
        core_copy(2, c).wait_send()
        x_copy(2, c).wait_send()
        for phase, full in ((0, mlp), (1, brn), (2, dgel)):
            for copy in gather_copies(full, phase, c):
                copy.wait_send()


def middle(heads, tokens, cot, wout, w1, w2, b1, vec):
    seq, part = heads.shape
    local, width = tokens.shape
    units = w1.shape[1]
    vmem = pl.BlockSpec(memory_space=pltpu.VMEM)
    shape = jax.ShapeDtypeStruct
    copies = 15 * 4
    low = lambda *dims: pltpu.VMEM(dims, BF)
    wide = lambda *dims: pltpu.VMEM(dims, F32)
    dma = lambda n: pltpu.SemaphoreType.DMA((n,))
    return pl.pallas_call(
        mid_kernel,
        in_specs=[vmem] * 8,
        out_specs=[vmem] * 8,
        out_shape=[
            shape((local, width), BF), shape((local, width), F32), shape((seq, part), BF),
            shape((units // 8, width), BF), shape((width // 2, units), F32), shape((part, width), F32),
            shape((8, width), F32), shape((1, units), F32),
        ],
        scratch_shapes=[
            low(seq, part), low(seq, width), low(seq, units), low(seq, units), low(seq, width), low(seq, units),
            wide(local, width), wide(local, width), wide(local, width), wide(local, LANES), wide(local, LANES),
            wide(2 * local, width), low(2 * local, width), low(2 * local, width), low(local, width),
            low(local, width), wide(64, width), wide(8, units),
            low(units // 2, width), low(units // 2, width), low(units // 4, width), low(units // 8, width),
            low(width // 2, units), dma(copies), dma(copies), dma(4), dma(4),
        ],
        compiler_params=pltpu.CompilerParams(collective_id=0, has_side_effects=True, vmem_limit_bytes=63 << 20),
        cost_estimate=pl.CostEstimate(
            flops=14 * seq * width * units, bytes_accessed=40 << 20, transcendentals=seq * units
        ),
        name="middle",
    )(heads, tokens, cot, wout, w1, w2, b1, vec)


def back_kernel(
    bounds, q_ref, k_ref, v_ref, o_ref, do_ref, lse_ref, xfull, w_in, ghid, tokens, gain0, w2e, w1h, wog_in, small_in,
    tgrad, w2f, w1f, wof, wqf, small_out,
    qm_s, dom_s, dqt_s, delta_s, gp, wq, wog, pbuf, cs, cr, xs, xr, acc,
    s1z, s1w, r1z, r1w, soy, soz, sow, roy, roz, row_, sqy, sqz, sqw, rqy, rqz, rqw, small, near, far,
    send, recv, dsend, drecv, nsend, nrecv, fsend, frecv,
):
    local, width = tokens.shape
    seq, part = q_ref.shape
    heads = part // HEAD
    spans = spans_of(local)
    count = len(spans)
    dp, me = lax.axis_index("dp"), lax.axis_index("mp")
    mx, mc = me // 2, me % 2
    owner = {0: me, 1: mx * 2 + 1 - mc, 2: (1 - mx) * 2 + mc, 3: (1 - mx) * 2 + 1 - mc}
    peer_core, peer_x, peer_far = (dp, owner[1]), (dp, owner[2]), (dp, owner[3])
    near_peers = (peer_core, peer_x, peer_far)
    far_peers = tuple(((dp + i) % 8, me) for i in range(1, 8))
    barrier = pltpu.get_barrier_semaphore()
    for peer in near_peers + far_peers:
        pl.semaphore_signal(barrier, inc=1, device_id=peer, device_id_type=MESH)
    pl.semaphore_wait(barrier, 10)

    _, dp_peers = dp_place()
    pair = part // 2
    sum2 = Reduction(w2f.shape[0], None, False, (None,) * 3, (None,) * 3, w2f, dsend, drecv, 0)
    sum1 = Reduction(w1f.shape[0], w1h, True, (None, s1z, s1w), (None, r1z, r1w), w1f, dsend, drecv, 6)
    sumo = Reduction(part, wog, False, (soy, soz, sow), (roy, roz, row_), wof, dsend, drecv, 12)
    sumq = [
        Reduction(
            3 * pair, wq.at[i], False, (sqy.at[i], sqz.at[i], sqw.at[i]), (rqy.at[i], rqz.at[i], rqw.at[i]),
            wqf.at[i], dsend, drecv, 18 + 6 * i,
        )
        for i in range(2)
    ]

    b0, b1, b2 = bounds[0], bounds[1], bounds[2]
    lo_edge, hi_edge, _, _, cut = plan(seq)
    lane = lax.broadcasted_iota(jnp.int32, (1, part), 1)

    def prepare(h):
        mine = (lane // HEAD) == h
        qm_s[...] = jnp.where(mine, q_ref[...].astype(F32) * HEAD**-0.5, 0.0).astype(BF)
        dom_s[...] = jnp.where(mine, do_ref[...], jnp.zeros((), BF))
        ones = jnp.ones((8, part), F32)
        for a, b in cut(0, seq, 256):
            prod = dom_s[a:b, :].astype(F32) * o_ref[a:b, :].astype(F32)
            delta_s[:, a:b] = lax.dot_general(
                ones, prod, NT, preferred_element_type=F32, precision=lax.Precision.HIGHEST
            )
        dqt_s[...] = jnp.zeros_like(dqt_s)

    def key_blocks(h, blocks):
        mine = (lane // HEAD) == h
        for a, b, stop in blocks:
            n = b - a
            kk = k_ref[a:b, :]
            vv = v_ref[a:b, :]
            kpos = a + lax.broadcasted_iota(jnp.int32, (n, 1), 0)
            kh = jnp.where(mine, kk, jnp.zeros((), BF))
            pts, dsts = [], []
            for c, d in cut(a, stop, 128):
                st = lax.dot_general(kk, qm_s[c:d, :], NT, preferred_element_type=F32)
                pt = jnp.exp(st - lse_ref[h, 0:1, c:d])
                if not free_of_mask(a, b, c, d, seq):
                    qpos = c + lax.broadcasted_iota(jnp.int32, (1, d - c), 1)
                    first = seg_start(qpos, b0, b1, b2)
                    pt = jnp.where((kpos >= first) & (kpos <= qpos), pt, 0.0)
                dpt = lax.dot_general(vv, dom_s[c:d, :], NT, preferred_element_type=F32)
                pts.append(pt.astype(BF))
                dsts.append((pt * (dpt - delta_s[0:1, c:d])).astype(BF))
            pt = jnp.concatenate(pts, axis=1)
            dst = jnp.concatenate(dsts, axis=1)
            dv = jnp.dot(pt, dom_s[a:stop, :], preferred_element_type=F32)
            dk = jnp.dot(dst, qm_s[a:stop, :], preferred_element_type=F32)
            gp[a:b, 2 * part:3 * part] = jnp.where(mine, dv.astype(BF), gp[a:b, 2 * part:3 * part])
            gp[a:b, part:2 * part] = jnp.where(mine, dk.astype(BF), gp[a:b, part:2 * part])
            dqt_s[:, a:stop] += lax.dot_general(kh, dst, TN, preferred_element_type=F32)

    def finish_queries(h):
        mine = (lane // HEAD) == h
        for a, b in cut(0, seq, 128):
            dq = (dqt_s[:, a:b] * HEAD**-0.5).T
            gp[a:b, 0:part] = jnp.where(mine, dq.astype(BF), gp[a:b, 0:part])

    def input_grad(i):
        for t in range(3):
            cols = gp[:, t * part + i * pair:t * part + (i + 1) * pair]
            wq[i, t * pair:(t + 1) * pair, :] = lax.dot_general(cols, xfull[...], TN, preferred_element_type=F32)

    at2 = pl.multiple_of(sum2.off[3], 16)
    w2f[pl.ds(at2, w2e.shape[0]), :] = w2e[...]
    sum2.gather(3)
    sum1.reduce(1, fresh=True)
    wog[...] = wog_in[...]
    sumo.reduce(0, fresh=True)
    gp[...] = jnp.zeros_like(gp)

    first_half = [(a, b, hi_edge) for a, b in cut(0, lo_edge, 256)] + [(a, b, seq) for a, b in cut(lo_edge, hi_edge, 256)]
    second_half = [(a, b, seq) for a, b in cut(hi_edge, seq, 256)]

    def settle(stream):
        stream.settle(stream.full, stream.off[3])
        stream.gather(3)

    def event(number):
        if number == 2:
            sumo.reduce(1)
        elif number == 3:
            sum2.gather(4)
            sumo.reduce(2)
        elif number == 4:
            sum1.reduce(2)
            input_grad(0)
            sumq[0].reduce(0, fresh=True)
        elif number == 5:
            sum2.gather(5)
            settle(sumo)
        elif number == 6:
            settle(sum1)
            sumq[0].reduce(1)
        elif number == 7:
            sumo.gather(4)
            sumq[0].reduce(2)

    def one_head(h, carry):
        prepare(h)
        key_blocks(h, first_half)
        for k in range(heads):

            @pl.when(h == k)
            def _(k=k):
                event(2 * k + 1)

        key_blocks(h, second_half)
        finish_queries(h)
        for k in range(heads):

            @pl.when(h == k)
            def _(k=k):
                event(2 * k + 2)

        return carry

    lax.fori_loop(0, heads, one_head, 0)

    def remote(src, dst, kind, c, device):
        i = kind * count + c
        return pltpu.make_async_remote_copy(
            src_ref=src, dst_ref=dst, send_sem=send.at[i], recv_sem=recv.at[i], device_id=device, device_id_type=MESH
        )

    def core_copy(c):
        lo, hi = spans[c]
        rows = pl.ds(2 * lo, 2 * (hi - lo))
        return remote(cs.at[rows], cr.at[rows], 0, c, peer_core)

    def x_copy(c):
        lo, hi = spans[c]
        rows = pl.ds(lo, hi - lo)
        return remote(xs.at[rows], xr.at[rows], 1, c, peer_x)

    def project(c):
        lo, hi = spans[c]
        r = hi - lo
        for j in (1, 3, 2, 0):
            src = pl.ds(pl.multiple_of(owner[j] * local + lo, 16), r)
            dst = pl.ds(2 * lo + SLOT[j] % 2 * r, r)

            def body(n, carry):
                cols = pl.ds(pl.multiple_of(n * TILE, TILE), TILE)
                value = lax.dot_general(gp[src, :], w_in[cols, :], NT, preferred_element_type=F32)
                if SLOT[j] < 2:
                    cs[dst, cols] = value.astype(BF)
                else:
                    pbuf[dst, cols] = value
                return carry

            lax.fori_loop(0, width // TILE, body, 0)
            if j == 3:
                core_copy(c).start()

    def pass_on(c):
        lo, hi = spans[c]
        r = hi - lo
        core_copy(c).wait_recv()
        xs[lo:hi, :] = (pbuf[2 * lo:2 * lo + r, :] + cr[2 * lo + r:2 * lo + 2 * r, :].astype(F32)).astype(BF)
        x_copy(c).start()

    project(0)
    for c in range(count):
        if c + 1 < count:
            project(c + 1)
        pass_on(c)
        if c == 0:
            input_grad(1)
            sumq[1].reduce(0, fresh=True)
            settle(sumq[0])
        if c == 2:
            sum1.gather(4)
            sumo.gather(5)

    acc[...] = jnp.zeros_like(acc)
    for c in range(count):
        x_copy(c).wait_recv()
        lo, hi = spans[c]
        r = hi - lo
        step = next(t for t in (48, 64, 32, 16) if r % t == 0)

        def pulls(i, carry):
            kept = pl.ds(pl.multiple_of(2 * lo + r + i * step, 16), step)
            close = pl.ds(pl.multiple_of(2 * lo + i * step, 16), step)
            rows = pl.ds(pl.multiple_of(lo + i * step, 16), step)
            total = pbuf[kept, :] + cr[close, :].astype(F32) + xr[rows, :].astype(F32)
            unit, inv = norm_stats(tokens[rows, :].astype(F32))
            acc[0:8, :] += fold8(total * unit)
            acc[8:16, :] += fold8(total)
            tgrad[rows, :] = (ghid[rows, :] + norm_pull(total, gain0[...], unit, inv)).astype(BF)
            return carry

        lax.fori_loop(0, r // step, pulls, 0)
        if c == 0:
            sumq[0].gather(4)
            sumq[1].reduce(1)
        elif c == 1:
            sum1.gather(5)
        elif c == 2:
            sumq[0].gather(5)
            sumq[1].reduce(2)

    small[...] = small_in[...]
    small[0:1, :] = jnp.sum(acc[0:8, :], axis=0, keepdims=True)
    small[1:2, :] = jnp.sum(acc[8:16, :], axis=0, keepdims=True)
    bias = jnp.sum(gp[...].astype(F32), axis=0, keepdims=True)
    small[11:12, 0:part] = bias[:, 0:part]
    small[11:12, part:2 * part] = bias[:, 2 * part:3 * part]

    def near_copy(i):
        return pltpu.make_async_remote_copy(
            src_ref=small, dst_ref=near.at[me], send_sem=nsend.at[i], recv_sem=nrecv.at[i], device_id=near_peers[i],
            device_id_type=MESH,
        )

    def far_copy(i):
        return pltpu.make_async_remote_copy(
            src_ref=small_out, dst_ref=far.at[dp], send_sem=fsend.at[i], recv_sem=frecv.at[i], device_id=far_peers[i],
            device_id_type=MESH,
        )

    for i in range(3):
        near_copy(i).start()
    settle(sumq[1])
    for i in range(3):
        near_copy(i).wait_recv()
    own = lax.broadcasted_iota(jnp.int32, (16, 1), 0) >= 10
    near[me] = small[...]
    small_out[...] = jnp.where(own, small[...], ((near[0] + near[1]) + near[2]) + near[3])
    for i in range(7):
        far_copy(i).start()
    sumq[1].gather(4)
    for i in range(7):
        far_copy(i).wait_recv()
    for i in range(7):
        far_copy(i).wait_send()
    far[dp] = small_out[...]
    total = far[0]
    for i in range(1, 8):
        total = total + far[i]
    small_out[...] = total
    sumq[1].gather(5)

    sum2.finish(3)
    sum1.finish(1)
    sumo.finish()
    sumq[0].finish()
    sumq[1].finish()
    for i in range(3):
        near_copy(i).wait_send()
    for c in range(count):
        core_copy(c).wait_send()
        x_copy(c).wait_send()


def back(bounds, q, k, v, o, do, lse, xfull, w_in, ghid, tokens, gain0, w2e, w1h, wog, small):
    seq, part = q.shape
    local, width = tokens.shape
    units = w1h.shape[1]
    pair = part // 2
    vmem = pl.BlockSpec(memory_space=pltpu.VMEM)
    shape = jax.ShapeDtypeStruct
    low = lambda *dims: pltpu.VMEM(dims, BF)
    wide = lambda *dims: pltpu.VMEM(dims, F32)
    dma = lambda n: pltpu.SemaphoreType.DMA((n,))
    return pl.pallas_call(
        back_kernel,
        in_specs=[pl.BlockSpec(memory_space=pltpu.SMEM)] + [vmem] * 15,
        out_specs=[vmem] * 6,
        out_shape=[
            shape((local, width), BF), shape((8 * w2e.shape[0], width), BF), shape((width, units), BF),
            shape((part, width), BF), shape((2, 3 * pair, width), BF), shape((16, width), F32),
        ],
        scratch_shapes=[
            low(seq, part), low(seq, part), wide(part, seq), wide(8, seq), low(seq, 3 * part),
            wide(2, 3 * pair, width), wide(part, width), wide(2 * local, width), low(2 * local, width),
            low(2 * local, width), low(local, width), low(local, width), wide(16, width),
            low(width // 4, units), low(width // 8, units), low(width // 4, units), low(width // 8, units),
            low(part // 2, width), low(part // 4, width), low(part // 8, width),
            low(part // 2, width), low(part // 4, width), low(part // 8, width),
            low(2, 3 * pair // 2, width), low(2, 3 * pair // 4, width), low(2, 3 * pair // 8, width),
            low(2, 3 * pair // 2, width), low(2, 3 * pair // 4, width), low(2, 3 * pair // 8, width),
            wide(16, width), wide(4, 16, width), wide(8, 16, width),
            dma(8), dma(8), dma(30), dma(30), dma(3), dma(3), dma(7), dma(7),
        ],
        compiler_params=pltpu.CompilerParams(collective_id=1, has_side_effects=True, vmem_limit_bytes=63 << 20),
        cost_estimate=pl.CostEstimate(flops=20 << 30, bytes_accessed=40 << 20, transcendentals=8 << 20),
        name="back",
    )(bounds, q, k, v, o, do, lse, xfull, w_in, ghid, tokens, gain0, w2e, w1h, wog, small)


def rest_by_ops(
    head_low, rows_in, cotangent, wout, out_bias, w1, b1, w2, b2, gains, shifts, rel_of, sort, bounds, queries, keys,
    values, lse, attn_full, w_in, pull_a,
):
    local_rows, width = rows_in.shape
    size = lax.axis_size("mp")
    seq_len, head_part = head_low.shape
    head_rel = rel_of(head_low)
    grad_out_all = cotangent.astype(F32)
    state = []
    for lo, hi in [(0, local_rows)]:
        rows = hi - lo
        total = size * rows
        attn_out = scatter_rel(
            jnp.dot(head_rel[:, lo:hi], wout, preferred_element_type=F32), "mp"
        ) + out_bias.astype(F32)
        norm_b, pull_b = jax.vjp(layer_norm, attn_out, gains[1], shifts[1])
        hidden_rows = rows_in[lo:hi] + norm_b
        norm_c, pull_c = jax.vjp(layer_norm, hidden_rows, gains[2], shifts[2])
        mlp_full = gather_rel(norm_c.astype(BF), "mp").reshape(total, width)
        pre_act = jnp.dot(mlp_full, w1, preferred_element_type=F32) + b1.astype(F32)
        activated, gelu_pull = jax.vjp(gelu_tanh, pre_act)
        act_low = activated.astype(BF)
        branch = scatter_rel(
            jnp.dot(act_low, w2, preferred_element_type=F32).reshape(size, rows, width), "mp"
        ) + b2.astype(F32)
        norm_d, pull_d = jax.vjp(layer_norm, branch, gains[3], shifts[3])
        mixed = (hidden_rows + norm_d).astype(BF)
        grad_out = grad_out_all[lo:hi]
        grad_branch, gain_d, shift_d = pull_d(grad_out)
        branch_low = grad_branch.astype(BF)
        b2_part = jnp.sum(branch_low.astype(F32), axis=0)
        branch_full = gather_rel(branch_low, "mp").reshape(total, width)
        grad_act = jnp.einsum("td,fd->tf", branch_full, w2, preferred_element_type=F32)
        grad_pre = gelu_pull(grad_act)[0].astype(BF)
        b1_part = jnp.sum(grad_pre.astype(F32), axis=0)
        grad_norm_c = scatter_rel(
            jnp.einsum("tf,df->td", grad_pre, w1, preferred_element_type=F32).reshape(size, rows, width), "mp"
        )
        grad_hidden_c, gain_c, shift_c = pull_c(grad_norm_c)
        grad_hidden = grad_out + grad_hidden_c
        grad_attn, gain_b, shift_b = pull_b(grad_hidden)
        attn_grad_low = grad_attn.astype(BF)
        out_bias_part = jnp.sum(attn_grad_low.astype(F32), axis=0)
        attn_grad_rel = gather_rel(attn_grad_low, "mp")
        state.append(dict(
            mixed=mixed, act=act_low, branch=branch_full, mlp=mlp_full, pre=grad_pre, hidden=grad_hidden,
            attn=attn_grad_rel, heads=head_rel[:, lo:hi].reshape(total, head_part),
            gh=jnp.einsum("jtd,cd->jtc", attn_grad_rel, wout, preferred_element_type=F32).astype(BF),
            sums=jnp.stack([gain_b, gain_c, gain_d, shift_b, shift_c, shift_d, out_bias_part, b2_part]),
            b1=b1_part,
        ))

    def joined(name, axis=0):
        return jnp.concatenate([s[name] for s in state], axis=axis)

    w2_grad = jnp.einsum("tf,td->fd", joined("act"), joined("branch"), preferred_element_type=F32)
    w2_grad = reduce_all(w2_grad, "dp")
    w1_grad = jnp.einsum("td,tf->df", joined("mlp"), joined("pre"), preferred_element_type=F32)
    w1_grad = reduce_all(w1_grad, "dp")
    attn_grad_full = joined("attn", 1).reshape(seq_len, width)
    wout_grad = jnp.einsum(
        "tc,td->cd", head_rel.reshape(seq_len, head_part), attn_grad_full, preferred_element_type=F32
    )
    wout_grad = reduce_all(wout_grad, "dp")
    grad_heads = sort(joined("gh", 1))
    mixed, grad_hidden = joined("mixed"), joined("hidden")
    mid_sums = sum(s["sums"] for s in state)
    b1_grad = sum(s["b1"] for s in state)
    grads = attn_bwd(bounds, queries, keys, values, head_low, grad_heads, lse)
    grad_proj = jnp.concatenate(grads, axis=1)
    part_sums = jnp.sum(grad_proj.astype(F32), axis=0).reshape(3, head_part)
    qv_part = jnp.stack([part_sums[0], part_sums[2]])
    wqkv_grad = jnp.einsum("td,tc->dc", attn_full, grad_proj, preferred_element_type=F32)
    wqkv_grad = reduce_all(wqkv_grad, "dp").reshape(width, 3, head_part)
    grad_rel = rel_of(grad_proj)
    grad_norm_a = scatter_rel(jnp.einsum("jtc,dc->jtd", grad_rel, w_in, preferred_element_type=F32), "mp")
    grad_rows_a, gain_a, shift_a = pull_a(grad_norm_a)
    tokens_grad = (grad_hidden + grad_rows_a).astype(BF)
    own_sums = sum_small(jnp.concatenate([qv_part.reshape(-1), b1_grad]), ("dp",))
    qv_sum = own_sums[: 2 * head_part].reshape(2, head_part)
    b1_sum = own_sums[2 * head_part:]
    stack = jnp.concatenate([gain_a[None], mid_sums[0:3], shift_a[None], mid_sums[3:8]])
    stack = sum_small(stack, ("mp", "dp"))
    return (
        mixed, tokens_grad, wqkv_grad, qv_sum, wout_grad, stack[8], w1_grad, b1_sum, w2_grad, stack[9],
        stack[0:4], stack[4:8],
    )


def shards(
    tokens, caption_len, row_offset, wqkv, qv_bias, wout, out_bias, w1, b1, w2, b2, ln_gain, ln_bias, cotangent,
):
    local_rows, width = tokens.shape
    size = lax.axis_size("mp")
    seq_len = local_rows * size
    head_part = wqkv.shape[2]
    gains = ln_gain.astype(F32)
    shifts = ln_bias.astype(F32)
    me = lax.axis_index("mp")

    def pick(blocks):
        return jnp.concatenate(
            [lax.dynamic_index_in_dim(blocks, me ^ j, 0, keepdims=True) for j in range(size)], axis=0
        )

    first = row_offset[0]
    second = first + caption_len[0, 0] + IMG
    third = second + caption_len[0, 1] + IMG
    bounds = jnp.stack([first, second, third]).astype(jnp.int32)

    def sort(rel):
        return pick(rel).reshape((seq_len,) + rel.shape[2:])

    def rel_of(rows):
        return pick(rows.reshape((size, local_rows) + rows.shape[1:]))

    rows_in = tokens.astype(F32)
    norm_a, pull_a = jax.vjp(layer_norm, rows_in, gains[0], shifts[0])
    attn_full = sort(gather_rel(norm_a.astype(BF), "mp"))
    w_in = wqkv.reshape(width, 3 * head_part)
    projected = jnp.dot(attn_full, w_in, preferred_element_type=F32)
    bias3 = jnp.concatenate([qv_bias[0], jnp.zeros_like(qv_bias[0]), qv_bias[1]]).astype(F32)
    projected = (projected + bias3).astype(BF)
    queries, keys, values = [projected[:, i * head_part:(i + 1) * head_part] for i in range(3)]
    head_low, lse = attn_fwd(bounds, queries, keys, values)
    whole = lax.axis_size("dp") == 8 and size == 4 and head_part == TILE and width == w1.shape[1] == 1024
    if not (whole and local_rows % 32 == 0):
        return rest_by_ops(
            head_low, rows_in, cotangent, wout, out_bias, w1, b1, w2, b2, gains, shifts, rel_of, sort, bounds,
            queries, keys, values, lse, attn_full, w_in, pull_a,
        )
    vec = jnp.stack(
        [out_bias.astype(F32), b2.astype(F32), gains[1], shifts[1], gains[2], shifts[2], gains[3], shifts[3]]
    )
    mixed, grad_hidden, grad_heads, w2_part, w1_part, wout_part, sums, b1_part = middle(
        head_low, tokens, cotangent, wout, w1, w2, b1.astype(F32)[None], vec
    )
    small = jnp.concatenate([jnp.zeros((2, width), F32), sums, b1_part, jnp.zeros((5, width), F32)])
    tokens_grad, w2_grad, w1_grad, wout_grad, wqkv_grad, small = back(
        bounds, queries, keys, values, head_low, grad_heads, lse, attn_full, w_in, grad_hidden, tokens, gains[0:1],
        w2_part, w1_part, wout_part, small,
    )
    wqkv_grad = wqkv_grad.reshape(2, 3, head_part // 2, width).transpose(3, 1, 0, 2).reshape(width, 3, head_part)
    gain_stack = jnp.concatenate([small[0:1], small[2:5]])
    shift_stack = jnp.concatenate([small[1:2], small[5:8]])
    return (
        mixed, tokens_grad, wqkv_grad.astype(F32), small[11, : 2 * head_part].reshape(2, head_part),
        wout_grad.astype(F32), small[8], w1_grad.astype(F32), small[10], w2_grad.astype(F32), small[9],
        gain_stack, shift_stack,
    )


def solution(mesh):
    rows = P(("dp", "mp"), None)
    placed = (
        rows, P("dp", None), P("dp"), P(None, None, "mp"), P(None, "mp"), P("mp", None), P(), P(None, "mp"),
        P("mp"), P("mp", None), P(), P(), P(), rows,
    )
    return jax.shard_map(
        shards,
        mesh=mesh,
        in_specs=placed,
        out_specs=(
            rows, rows, P(None, None, "mp"), P(None, "mp"), P("mp", None), P(), P(None, "mp"), P("mp"),
            P("mp", None), P(), P(), P(),
        ),
        check_vma=False,
    )
```

```python
import functools
import jax, jax.numpy as jnp
from jax import lax
from jax.experimental import pallas as pl
from jax.experimental.pallas import tpu as pltpu
from jax.sharding import PartitionSpec as P
HEAD=64; IMG=1024; CAP_MIN=5; LANES=128
F32=jnp.float32; BF=jnp.bfloat16
MESH=pl.DeviceIdType.MESH
NT=(((1,),(1,)),((),()))
TN=(((0,),(0,)),((),()))

def plan(seq):
    least=IMG+CAP_MIN
    slack=seq-2*least
    lo=least//LANES*LANES
    hi=-(-(seq-least)//LANES)*LANES
    head_pad=-(-slack//LANES)*LANES
    tail_pad=(2*least)//LANES*LANES
    def cut(a,b,step):
        out=[]
        while a<b:
            out.append((a,min(a+step,b))); a=min(a+step,b)
        return out
    return lo,hi,head_pad,tail_pad,cut

def free_of_mask(k0,k1,q0,q1,seq):
    lo,hi,head_pad,tail_pad,_=plan(seq)
    if k1>q0: return False
    if q1<=lo: return k0>=head_pad
    if q0>=hi: return k0>=hi and q1<=tail_pad
    return False

def seg_start(pos,b0,b1,b2):
    return jnp.where(pos>=b2,b2,jnp.where(pos>=b1,b1,jnp.where(pos>=b0,b0,0)))

def fwd_kernel(bounds,q_ref,k_ref,v_ref,o_ref,lse_ref):
    seq,width=q_ref.shape
    h=pl.program_id(0)
    b0,b1,b2=bounds[0],bounds[1],bounds[2]
    lo,hi,_,_,cut=plan(seq)
    lane=lax.broadcasted_iota(jnp.int32,(1,width),1)
    mine=(lane//HEAD)==h
    blocks=[(a,b,0) for a,b in cut(0,lo,256)]+[(a,b,0) for a,b in cut(lo,hi,256)]+[(a,b,lo) for a,b in cut(hi,seq,256)]
    for a,b,start in blocks:
        n=b-a
        qm=jnp.where(mine,q_ref[a:b,:].astype(F32)*HEAD**-0.5,0.0).astype(BF)
        qpos=a+lax.broadcasted_iota(jnp.int32,(n,1),0)
        first=seg_start(qpos,b0,b1,b2)
        parts=[]
        top=None
        for c,d in cut(start,b,128):
            s=lax.dot_general(qm,k_ref[c:d,:],NT,preferred_element_type=F32)
            if not free_of_mask(c,d,a,b,seq):
                kpos=c+lax.broadcasted_iota(jnp.int32,(n,d-c),1)
                s=jnp.where((kpos>=first)&(kpos<=qpos),s,-1e9)
            parts.append(s)
            top=s if top is None else jnp.maximum(top,s)
        m=jnp.max(top,axis=1,keepdims=True)
        es=[jnp.exp(s-m) for s in parts]
        tot=es[0]
        for e in es[1:]: tot=tot+e
        l=jnp.sum(tot,axis=1,keepdims=True)
        p=jnp.concatenate([e.astype(BF) for e in es],axis=1)
        o=jnp.dot(p,v_ref[start:b,:],preferred_element_type=F32)/l
        o_ref[a:b,:]=jnp.where(mine,o.astype(BF),o_ref[a:b,:])
        lse=m+jnp.log(l)
        lse_ref[0,:,a:b]=jnp.broadcast_to(lse,(n,128)).T[0:8,:]

def bwd_kernel(bounds,q_ref,k_ref,v_ref,o_ref,do_ref,lse_ref,dq_ref,dk_ref,dv_ref,qm_s,dom_s,dqt_s,delta_s):
    seq,width=q_ref.shape
    h=pl.program_id(0)
    b0,b1,b2=bounds[0],bounds[1],bounds[2]
    lo,hi,_,_,cut=plan(seq)
    lane=lax.broadcasted_iota(jnp.int32,(1,width),1)
    mine=(lane//HEAD)==h
    qm_s[...]=jnp.where(mine,q_ref[...].astype(F32)*HEAD**-0.5,0.0).astype(BF)
    dom_s[...]=jnp.where(mine,do_ref[...],jnp.zeros((),BF))
    ones=jnp.ones((8,width),F32)
    for a,b in cut(0,seq,256):
        prod=dom_s[a:b,:].astype(F32)*o_ref[a:b,:].astype(F32)
        delta_s[:,a:b]=lax.dot_general(ones,prod,NT,preferred_element_type=F32,precision=lax.Precision.HIGHEST)
    dqt_s[...]=jnp.zeros_like(dqt_s)
    blocks=[(a,b,hi) for a,b in cut(0,lo,256)]+[(a,b,seq) for a,b in cut(lo,hi,256)]+[(a,b,seq) for a,b in cut(hi,seq,256)]
    for a,b,stop in blocks:
        n=b-a
        kk=k_ref[a:b,:]; vv=v_ref[a:b,:]
        kpos=a+lax.broadcasted_iota(jnp.int32,(n,1),0)
        kh=jnp.where(mine,kk,jnp.zeros((),BF))
        pts=[];dsts=[]
        for c,d in cut(a,stop,128):
            st=lax.dot_general(kk,qm_s[c:d,:],NT,preferred_element_type=F32)
            pt=jnp.exp(st-lse_ref[0,0:1,c:d])
            if not free_of_mask(a,b,c,d,seq):
                qpos=c+lax.broadcasted_iota(jnp.int32,(1,d-c),1)
                first=seg_start(qpos,b0,b1,b2)
                pt=jnp.where((kpos>=first)&(kpos<=qpos),pt,0.0)
            dpt=lax.dot_general(vv,dom_s[c:d,:],NT,preferred_element_type=F32)
            dst=pt*(dpt-delta_s[0:1,c:d])
            pts.append(pt.astype(BF)); dsts.append(dst.astype(BF))
        pt=jnp.concatenate(pts,axis=1); dst=jnp.concatenate(dsts,axis=1)
        dv=jnp.dot(pt,dom_s[a:stop,:],preferred_element_type=F32)
        dk=jnp.dot(dst,qm_s[a:stop,:],preferred_element_type=F32)
        dv_ref[a:b,:]=jnp.where(mine,dv.astype(BF),dv_ref[a:b,:])
        dk_ref[a:b,:]=jnp.where(mine,dk.astype(BF),dk_ref[a:b,:])
        dqt_s[:,a:stop]+=lax.dot_general(kh,dst,TN,preferred_element_type=F32)
    for a,b in cut(0,seq,128):
        dq=(dqt_s[:,a:b]*HEAD**-0.5).T
        dq_ref[a:b,:]=jnp.where(mine,dq.astype(BF),dq_ref[a:b,:])

def attn_fwd(bounds,q,k,v):
    seq,width=q.shape; H=width//HEAD
    full=pl.BlockSpec((seq,width),lambda h:(0,0))
    return pl.pallas_call(fwd_kernel,grid=(H,),
        in_specs=[pl.BlockSpec(memory_space=pltpu.SMEM),full,full,full],
        out_specs=[full,pl.BlockSpec((1,8,seq),lambda h:(h,0,0))],
        out_shape=[jax.ShapeDtypeStruct((seq,width),BF),jax.ShapeDtypeStruct((H,8,seq),F32)],
        compiler_params=pltpu.CompilerParams(vmem_limit_bytes=56<<20),name="attn_fwd")(bounds,q,k,v)

def attn_bwd(bounds,q,k,v,o,do,lse):
    seq,width=q.shape; H=width//HEAD
    full=pl.BlockSpec((seq,width),lambda h:(0,0))
    sh=jax.ShapeDtypeStruct((seq,width),BF)
    return pl.pallas_call(bwd_kernel,grid=(H,),
        in_specs=[pl.BlockSpec(memory_space=pltpu.SMEM),full,full,full,full,full,pl.BlockSpec((1,8,seq),lambda h:(h,0,0))],
        out_specs=[full,full,full],out_shape=[sh,sh,sh],
        scratch_shapes=[pltpu.VMEM((seq,width),BF),pltpu.VMEM((seq,width),BF),pltpu.VMEM((width,seq),F32),pltpu.VMEM((8,seq),F32)],
        compiler_params=pltpu.CompilerParams(vmem_limit_bytes=56<<20),name="attn_bwd")(bounds,q,k,v,o,do,lse)

eps_norm = 1e-05


def layer_norm(values, gain, shift):
    center = values - jnp.mean(values, axis=-1, keepdims=True)
    spread = jnp.mean(center * center, axis=-1, keepdims=True)
    return center * lax.rsqrt(spread + eps_norm) * gain + shift


def gelu_tanh(values):
    return jax.nn.gelu(values, approximate=True)


def swap(values, axis, mask):
    size = lax.axis_size(axis)
    return lax.ppermute(values, axis, [(i, i ^ mask) for i in range(size)])


def masks_of(axis):
    size = lax.axis_size(axis)
    out = []
    step = size // 2
    while step:
        out.append(step)
        step //= 2
    return out


def gather_rel(block, axis):
    have = {0: block}
    for mask in masks_of(axis):
        have.update({j ^ mask: swap(v, axis, mask) for j, v in list(have.items())})
    return jnp.stack([have[j] for j in range(lax.axis_size(axis))])


def scatter_rel(parts, axis):
    have = {j: parts[j] for j in range(parts.shape[0])}
    for mask in reversed(masks_of(axis)):
        got = {j: swap(have[j].astype(BF), axis, mask) for j in have if j & mask}
        have = {j: have[j] + got[j ^ mask].astype(F32) for j in have if not j & mask}
    return have[0]


def reduce_all(values, axis):
    me = lax.axis_index(axis)
    masks = list(reversed(masks_of(axis)))
    rows = values.shape[0]
    for mask in masks:
        rows //= 2
        bit = (me // mask) % 2
        keep = lax.dynamic_slice_in_dim(values, bit * rows, rows, 0)
        send = lax.dynamic_slice_in_dim(values, (1 - bit) * rows, rows, 0)
        values = keep + swap(send.astype(BF), axis, mask).astype(F32)
    low = values.astype(BF)
    for mask in reversed(masks):
        bit = (me // mask) % 2
        got = swap(low, axis, mask)
        both = jnp.concatenate([low, got], axis=0)
        flipped = jnp.concatenate([got, low], axis=0)
        low = jnp.where(bit == 0, both, flipped)
    return low.astype(F32)


def sum_small(values, axes):
    for axis in axes:
        for mask in masks_of(axis):
            values = values + swap(values, axis, mask)
    return values


def shards_by_ops(
    tokens, caption_len, row_offset, wqkv, qv_bias, wout, out_bias, w1, b1, w2, b2, ln_gain, ln_bias, cotangent,
):
    local_rows, width = tokens.shape
    size = lax.axis_size("mp")
    seq_len = local_rows * size
    head_part = wqkv.shape[2]
    gains = ln_gain.astype(F32)
    shifts = ln_bias.astype(F32)
    me = lax.axis_index("mp")

    def pick(blocks):
        return jnp.concatenate(
            [lax.dynamic_index_in_dim(blocks, me ^ j, 0, keepdims=True) for j in range(size)], axis=0
        )

    first = row_offset[0]
    second = first + caption_len[0, 0] + IMG
    third = second + caption_len[0, 1] + IMG
    bounds = jnp.stack([first, second, third]).astype(jnp.int32)

    def sort(rel):
        return pick(rel).reshape((seq_len,) + rel.shape[2:])

    def rel_of(rows):
        return pick(rows.reshape((size, local_rows) + rows.shape[1:]))

    rows_in = tokens.astype(F32)
    norm_a, pull_a = jax.vjp(layer_norm, rows_in, gains[0], shifts[0])
    attn_full = sort(gather_rel(norm_a.astype(BF), "mp"))
    w_in = wqkv.reshape(width, 3 * head_part)
    projected = jnp.dot(attn_full, w_in, preferred_element_type=F32)
    bias3 = jnp.concatenate([qv_bias[0], jnp.zeros_like(qv_bias[0]), qv_bias[1]]).astype(F32)
    projected = (projected + bias3).astype(BF)
    queries, keys, values = [projected[:, i * head_part:(i + 1) * head_part] for i in range(3)]
    head_low, lse = attn_fwd(bounds, queries, keys, values)
    head_rel = rel_of(head_low)
    grad_out_all = cotangent.astype(F32)
    state = []
    for lo, hi in [(0, local_rows)]:
        rows = hi - lo
        total = size * rows
        attn_out = scatter_rel(
            jnp.dot(head_rel[:, lo:hi], wout, preferred_element_type=F32), "mp"
        ) + out_bias.astype(F32)
        norm_b, pull_b = jax.vjp(layer_norm, attn_out, gains[1], shifts[1])
        hidden_rows = rows_in[lo:hi] + norm_b
        norm_c, pull_c = jax.vjp(layer_norm, hidden_rows, gains[2], shifts[2])
        mlp_full = gather_rel(norm_c.astype(BF), "mp").reshape(total, width)
        pre_act = jnp.dot(mlp_full, w1, preferred_element_type=F32) + b1.astype(F32)
        activated, gelu_pull = jax.vjp(gelu_tanh, pre_act)
        act_low = activated.astype(BF)
        branch = scatter_rel(
            jnp.dot(act_low, w2, preferred_element_type=F32).reshape(size, rows, width), "mp"
        ) + b2.astype(F32)
        norm_d, pull_d = jax.vjp(layer_norm, branch, gains[3], shifts[3])
        mixed = (hidden_rows + norm_d).astype(BF)
        grad_out = grad_out_all[lo:hi]
        grad_branch, gain_d, shift_d = pull_d(grad_out)
        branch_low = grad_branch.astype(BF)
        b2_part = jnp.sum(branch_low.astype(F32), axis=0)
        branch_full = gather_rel(branch_low, "mp").reshape(total, width)
        grad_act = jnp.einsum("td,fd->tf", branch_full, w2, preferred_element_type=F32)
        grad_pre = gelu_pull(grad_act)[0].astype(BF)
        b1_part = jnp.sum(grad_pre.astype(F32), axis=0)
        grad_norm_c = scatter_rel(
            jnp.einsum("tf,df->td", grad_pre, w1, preferred_element_type=F32).reshape(size, rows, width), "mp"
        )
        grad_hidden_c, gain_c, shift_c = pull_c(grad_norm_c)
        grad_hidden = grad_out + grad_hidden_c
        grad_attn, gain_b, shift_b = pull_b(grad_hidden)
        attn_grad_low = grad_attn.astype(BF)
        out_bias_part = jnp.sum(attn_grad_low.astype(F32), axis=0)
        attn_grad_rel = gather_rel(attn_grad_low, "mp")
        state.append(dict(
            mixed=mixed, act=act_low, branch=branch_full, mlp=mlp_full, pre=grad_pre, hidden=grad_hidden,
            attn=attn_grad_rel, heads=head_rel[:, lo:hi].reshape(total, head_part),
            gh=jnp.einsum("jtd,cd->jtc", attn_grad_rel, wout, preferred_element_type=F32).astype(BF),
            sums=jnp.stack([gain_b, gain_c, gain_d, shift_b, shift_c, shift_d, out_bias_part, b2_part]),
            b1=b1_part,
        ))

    def joined(name, axis=0):
        return jnp.concatenate([s[name] for s in state], axis=axis)

    w2_grad = jnp.einsum("tf,td->fd", joined("act"), joined("branch"), preferred_element_type=F32)
    w2_grad = reduce_all(w2_grad, "dp")
    w1_grad = jnp.einsum("td,tf->df", joined("mlp"), joined("pre"), preferred_element_type=F32)
    w1_grad = reduce_all(w1_grad, "dp")
    attn_grad_full = joined("attn", 1).reshape(seq_len, width)
    wout_grad = jnp.einsum(
        "tc,td->cd", head_rel.reshape(seq_len, head_part), attn_grad_full, preferred_element_type=F32
    )
    wout_grad = reduce_all(wout_grad, "dp")
    grad_heads = sort(joined("gh", 1))
    mixed, grad_hidden = joined("mixed"), joined("hidden")
    mid_sums = sum(s["sums"] for s in state)
    b1_grad = sum(s["b1"] for s in state)
    grads = attn_bwd(bounds, queries, keys, values, head_low, grad_heads, lse)
    grad_proj = jnp.concatenate(grads, axis=1)
    part_sums = jnp.sum(grad_proj.astype(F32), axis=0).reshape(3, head_part)
    qv_part = jnp.stack([part_sums[0], part_sums[2]])
    wqkv_grad = jnp.einsum("td,tc->dc", attn_full, grad_proj, preferred_element_type=F32)
    wqkv_grad = reduce_all(wqkv_grad, "dp").reshape(width, 3, head_part)
    grad_rel = rel_of(grad_proj)
    grad_norm_a = scatter_rel(jnp.einsum("jtc,dc->jtd", grad_rel, w_in, preferred_element_type=F32), "mp")
    grad_rows_a, gain_a, shift_a = pull_a(grad_norm_a)
    tokens_grad = (grad_hidden + grad_rows_a).astype(BF)
    own_sums = sum_small(jnp.concatenate([qv_part.reshape(-1), b1_grad]), ("dp",))
    qv_sum = own_sums[: 2 * head_part].reshape(2, head_part)
    b1_sum = own_sums[2 * head_part:]
    stack = jnp.concatenate([gain_a[None], mid_sums[0:3], shift_a[None], mid_sums[3:8]])
    stack = sum_small(stack, ("mp", "dp"))
    return (
        mixed, tokens_grad, wqkv_grad, qv_sum, wout_grad, stack[8], w1_grad, b1_sum, w2_grad, stack[9],
        stack[0:4], stack[4:8],
    )


SLOT = {1: 0, 3: 1, 2: 2, 0: 3}
TILE = 256


def spans_of(rows):
    units = rows // 16
    sizes = [16 * (units // 4 + (1 if i < units % 4 else 0)) for i in range(4)]
    edges = [sum(sizes[:i]) for i in range(5)]
    return [(edges[i], edges[i + 1]) for i in range(4)]


def fold8(values):
    rows, cols = values.shape
    return jnp.sum(values.reshape(rows // 8, 8, cols), axis=0)


def norm_stats(values):
    center = values - jnp.mean(values, axis=-1, keepdims=True)
    inv = lax.rsqrt(jnp.mean(center * center, axis=-1, keepdims=True) + eps_norm)
    return center * inv, inv


def norm_pull(upstream, gain, unit, inv):
    scaled = upstream * gain
    first = jnp.mean(scaled, axis=-1, keepdims=True)
    second = jnp.mean(scaled * unit, axis=-1, keepdims=True)
    return (scaled - first - unit * second) * inv


def dp_place():
    dp, me = lax.axis_index("dp"), lax.axis_index("mp")
    y, low, high = dp % 2, dp // 2 % 2, dp // 4
    return (y, low, high), (
        (dp + 1 - 2 * y, me), (dp + 2 * (1 - 2 * low), me), (dp + 4 * (1 - 2 * high), me)
    )


def by_rows(count, body):
    step = next(t for t in (64, 48, 32, 16) if count % t == 0)

    def trip(i, carry):
        body(pl.multiple_of(i * step, 16), step)
        return carry

    lax.fori_loop(0, count // step, trip, 0)


class Reduction:
    def __init__(self, rows, work, first, held, sbuf, rbuf, full, send, recv, base, order=(0, 1, 2)):
        self.rows, self.work, self.first, self.held, self.full = rows, work, first, held, full
        self.sbuf, self.rbuf, self.send, self.recv, self.base = sbuf, rbuf, send, recv, base
        bits, peers = dp_place()
        self.bits, self.peers = [bits[i] for i in order], [peers[i] for i in order]
        off = [0]
        for k in range(3):
            off.append(off[-1] + self.bits[k] * (rows >> (k + 1)))
        self.off = off
        self.steps = 6

    def copy(self, i):
        if i < 3:
            src, dst, peer = self.sbuf[i], self.rbuf[i], self.peers[i]
        else:
            k = 5 - i
            part = self.full.at[pl.ds(pl.multiple_of(self.off[k + 1], 16), self.rows >> (k + 1))]
            src, dst, peer = part, part, self.peers[k]
        return pltpu.make_async_remote_copy(
            src_ref=src, dst_ref=dst, send_sem=self.send.at[self.base + i], recv_sem=self.recv.at[self.base + i],
            device_id=peer, device_id_type=MESH,
        )

    def copies(self, i):
        return (self.copy(i),)

    def arrive(self, i):
        for copy in self.copies(i):
            copy.wait_recv()

    def leave(self, i):
        for copy in self.copies(i):
            copy.wait_send()

    def depart(self, i):
        for copy in self.copies(i):
            copy.start()

    def at(self, offset, i, step):
        return pl.ds(pl.multiple_of(offset + i - self.off[self.held], 16), step)

    def halve(self, k):
        n = self.rows >> (k + 1)
        bit = self.bits[k]
        give, keep = self.off[k] + (1 - bit) * n, self.off[k] + bit * n
        fresh = k == self.first

        def out(i, step):
            value = self.work[self.at(give, i, step), :]
            if not fresh:
                value = value + self.rbuf[k - 1][pl.ds(pl.multiple_of((1 - bit) * n + i, 16), step), :].astype(F32)
            self.sbuf[k][pl.ds(i, step), :] = value.astype(BF)

        def stay(i, step):
            rows = self.at(keep, i, step)
            self.work[rows, :] += self.rbuf[k - 1][pl.ds(pl.multiple_of(bit * n + i, 16), step), :].astype(F32)

        by_rows(n, out)
        self.depart(k)
        if not fresh:
            by_rows(n, stay)

    def settle(self, dst, at):
        def body(i, step):
            value = self.work[self.at(self.off[3], i, step), :] + self.rbuf[2][pl.ds(i, step), :].astype(F32)
            dst[pl.ds(pl.multiple_of(at + i, 16), step), :] = value.astype(dst.dtype)

        by_rows(self.rows >> 3, body)

    def step(self, i):
        if i > self.first:
            self.arrive(i - 1)
        if i < 3:
            self.halve(i)
        else:
            if i == 3:
                self.settle(self.full, self.off[3])
            self.depart(i)

    def drain(self):
        for i in range(self.first, self.steps):
            self.leave(i)


class Direct(Reduction):
    def __init__(self, rows, work, sbuf, rbuf, full, send, recv, base):
        super().__init__(rows, work, 0, 0, sbuf, rbuf, full, send, recv, base)
        self.steps = 4
        self.z = lax.axis_index("dp") // 2
        self.y = lax.axis_index("dp") % 2

    def copies(self, i):
        me = lax.axis_index("mp")
        n = self.rows >> 3
        half = pl.ds(pl.multiple_of(self.off[1], 16), 4 * n)
        if i in (0, 3):
            part = self.full.at[half]
            pairs = [(self.sbuf[0], self.rbuf[0], self.peers[0])] if i == 0 else [(part, part, self.peers[0])]
        else:
            pairs = []
            own = self.full.at[pl.ds(pl.multiple_of(self.off[1] + self.z * n, 16), n)]
            for j in range(1, 4):
                there = (self.z + j) % 4
                peer = (2 * there + self.y, me)
                if i == 1:
                    src = self.sbuf[1].at[pl.ds(pl.multiple_of(there * n, 16), n)]
                    pairs.append((src, self.rbuf[1].at[pl.ds((j - 1) * n, n)], peer))
                else:
                    pairs.append((own, own, peer))
        first = self.base + (0, 1, 4, 7)[i]
        return [
            pltpu.make_async_remote_copy(
                src_ref=src, dst_ref=dst, send_sem=self.send.at[first + j], recv_sem=self.recv.at[first + j],
                device_id=peer, device_id_type=MESH,
            )
            for j, (src, dst, peer) in enumerate(pairs)
        ]

    def step(self, i):
        n = self.rows >> 3
        if i:
            self.arrive(i - 1)
        if i == 0:
            self.halve(0)
            return
        if i == 1:

            def spread(k, step):
                rows = self.at(self.off[1], k, step)
                value = self.work[rows, :] + self.rbuf[0][pl.ds(k, step), :].astype(F32)
                self.work[rows, :] = value
                self.sbuf[1][pl.ds(k, step), :] = value.astype(BF)

            by_rows(4 * n, spread)
        elif i == 2:

            def body(k, step):
                at = self.off[1] + self.z * n
                value = self.work[self.at(at, k, step), :]
                for j in range(3):
                    value = value + self.rbuf[1][pl.ds(pl.multiple_of(j * n + k, 16), step), :].astype(F32)
                self.full[pl.ds(pl.multiple_of(at + k, 16), step), :] = value.astype(BF)

            by_rows(n, body)
        self.depart(i)


def edges(lengths, offset):
    first = offset[0]
    second = first + lengths[0, 0] + IMG
    return first, second, second + lengths[0, 1] + IMG


def ahead_kernel(
    lengths, offset, tokens, cot, w3, wout, w1, w2, biases, ln_gain, ln_bias, qv_bias,
    xfull, qkv, heads, lse, mixed, ghid, ghead, w2q, w1p, w1q, wog, sums, b1sum,
    vec, b1, mlp, act, dgel, brn, gpre, u1, u2, hid, r1, pbuf, cs, cr, xs, xr, acc, b1acc,
    qkeep, s2y, r2y, r2z, rpy, rqz, rqw, send, recv, dsend, drecv, local_sem,
):
    local, width = tokens.shape
    seq, part = heads.shape
    hidden_units = w1.shape[1]
    spans = spans_of(local)
    count = len(spans)
    dp, me = lax.axis_index("dp"), lax.axis_index("mp")
    mx, mc = me // 2, me % 2
    peer_core = (dp, mx * 2 + 1 - mc)
    peer_x = (dp, (1 - mx) * 2 + mc)
    owner = {0: me, 1: mx * 2 + 1 - mc, 2: (1 - mx) * 2 + mc, 3: (1 - mx) * 2 + 1 - mc}

    barrier = pltpu.get_barrier_semaphore()
    bits, dp_peers = dp_place()
    for peer in (peer_core, peer_x) + dp_peers:
        pl.semaphore_signal(barrier, inc=1, device_id=peer, device_id_type=MESH)
    pl.semaphore_wait(barrier, 5)

    def remote(src, dst, phase, kind, c, device):
        i = (phase * 5 + kind) * count + c
        return pltpu.make_async_remote_copy(
            src_ref=src, dst_ref=dst, send_sem=send.at[i], recv_sem=recv.at[i], device_id=device, device_id_type=MESH
        )

    def core_copy(phase, c):
        lo, hi = spans[c]
        rows = pl.ds(2 * lo, 2 * (hi - lo))
        return remote(cs.at[rows], cr.at[rows], phase, 0, c, peer_core)

    def x_copy(phase, c):
        lo, hi = spans[c]
        rows = pl.ds(lo, hi - lo)
        return remote(xs.at[rows], xr.at[rows], phase, 1, c, peer_x)

    def block(c, j):
        lo, hi = spans[c]
        return pl.ds(4 * lo + SLOT[j] * (hi - lo), hi - lo)

    def gather_copies(full, phase, c):
        own = full.at[block(c, 0)]
        return (
            remote(own, full.at[block(c, 2)], phase, 2, c, peer_x),
            remote(own, full.at[block(c, 1)], phase, 3, c, peer_core),
            remote(full.at[block(c, 2)], full.at[block(c, 3)], phase, 4, c, peer_core),
        )

    def tiles(c):
        lo, hi = spans[c]
        step = next(t for t in (48, 64, 32, 16) if (hi - lo) % t == 0)
        return (hi - lo) // step, step

    def start_gather(full, phase, c):
        first, second, _ = gather_copies(full, phase, c)
        first.start()
        second.start()

    def forward(full, phase, c):
        first, second, third = gather_copies(full, phase, c)
        first.wait_recv()
        third.start()
        second.wait_recv()
        third.wait_recv()

    def partial_products(lhs, rhs, turned, phase, c, half, wide=TILE):
        lo, hi = spans[c]
        r = hi - lo
        rows = pl.ds(4 * lo + half * 2 * r, 2 * r)
        out = pl.ds(2 * lo, 2 * r)

        def body(n, carry):
            cols = pl.ds(pl.multiple_of(n * wide, wide), wide)
            if turned:
                value = lax.dot_general(lhs[rows, :], rhs[cols, :], NT, preferred_element_type=F32)
            else:
                value = jnp.dot(lhs[rows, 0:rhs.shape[0]], rhs[:, cols], preferred_element_type=F32)
            if half == 0:
                cs[out, cols] = value.astype(BF)
            else:
                pbuf[out, cols] = value
            return carry

        lax.fori_loop(0, width // wide, body, 0)

    def pass_on(phase, c):
        lo, hi = spans[c]
        r = hi - lo
        core_copy(phase, c).wait_recv()
        if phase:
            x_copy(phase - 1, c).wait_send()
        xs[lo:hi, :] = (pbuf[2 * lo:2 * lo + r, :] + cr[2 * lo + r:2 * lo + 2 * r, :].astype(F32)).astype(BF)
        x_copy(phase, c).start()

    def own_total(c, i, step):
        lo, hi = spans[c]
        r = hi - lo
        kept = pl.ds(pl.multiple_of(2 * lo + r + i * step, 16), step)
        near = pl.ds(pl.multiple_of(2 * lo + i * step, 16), step)
        far = pl.ds(pl.multiple_of(lo + i * step, 16), step)
        return far, pbuf[kept, :] + cr[near, :].astype(F32) + xr[far, :].astype(F32)

    def row(i):
        return vec[i:i + 1, :]

    wide_biases = biases[...].astype(F32)
    vec[0:2, :] = wide_biases[0:2, :]
    gain, shift = ln_gain[...].astype(F32), ln_bias[...].astype(F32)
    for i in range(4):
        at = 2 * i if i else 8
        vec[at:at + 1, :] = gain[i:i + 1, :]
        vec[at + 1:at + 2, :] = shift[i:i + 1, :]
    b1[...] = wide_biases[2:3, :]
    bias = qv_bias[...].astype(F32)
    acc[...] = jnp.zeros_like(acc)
    b1acc[...] = jnp.zeros_like(b1acc)

    def add(i, values):
        acc[8 * i:8 * i + 8, :] += fold8(values)

    def project(c):
        lo, hi = spans[c]
        for j in (1, 3, 2, 0):
            start = pl.multiple_of(owner[j] * local + lo, 16)
            mlp[block(c, j), 0:part] = heads[pl.ds(start, hi - lo), :]
        partial_products(mlp, wout, False, 0, c, 0)
        core_copy(0, c).start()
        partial_products(mlp, wout, False, 0, c, 1)

    xf = gpre

    def place(j, c):
        lo, hi = spans[c]
        return pl.ds(pl.multiple_of(owner[j] * local + lo, 16), hi - lo)

    def first_copies(c):
        own, across = xf.at[place(0, c)], xf.at[place(2, c)]
        return (
            remote(own, own, 3, 2, c, peer_x),
            remote(own, own, 3, 3, c, peer_core),
            remote(across, across, 3, 4, c, peer_core),
        )

    for c in range(count):
        lo, hi = spans[c]
        trips, step = tiles(c)

        def first_norm(i, carry):
            rows = pl.ds(pl.multiple_of(lo + i * step, 16), step)
            unit, _ = norm_stats(tokens[rows, :].astype(F32))
            dst = pl.ds(pl.multiple_of(me * local + lo + i * step, 16), step)
            xf[dst, :] = (unit * row(8) + row(9)).astype(BF)
            return carry

        lax.fori_loop(0, trips, first_norm, 0)
        for copy in first_copies(c)[:2]:
            copy.start()

    def projections(rows):
        for t in range(3):
            value = jnp.dot(xf[rows, :], w3[t], preferred_element_type=F32)
            if t != 1:
                value = value + bias[t // 2:t // 2 + 1, :]
            act[rows, t * part:(t + 1) * part] = value.astype(BF)

    projections(pl.ds(pl.multiple_of(owner[0] * local, 16), local))
    for c in range(count):
        first_copies(c)[1].wait_recv()
    projections(pl.ds(pl.multiple_of(owner[1] * local, 16), local))
    for c in range(count):
        first_copies(c)[0].wait_recv()
        first_copies(c)[2].start()
        projections(place(2, c))
        if c:
            first_copies(c - 1)[2].wait_recv()
            projections(place(3, c - 1))
    first_copies(count - 1)[2].wait_recv()
    projections(place(3, count - 1))
    keep_x = pltpu.make_async_copy(xf, xfull, local_sem.at[0])
    keep_qkv = pltpu.make_async_copy(act.at[:, 0:3 * part], qkv, local_sem.at[1])
    keep_x.start()
    keep_qkv.start()

    edge0, edge1, edge2 = edges(lengths, offset)
    lo_edge, hi_edge, _, _, cuts = plan(seq)
    pair = 2 * HEAD
    lane = lax.broadcasted_iota(jnp.int32, (1, pair), 1)

    def attend(c):
        lo, hi = spans[c]
        n = hi - lo

        def one_head(h, carry):
            mine = (lane // HEAD) == h % 2
            shift = h // 2 * pair
            qcols, kcols, vcols = (
                pl.ds(pl.multiple_of(t * part + shift, pair), pair) for t in range(3)
            )
            for o in range(4):
                a = o * local + lo
                b = a + n
                start = 0 if a < hi_edge else lo_edge
                stop = -(-b // LANES) * LANES
                qm = jnp.where(mine, act[a:b, qcols].astype(F32) * HEAD**-0.5, 0.0).astype(BF)
                qpos = a + lax.broadcasted_iota(jnp.int32, (n, 1), 0)
                first = seg_start(qpos, edge0, edge1, edge2)
                parts, top = [], None
                for k0, k1 in cuts(start, stop, LANES):
                    s = lax.dot_general(qm, act[k0:k1, kcols], NT, preferred_element_type=F32)
                    if not free_of_mask(k0, k1, a, b, seq):
                        kpos = k0 + lax.broadcasted_iota(jnp.int32, (n, k1 - k0), 1)
                        s = jnp.where((kpos >= first) & (kpos <= qpos), s, -1e9)
                    parts.append(s)
                    top = s if top is None else jnp.maximum(top, s)
                m = jnp.max(top, axis=1, keepdims=True)
                es = [jnp.exp(s - m) for s in parts]
                tot = es[0]
                for e in es[1:]:
                    tot = tot + e
                l = jnp.sum(tot, axis=1, keepdims=True)
                p = jnp.concatenate([e.astype(BF) for e in es], axis=1)
                out = jnp.dot(p, act[start:stop, vcols], preferred_element_type=F32) / l
                hcols = pl.ds(pl.multiple_of(shift, pair), pair)
                heads[a:b, hcols] = jnp.where(mine, out.astype(BF), heads[a:b, hcols])
                log_total = m + jnp.log(l)
                which = lax.broadcasted_iota(jnp.int32, (1, LANES), 1) == h
                at = slice(o * LANES, (o + 1) * LANES)
                u1[lo:hi, at] = jnp.where(which, log_total, u1[lo:hi, at])
            return carry

        lax.fori_loop(0, part // HEAD, one_head, 0)

    for c in range(count):
        attend(c)
        project(c)
        pass_on(0, c)
    keep_lse = [
        pltpu.make_async_copy(u1.at[:, o * LANES:(o + 1) * LANES], lse.at[o], local_sem.at[2 + o]) for o in range(4)
    ]
    for copy in keep_lse:
        copy.start()
    for copy in [keep_qkv, keep_x] + keep_lse:
        copy.wait()
    for c in range(count):
        for copy in first_copies(c):
            copy.wait_send()

    for c in range(count):
        x_copy(0, c).wait_recv()
        lo, hi = spans[c]
        trips, step = tiles(c)

        def norms(i, carry):
            rows, total = own_total(c, i, step)
            unit, inv = norm_stats(total + row(0))
            u1[rows, :] = unit
            r1[rows, 0:HEAD] = jnp.broadcast_to(inv, (step, HEAD))
            hidden = tokens[rows, :].astype(F32) + unit * row(2) + row(3)
            hid[rows, :] = hidden
            unit, inv = norm_stats(hidden)
            u2[rows, :] = unit
            r1[rows, HEAD:LANES] = jnp.broadcast_to(inv, (step, HEAD))
            dst = pl.ds(pl.multiple_of(4 * lo + SLOT[0] * (hi - lo) + i * step, 16), step)
            mlp[dst, :] = (unit * row(4) + row(5)).astype(BF)
            return carry

        lax.fori_loop(0, trips, norms, 0)
        start_gather(mlp, 0, c)

    for c in range(count):
        lo, hi = spans[c]
        r = hi - lo
        forward(mlp, 0, c)
        core_copy(0, c).wait_send()
        for half in range(2):
            rows = pl.ds(4 * lo + half * 2 * r, 2 * r)

            def units(n, carry):
                cols = pl.ds(pl.multiple_of(n * TILE, TILE), TILE)
                pre = jnp.dot(mlp[rows, :], w1[:, cols], preferred_element_type=F32) + b1[:, cols]
                square = pre * pre
                inner = (0.7978845608028654 * pre) * (1.0 + 0.044715 * square)
                tanh = jnp.tanh(inner)
                plus = 0.5 * (1.0 + tanh)
                act[rows, cols] = (pre * plus).astype(BF)
                slope = plus + (0.5 * pre) * (1.0 - tanh * tanh) * (
                    0.7978845608028654 * (1.0 + (3 * 0.044715) * square)
                )
                dgel[rows, cols] = slope.astype(BF)
                return carry

            lax.fori_loop(0, hidden_units // TILE, units, 0)
            partial_products(act, w2, False, 1, c, half)
            if half == 0:
                core_copy(1, c).start()
        pass_on(1, c)

    for c in range(count):
        x_copy(1, c).wait_recv()
        lo, hi = spans[c]
        trips, step = tiles(c)

        def last(i, carry):
            rows, total = own_total(c, i, step)
            unit, inv = norm_stats(total + row(1))
            mixed[rows, :] = (hid[rows, :] + unit * row(6) + row(7)).astype(BF)
            grad = cot[rows, :].astype(F32)
            add(2, grad * unit)
            add(5, grad)
            low = norm_pull(grad, row(6), unit, inv).astype(BF)
            add(7, low.astype(F32))
            dst = pl.ds(pl.multiple_of(4 * lo + SLOT[0] * (hi - lo) + i * step, 16), step)
            brn[dst, :] = low
            return carry

        lax.fori_loop(0, trips, last, 0)
        start_gather(brn, 1, c)

    sum2 = Reduction(hidden_units, hid, 0, 1, (s2y, act.at[512:768]), (r2y, r2z), None, dsend, drecv, 0)
    sump = Reduction(width // 2, w1p, 0, 1, (act.at[0:256],), (rpy,), None, dsend, drecv, 2)
    sumq = Reduction(
        width // 2, qkeep, 0, 1, (act.at[256:512], act.at[768:896]), (rqz, rqw), None, dsend, drecv, 3,
        order=(1, 2, 0),
    )

    def weight_grad(lhs, rhs, first, rows, dst):
        for n in range(rows // TILE):
            cols = pl.ds(pl.multiple_of(first + n * TILE, TILE), TILE)
            value = lax.dot_general(lhs[:, cols], rhs[...], TN, preferred_element_type=F32)
            dst[n * TILE:(n + 1) * TILE, :] = value.astype(dst.dtype)

    half2, half1 = hidden_units // 2, width // 4

    for c in range(count):
        lo, hi = spans[c]
        r = hi - lo
        forward(brn, 1, c)
        if c == count - 1:
            weight_grad(act, brn, (1 - sum2.bits[0]) * half2, half2, s2y)
            sum2.depart(0)
        core_copy(1, c).wait_send()
        for half in range(2):
            rows = pl.ds(4 * lo + half * 2 * r, 2 * r)

            def slopes(n, carry):
                cols = pl.ds(pl.multiple_of(n * TILE, TILE), TILE)
                grad = lax.dot_general(brn[rows, :], w2[cols, :], NT, preferred_element_type=F32)
                low = (grad * dgel[rows, cols].astype(F32)).astype(BF)
                gpre[rows, cols] = low
                b1acc[:, cols] += fold8(low.astype(F32))
                return carry

            lax.fori_loop(0, hidden_units // TILE, slopes, 0)
            partial_products(gpre, w1, True, 2, c, half)
            if half == 0:
                core_copy(2, c).start()
        pass_on(2, c)

    weight_grad(act, brn, sum2.bits[0] * half2, half2, hid)

    for c in range(count):
        x_copy(2, c).wait_recv()
        lo, hi = spans[c]
        trips, step = tiles(c)

        def pulls(i, carry):
            rows, total = own_total(c, i, step)
            unit = u2[rows, :]
            add(1, total * unit)
            add(4, total)
            grad = cot[rows, :].astype(F32) + norm_pull(total, row(4), unit, r1[rows, HEAD:HEAD + 1])
            ghid[rows, :] = grad
            unit = u1[rows, :]
            add(0, grad * unit)
            add(3, grad)
            low = norm_pull(grad, row(2), unit, r1[rows, 0:1]).astype(BF)
            add(6, low.astype(F32))
            dst = pl.ds(pl.multiple_of(4 * lo + SLOT[0] * (hi - lo) + i * step, 16), step)
            dgel[dst, :] = low
            return carry

        lax.fori_loop(0, trips, pulls, 0)
        start_gather(dgel, 2, c)
        if c == 0:
            weight_grad(mlp, gpre, (1 - sump.bits[0]) * half1, half1, act)
            sump.depart(0)
            weight_grad(mlp, gpre, width // 2 + (1 - sumq.bits[0]) * half1, half1, act.at[256:512])
            sumq.depart(0)
        elif c == 2:
            weight_grad(mlp, gpre, width // 2 + sumq.bits[0] * half1, half1, qkeep)

    sum2.step(1)
    weight_grad(mlp, gpre, sump.bits[0] * half1, half1, w1p)
    for c in range(count):
        for copy in gather_copies(brn, 1, c):
            copy.wait_send()
    for c in range(count):
        lo, hi = spans[c]
        forward(dgel, 2, c)
        for j in (1, 3, 2, 0):
            start = pl.multiple_of(owner[j] * local + lo, 16)
            brn[block(c, j), 0:part] = heads[pl.ds(start, hi - lo), :]
            ghead[pl.ds(start, hi - lo), :] = lax.dot_general(
                dgel[block(c, j), :], wout[...], NT, preferred_element_type=F32
            ).astype(BF)
        if c == 0:
            sumq.step(1)
    wog[...] = lax.dot_general(brn[:, 0:part], dgel[...], TN, preferred_element_type=F32)
    for stream, last, work, got, dst in (
        (sump, 0, w1p, rpy, w1p), (sum2, 1, hid, r2z, w2q), (sumq, 1, qkeep, rqw, w1q)
    ):
        stream.arrive(last)

        def join(i, step, stream=stream, last=last, work=work, got=got, dst=dst):
            rows = stream.at(stream.off[last + 1], i, step)
            dst[pl.ds(i, step), :] = work[rows, :] + got[pl.ds(i, step), :].astype(F32)

        by_rows(stream.rows >> (last + 1), join)
        for i in range(last + 1):
            stream.leave(i)

    for i in range(8):
        sums[i:i + 1, :] = jnp.sum(acc[8 * i:8 * i + 8, :], axis=0, keepdims=True)
    b1sum[...] = jnp.sum(b1acc[...], axis=0, keepdims=True)

    for c in range(count):
        core_copy(2, c).wait_send()
        x_copy(2, c).wait_send()
        for phase, full in ((0, mlp), (2, dgel)):
            for copy in gather_copies(full, phase, c):
                copy.wait_send()


def ahead(lengths, offset, tokens, cot, w3, wout, w1, w2, biases, ln_gain, ln_bias, qv_bias):
    local, width = tokens.shape
    seq = 4 * local
    part = w3.shape[2]
    units = w1.shape[1]
    vmem = pl.BlockSpec(memory_space=pltpu.VMEM)
    any_spec = pl.BlockSpec(memory_space=pl.ANY)
    shape = jax.ShapeDtypeStruct
    copies = 20 * 4
    low = lambda *dims: pltpu.VMEM(dims, BF)
    wide = lambda *dims: pltpu.VMEM(dims, F32)
    dma = lambda n: pltpu.SemaphoreType.DMA((n,))
    return pl.pallas_call(
        ahead_kernel,
        in_specs=[pl.BlockSpec(memory_space=pltpu.SMEM)] * 2 + [vmem] * 10,
        out_specs=[any_spec, any_spec, vmem, any_spec] + [vmem] * 9,
        out_shape=[
            shape((seq, width), BF), shape((seq, 3 * part), BF), shape((seq, part), BF), shape((4, local, LANES), F32),
            shape((local, width), BF), shape((local, width), F32), shape((seq, part), BF),
            shape((units // 4, width), F32), shape((width // 4, units), F32), shape((width // 8, units), F32),
            shape((part, width), F32), shape((8, width), F32), shape((1, units), F32),
        ],
        scratch_shapes=[
            wide(16, width), wide(1, units), low(seq, width), low(seq, units), low(seq, units), low(seq, width), low(seq, units),
            wide(local, width), wide(local, width), wide(local, width), wide(local, LANES),
            wide(2 * local, width), low(2 * local, width), low(2 * local, width), low(local, width),
            low(local, width), wide(64, width), wide(8, units),
            wide(width // 4, units), low(units // 2, width), low(units // 2, width), low(units // 4, width),
            low(width // 4, units), low(width // 4, units), low(width // 8, units),
            dma(copies), dma(copies), dma(5), dma(5), dma(6),
        ],
        compiler_params=pltpu.CompilerParams(collective_id=0, has_side_effects=True, vmem_limit_bytes=63 << 20),
        cost_estimate=pl.CostEstimate(
            flops=16 * seq * width * units, bytes_accessed=50 << 20, transcendentals=2 * seq * units
        ),
        name="ahead",
    )(lengths, offset, tokens, cot, w3, wout, w1, w2, biases, ln_gain, ln_bias, qv_bias)


ORDER = {
    "start": (("q", 2), ("2", 2), ("o", 0),),
    1: (("p", 1),),
    5: (("o", 1), ("q", 3),),
    6: (("2", 3),),
    8: (("q", 4), ("a", 0),),
    11: (("2", 4),),
    12: (("b", 0), ("p", 2),),
    "x0": (("o", 2), ("2", 5),),
    "x1": (("p", 3), ("a", 1), ("o", 3),),
    "x3": (("p", 4),),
    "n1": (("b", 1), ("o", 4), ("p", 5),),
    "near": (("a", 2), ("b", 2),),
    "far": (("o", 5), ("a", 3),),
    "end": (("q", 5), ("b", 3),),
}


def back_kernel(
    lengths, offset, qkv, o_ref, do_ref, lse_col, xfull, w3, ghid, tokens, ln_gain, w2q, w1p, w1q, wog_in, sums_in, b1_in,
    tgrad, w2f, w1f, wof, wqt, small_out,
    lse_s, qm_s, dom_s, dqt_s, delta_s, gp, w_in, wq, wqf, wog, pbuf, cs, cr, xs, xr, gs, acc,
    s2w, r2w, spz, spw, rpz, rpw, s1q, r1q, soy, soz, sow, roy, roz, row_, say, saz, ray, raz, small, near, far,
    send, recv, dsend, drecv, nsend, nrecv, fsend, frecv,
):
    local, width = tokens.shape
    seq, part = o_ref.shape
    heads = part // HEAD
    spans = spans_of(local)
    count = len(spans)
    dp, me = lax.axis_index("dp"), lax.axis_index("mp")
    mx, mc = me // 2, me % 2
    owner = {0: me, 1: mx * 2 + 1 - mc, 2: (1 - mx) * 2 + mc, 3: (1 - mx) * 2 + 1 - mc}
    peer_core, peer_x, peer_far = (dp, owner[1]), (dp, owner[2]), (dp, owner[3])
    near_peers = (peer_core, peer_x, peer_far)
    far_peers = tuple(((dp + i) % 8, me) for i in range(1, 8))
    barrier = pltpu.get_barrier_semaphore()
    for peer in near_peers + far_peers:
        pl.semaphore_signal(barrier, inc=1, device_id=peer, device_id_type=MESH)
    pl.semaphore_wait(barrier, 10)

    _, dp_peers = dp_place()
    pair = part // 2
    half = w1f.shape[0] // 2
    streams = {
        "2": Reduction(w2f.shape[0], w2q, 2, 2, (None, None, s2w), (None, None, r2w), w2f, dsend, drecv, 0),
        "p": Reduction(half, w1p, 1, 1, (None, spz, spw), (None, rpz, rpw), w1f.at[0:half], dsend, drecv, 6),
        "q": Reduction(
            half, w1q, 2, 2, (None, None, s1q), (None, None, r1q), w1f.at[half:2 * half], dsend, drecv, 12,
            order=(1, 2, 0),
        ),
        "o": Reduction(part, wog, 0, 0, (soy, soz, sow), (roy, roz, row_), wof, dsend, drecv, 18),
        "a": Direct(3 * pair, wq.at[0], (say.at[0], saz.at[0]), (ray.at[0], raz.at[0]), wqf.at[0], dsend, drecv, 24),
        "b": Direct(3 * pair, wq.at[1], (say.at[1], saz.at[1]), (ray.at[1], raz.at[1]), wqf.at[1], dsend, drecv, 32),
    }

    b0, b1, b2 = edges(lengths, offset)
    gain0 = ln_gain[...].astype(F32)[0:1, :]
    lo_edge, hi_edge, _, _, cut = plan(seq)
    lane = lax.broadcasted_iota(jnp.int32, (1, pair), 1)

    def mask_of(h):
        return (lane // HEAD) == h % 2

    def cols_of(h):
        return pl.ds(pl.multiple_of(h // 2 * pair, pair), pair)

    def grad_cols(h, t):
        return pl.ds(pl.multiple_of(h // 2 * 3 * pair + t * pair, pair), pair)

    def prepare(h):
        mine, cols = mask_of(h), cols_of(h)
        qm_s[...] = jnp.where(mine, qkv[:, cols].astype(F32) * HEAD**-0.5, 0.0).astype(BF)
        dom_s[...] = jnp.where(mine, do_ref[:, cols], jnp.zeros((), BF))
        ones = jnp.ones((8, pair), F32)
        for a, b in cut(0, seq, 256):
            prod = dom_s[a:b, :].astype(F32) * o_ref[a:b, cols].astype(F32)
            delta_s[:, a:b] = lax.dot_general(
                ones, prod, NT, preferred_element_type=F32, precision=lax.Precision.HIGHEST
            )
        dqt_s[...] = jnp.zeros_like(dqt_s)

    def key_blocks(h, blocks):
        mine = mask_of(h)
        key_cols, value_cols = (pl.ds(pl.multiple_of(t * part + h // 2 * pair, pair), pair) for t in (1, 2))
        for a, b, stop in blocks:
            n = b - a
            kk = qkv[a:b, key_cols]
            vv = qkv[a:b, value_cols]
            kpos = a + lax.broadcasted_iota(jnp.int32, (n, 1), 0)
            kh = jnp.where(mine, kk, jnp.zeros((), BF))
            pts, dsts = [], []
            for c, d in cut(a, stop, 128):
                st = lax.dot_general(kk, qm_s[c:d, :], NT, preferred_element_type=F32)
                pt = jnp.exp(st - lse_s[h, 0:1, c:d])
                if not free_of_mask(a, b, c, d, seq):
                    qpos = c + lax.broadcasted_iota(jnp.int32, (1, d - c), 1)
                    first = seg_start(qpos, b0, b1, b2)
                    pt = jnp.where((kpos >= first) & (kpos <= qpos), pt, 0.0)
                dpt = lax.dot_general(vv, dom_s[c:d, :], NT, preferred_element_type=F32)
                pts.append(pt.astype(BF))
                dsts.append((pt * (dpt - delta_s[0:1, c:d])).astype(BF))
            pt = jnp.concatenate(pts, axis=1)
            dst = jnp.concatenate(dsts, axis=1)
            dv = jnp.dot(pt, dom_s[a:stop, :], preferred_element_type=F32)
            dk = jnp.dot(dst, qm_s[a:stop, :], preferred_element_type=F32)
            gv, gk = grad_cols(h, 2), grad_cols(h, 1)
            gp[a:b, gv] = jnp.where(mine, dv.astype(BF), gp[a:b, gv])
            gp[a:b, gk] = jnp.where(mine, dk.astype(BF), gp[a:b, gk])
            dqt_s[:, a:stop] += lax.dot_general(kh, dst, TN, preferred_element_type=F32)

    def finish_queries(h):
        mine, gq = mask_of(h), grad_cols(h, 0)
        for a, b in cut(0, seq, 128):
            dq = (dqt_s[:, a:b] * HEAD**-0.5).T
            gp[a:b, gq] = jnp.where(mine, dq.astype(BF), gp[a:b, gq])

    def input_grad(i):
        wq[i] = lax.dot_general(
            gp[:, i * 3 * pair:(i + 1) * 3 * pair], xfull[...], TN, preferred_element_type=F32
        )

    def turn(i):
        for t in range(3):
            wqt[t, :, i * pair:(i + 1) * pair] = wqf[i, t * pair:(t + 1) * pair, :].T

    def run(point):
        for name, step in ORDER.get(point, ()):
            if step == 0 and name in "ab":
                input_grad("ab".index(name))
            streams[name].step(step)

    wog[...] = wog_in[...]
    run("start")
    gp[...] = jnp.zeros_like(gp)
    for a, b in cut(0, seq, LANES):
        turned = lse_col[a:b, :].T
        for h in range(heads):
            lse_s[h, 0:1, a:b] = turned[h:h + 1, :]
    for i in range(2):
        for t in range(3):
            w_in[:, (3 * i + t) * pair:(3 * i + t + 1) * pair] = w3[t, :, i * pair:(i + 1) * pair]

    groups = (
        [(a, b, hi_edge) for a, b in cut(0, lo_edge, 256)][:2],
        [(a, b, hi_edge) for a, b in cut(0, lo_edge, 256)][2:] + [(a, b, seq) for a, b in cut(lo_edge, hi_edge, 256)],
        [(a, b, seq) for a, b in cut(hi_edge, seq, 256)],
    )

    def one_head(h, carry):
        prepare(h)
        for g, blocks in enumerate(groups):
            key_blocks(h, blocks)
            if g == 2:
                finish_queries(h)
            for k in range(heads):
                if (3 * k + g + 1) in ORDER:

                    @pl.when(h == k)
                    def _(k=k, g=g):
                        run(3 * k + g + 1)

        return carry

    lax.fori_loop(0, heads, one_head, 0)

    def remote(src, dst, kind, c, device):
        i = kind * count + c
        return pltpu.make_async_remote_copy(
            src_ref=src, dst_ref=dst, send_sem=send.at[i], recv_sem=recv.at[i], device_id=device, device_id_type=MESH
        )

    def core_copy(c):
        lo, hi = spans[c]
        rows = pl.ds(2 * lo, 2 * (hi - lo))
        return remote(cs.at[rows], cr.at[rows], 0, c, peer_core)

    def x_copy(c):
        lo, hi = spans[c]
        rows = pl.ds(lo, hi - lo)
        return remote(xs.at[rows], xr.at[rows], 1, c, peer_x)

    def project(c):
        lo, hi = spans[c]
        r = hi - lo
        for half in range(2):
            out = pl.ds(2 * lo, 2 * r)
            for s, j in enumerate(((1, 3), (2, 0))[half]):
                src = pl.ds(pl.multiple_of(owner[j] * local + lo, 16), r)
                gs[s * r:(s + 1) * r, :] = gp[src, :]

            def body(n, carry):
                cols = pl.ds(pl.multiple_of(n * TILE, TILE), TILE)
                value = lax.dot_general(gs[0:2 * r, :], w_in[cols, :], NT, preferred_element_type=F32)
                if half == 0:
                    cs[out, cols] = value.astype(BF)
                else:
                    pbuf[out, cols] = value
                return carry

            lax.fori_loop(0, width // TILE, body, 0)
            if half == 0:
                core_copy(c).start()

    def pass_on(c):
        lo, hi = spans[c]
        r = hi - lo
        core_copy(c).wait_recv()
        xs[lo:hi, :] = (pbuf[2 * lo:2 * lo + r, :] + cr[2 * lo + r:2 * lo + 2 * r, :].astype(F32)).astype(BF)
        x_copy(c).start()

    project(0)
    for c in range(count):
        if c + 1 < count:
            project(c + 1)
        pass_on(c)
        run("x%d" % c)

    acc[...] = jnp.zeros_like(acc)
    for c in range(count):
        x_copy(c).wait_recv()
        lo, hi = spans[c]
        r = hi - lo
        step = next(t for t in (48, 64, 32, 16) if r % t == 0)

        def pulls(i, carry):
            kept = pl.ds(pl.multiple_of(2 * lo + r + i * step, 16), step)
            close = pl.ds(pl.multiple_of(2 * lo + i * step, 16), step)
            rows = pl.ds(pl.multiple_of(lo + i * step, 16), step)
            total = pbuf[kept, :] + cr[close, :].astype(F32) + xr[rows, :].astype(F32)
            unit, inv = norm_stats(tokens[rows, :].astype(F32))
            acc[0:8, :] += fold8(total * unit)
            acc[8:16, :] += fold8(total)
            tgrad[rows, :] = (ghid[rows, :] + norm_pull(total, gain0, unit, inv)).astype(BF)
            return carry

        lax.fori_loop(0, r // step, pulls, 0)
        run("n%d" % c)

    small[...] = jnp.zeros_like(small)
    small[2:10, :] = sums_in[...]
    small[10:11, :] = b1_in[...]
    small[0:1, :] = jnp.sum(acc[0:8, :], axis=0, keepdims=True)
    small[1:2, :] = jnp.sum(acc[8:16, :], axis=0, keepdims=True)
    bias = jnp.sum(gp[...].astype(F32), axis=0, keepdims=True)
    for i in range(2):
        for t in range(2):
            at = (3 * i + 2 * t) * pair
            small[11:12, t * part + i * pair:t * part + (i + 1) * pair] = bias[:, at:at + pair]

    def near_copy(i):
        return pltpu.make_async_remote_copy(
            src_ref=small, dst_ref=near.at[me], send_sem=nsend.at[i], recv_sem=nrecv.at[i], device_id=near_peers[i],
            device_id_type=MESH,
        )

    def far_copy(i):
        return pltpu.make_async_remote_copy(
            src_ref=small_out, dst_ref=far.at[dp], send_sem=fsend.at[i], recv_sem=frecv.at[i], device_id=far_peers[i],
            device_id_type=MESH,
        )

    for i in range(3):
        near_copy(i).start()
    run("near")
    for i in range(3):
        near_copy(i).wait_recv()
    own = lax.broadcasted_iota(jnp.int32, (16, 1), 0) >= 10
    near[me] = small[...]
    small_out[...] = jnp.where(own, small[...], ((near[0] + near[1]) + near[2]) + near[3])
    for i in range(7):
        far_copy(i).start()
    run("far")
    for i in range(7):
        far_copy(i).wait_recv()
    for i in range(7):
        far_copy(i).wait_send()
    far[dp] = small_out[...]
    total = far[0]
    for i in range(1, 8):
        total = total + far[i]
    small_out[...] = total
    run("end")
    for name in ("a", "b"):
        streams[name].arrive(3)
        turn("ab".index(name))

    for name in ("2", "p", "q", "o"):
        streams[name].arrive(5)
    for stream in streams.values():
        stream.drain()
    for i in range(3):
        near_copy(i).wait_send()
    for c in range(count):
        core_copy(c).wait_send()
        x_copy(c).wait_send()


def back(lengths, offset, qkv, o, do, lse, xfull, w3, ghid, tokens, ln_gain, w2q, w1p, w1q, wog, sums, b1_part):
    seq, part = o.shape
    local, width = tokens.shape
    units = w1p.shape[1]
    pair = part // 2
    vmem = pl.BlockSpec(memory_space=pltpu.VMEM)
    shape = jax.ShapeDtypeStruct
    low = lambda *dims: pltpu.VMEM(dims, BF)
    wide = lambda *dims: pltpu.VMEM(dims, F32)
    dma = lambda n: pltpu.SemaphoreType.DMA((n,))
    return pl.pallas_call(
        back_kernel,
        in_specs=[pl.BlockSpec(memory_space=pltpu.SMEM)] * 2 + [vmem] * 15,
        out_specs=[vmem] * 6,
        out_shape=[
            shape((local, width), BF), shape((4 * w2q.shape[0], width), BF), shape((width, units), BF),
            shape((part, width), BF), shape((3, width, part), BF), shape((16, width), F32),
        ],
        scratch_shapes=[
            wide(part // HEAD, 8, seq), low(seq, pair), low(seq, pair), wide(pair, seq), wide(8, seq), low(seq, 3 * part), low(width, 3 * part),
            wide(2, 3 * pair, width), low(2, 3 * pair, width), wide(part, width), wide(2 * local, width), low(2 * local, width),
            low(2 * local, width), low(local, width), low(local, width), low(seq // 6 // 16 * 16, 3 * part), wide(16, width),
            low(units // 8, width), low(units // 8, width), low(width // 8, units), low(width // 16, units),
            low(width // 8, units), low(width // 16, units), low(width // 16, units), low(width // 16, units),
            low(part // 2, width), low(part // 4, width), low(part // 8, width),
            low(part // 2, width), low(part // 4, width), low(part // 8, width),
            low(2, 3 * pair // 2, width), low(2, 3 * pair // 2, width), low(2, 3 * pair // 2, width),
            low(2, 9 * pair // 8, width),
            wide(16, width), wide(4, 16, width), wide(8, 16, width),
            dma(8), dma(8), dma(40), dma(40), dma(3), dma(3), dma(7), dma(7),
        ],
        compiler_params=pltpu.CompilerParams(collective_id=1, has_side_effects=True, vmem_limit_bytes=63 << 20),
        cost_estimate=pl.CostEstimate(flops=20 << 30, bytes_accessed=40 << 20, transcendentals=8 << 20),
        name="back",
    )(lengths, offset, qkv, o, do, lse, xfull, w3, ghid, tokens, ln_gain, w2q, w1p, w1q, wog, sums, b1_part)


def finish_kernel(
    w2f, w1f, wof, wqt, small, tgrad_in, mixed_in, w2o, w1o, woo, wqo, gains, shifts, out_bias, b2, b1, qv, tgrad,
    mixed,
):
    tgrad[...] = tgrad_in[...]
    mixed[...] = mixed_in[...]
    w2o[...] = w2f[...].astype(F32)
    w1o[...] = w1f[...].astype(F32)
    woo[...] = wof[...].astype(F32)
    wqo[...] = wqt[...].astype(F32)
    part = qv.shape[1]
    gains[0:1, :] = small[0:1, :]
    gains[1:4, :] = small[2:5, :]
    shifts[0:1, :] = small[1:2, :]
    shifts[1:4, :] = small[5:8, :]
    out_bias[...] = small[8:9, :]
    b2[...] = small[9:10, :]
    b1[...] = small[10:11, :]
    qv[0:1, :] = small[11:12, 0:part]
    qv[1:2, :] = small[11:12, part:2 * part]


def finish(w2f, w1f, wof, wqt, small, tgrad, mixed):
    parts = 4
    shape = jax.ShapeDtypeStruct
    part = wof.shape[0]
    halves = pl.BlockSpec((tgrad.shape[0] // 2, tgrad.shape[1]), lambda i: (i * 2 // parts, 0))
    rows = lambda a: pl.BlockSpec((a.shape[0] // parts, a.shape[1]), lambda i: (i, 0))
    turned = pl.BlockSpec((3, wqt.shape[1] // parts, part), lambda i: (0, i, 0))
    fixed = lambda n, m: pl.BlockSpec((n, m), lambda i: (0, 0))
    width, units = w2f.shape[1], w1f.shape[1]
    return pl.pallas_call(
        finish_kernel,
        grid=(parts,),
        in_specs=[rows(w2f), rows(w1f), rows(wof), turned, fixed(*small.shape), halves, halves],
        out_specs=[
            rows(w2f), rows(w1f), rows(wof), turned, fixed(4, width), fixed(4, width), fixed(1, width),
            fixed(1, width), fixed(1, units), fixed(2, part), halves, halves,
        ],
        out_shape=[
            shape(w2f.shape, F32), shape(w1f.shape, F32), shape(wof.shape, F32), shape(wqt.shape, F32),
            shape((4, width), F32), shape((4, width), F32), shape((1, width), F32), shape((1, width), F32),
            shape((1, units), F32), shape((2, part), F32), shape(tgrad.shape, BF), shape(mixed.shape, BF),
        ],
        compiler_params=pltpu.CompilerParams(vmem_limit_bytes=56 << 20),
        name="finish",
    )(w2f, w1f, wof, wqt, small, tgrad, mixed)


def shards(
    tokens, caption_len, row_offset, wqkv, qv_bias, wout, out_bias, w1, b1, w2, b2, ln_gain, ln_bias, cotangent,
):
    local_rows, width = tokens.shape
    head_part = wqkv.shape[2]
    here = lax.axis_size("dp") == 8 and lax.axis_size("mp") == 4 and head_part == TILE
    if not (here and width == w1.shape[1] == 1024 and local_rows % 32 == 0):
        return shards_by_ops(
            tokens, caption_len, row_offset, wqkv, qv_bias, wout, out_bias, w1, b1, w2, b2, ln_gain, ln_bias,
            cotangent,
        )
    w3 = wqkv.transpose(1, 0, 2)
    (
        xfull, qkv, heads, lse, mixed, grad_hidden, grad_heads, w2_part, w1_first, w1_last, wout_part, sums, b1_part,
    ) = ahead(
        caption_len, row_offset, tokens, cotangent, w3, wout, w1, w2,
        jnp.concatenate([out_bias, b2, b1]).reshape(3, width), ln_gain, ln_bias, qv_bias,
    )
    tokens_grad, w2_grad, w1_grad, wout_grad, wqkv_grad, small = back(
        caption_len, row_offset, qkv, heads, grad_heads, lse.reshape(-1, LANES), xfull, w3, grad_hidden, tokens,
        ln_gain, w2_part, w1_first, w1_last, wout_part, sums, b1_part,
    )
    (
        w2_grad, w1_grad, wout_grad, wqkv_grad, gain_grad, shift_grad, out_bias_grad, b2_grad, b1_grad, qv_grad,
        tokens_grad, mixed,
    ) = finish(w2_grad, w1_grad, wout_grad, wqkv_grad, small, tokens_grad, mixed)
    return (
        mixed, tokens_grad, wqkv_grad.transpose(1, 0, 2), qv_grad, wout_grad, out_bias_grad[0], w1_grad, b1_grad[0],
        w2_grad, b2_grad[0], gain_grad, shift_grad,
    )


def solution(mesh):
    rows = P(("dp", "mp"), None)
    placed = (
        rows, P("dp", None), P("dp"), P(None, None, "mp"), P(None, "mp"), P("mp", None), P(), P(None, "mp"),
        P("mp"), P("mp", None), P(), P(), P(), rows,
    )
    return jax.shard_map(
        shards,
        mesh=mesh,
        in_specs=placed,
        out_specs=(
            rows, rows, P(None, None, "mp"), P(None, "mp"), P("mp", None), P(), P(None, "mp"), P("mp"),
            P("mp", None), P(), P(), P(),
        ),
        check_vma=False,
    )
```

```python
import functools
import jax, jax.numpy as jnp
from jax import lax
from jax.experimental import pallas as pl
from jax.experimental.pallas import tpu as pltpu
from jax.sharding import PartitionSpec as P
HEAD=64; IMG=1024; CAP_MIN=5; LANES=128
F32=jnp.float32; BF=jnp.bfloat16
MESH=pl.DeviceIdType.MESH
NT=(((1,),(1,)),((),()))
TN=(((0,),(0,)),((),()))

def plan(seq):
    least=IMG+CAP_MIN
    slack=seq-2*least
    lo=least//LANES*LANES
    hi=-(-(seq-least)//LANES)*LANES
    head_pad=-(-slack//LANES)*LANES
    tail_pad=(2*least)//LANES*LANES
    def cut(a,b,step):
        out=[]
        while a<b:
            out.append((a,min(a+step,b))); a=min(a+step,b)
        return out
    return lo,hi,head_pad,tail_pad,cut

def free_of_mask(k0,k1,q0,q1,seq):
    lo,hi,head_pad,tail_pad,_=plan(seq)
    if k1>q0: return False
    if q1<=lo: return k0>=head_pad
    if q0>=hi: return k0>=hi and q1<=tail_pad
    return False

def seg_start(pos,b0,b1,b2):
    return jnp.where(pos>=b2,b2,jnp.where(pos>=b1,b1,jnp.where(pos>=b0,b0,0)))

def fwd_kernel(bounds,q_ref,k_ref,v_ref,o_ref,lse_ref):
    seq,width=q_ref.shape
    h=pl.program_id(0)
    b0,b1,b2=bounds[0],bounds[1],bounds[2]
    lo,hi,_,_,cut=plan(seq)
    lane=lax.broadcasted_iota(jnp.int32,(1,width),1)
    mine=(lane//HEAD)==h
    blocks=[(a,b,0) for a,b in cut(0,lo,256)]+[(a,b,0) for a,b in cut(lo,hi,256)]+[(a,b,lo) for a,b in cut(hi,seq,256)]
    for a,b,start in blocks:
        n=b-a
        qm=jnp.where(mine,q_ref[a:b,:].astype(F32)*HEAD**-0.5,0.0).astype(BF)
        qpos=a+lax.broadcasted_iota(jnp.int32,(n,1),0)
        first=seg_start(qpos,b0,b1,b2)
        parts=[]
        top=None
        for c,d in cut(start,b,128):
            s=lax.dot_general(qm,k_ref[c:d,:],NT,preferred_element_type=F32)
            if not free_of_mask(c,d,a,b,seq):
                kpos=c+lax.broadcasted_iota(jnp.int32,(n,d-c),1)
                s=jnp.where((kpos>=first)&(kpos<=qpos),s,-1e9)
            parts.append(s)
            top=s if top is None else jnp.maximum(top,s)
        m=jnp.max(top,axis=1,keepdims=True)
        es=[jnp.exp(s-m) for s in parts]
        tot=es[0]
        for e in es[1:]: tot=tot+e
        l=jnp.sum(tot,axis=1,keepdims=True)
        p=jnp.concatenate([e.astype(BF) for e in es],axis=1)
        o=jnp.dot(p,v_ref[start:b,:],preferred_element_type=F32)/l
        o_ref[a:b,:]=jnp.where(mine,o.astype(BF),o_ref[a:b,:])
        lse=m+jnp.log(l)
        lse_ref[0,:,a:b]=jnp.broadcast_to(lse,(n,128)).T[0:8,:]

def bwd_kernel(bounds,q_ref,k_ref,v_ref,o_ref,do_ref,lse_ref,dq_ref,dk_ref,dv_ref,qm_s,dom_s,dqt_s,delta_s):
    seq,width=q_ref.shape
    h=pl.program_id(0)
    b0,b1,b2=bounds[0],bounds[1],bounds[2]
    lo,hi,_,_,cut=plan(seq)
    lane=lax.broadcasted_iota(jnp.int32,(1,width),1)
    mine=(lane//HEAD)==h
    qm_s[...]=jnp.where(mine,q_ref[...].astype(F32)*HEAD**-0.5,0.0).astype(BF)
    dom_s[...]=jnp.where(mine,do_ref[...],jnp.zeros((),BF))
    ones=jnp.ones((8,width),F32)
    for a,b in cut(0,seq,256):
        prod=dom_s[a:b,:].astype(F32)*o_ref[a:b,:].astype(F32)
        delta_s[:,a:b]=lax.dot_general(ones,prod,NT,preferred_element_type=F32,precision=lax.Precision.HIGHEST)
    dqt_s[...]=jnp.zeros_like(dqt_s)
    blocks=[(a,b,hi) for a,b in cut(0,lo,256)]+[(a,b,seq) for a,b in cut(lo,hi,256)]+[(a,b,seq) for a,b in cut(hi,seq,256)]
    for a,b,stop in blocks:
        n=b-a
        kk=k_ref[a:b,:]; vv=v_ref[a:b,:]
        kpos=a+lax.broadcasted_iota(jnp.int32,(n,1),0)
        kh=jnp.where(mine,kk,jnp.zeros((),BF))
        pts=[];dsts=[]
        for c,d in cut(a,stop,128):
            st=lax.dot_general(kk,qm_s[c:d,:],NT,preferred_element_type=F32)
            pt=jnp.exp(st-lse_ref[0,0:1,c:d])
            if not free_of_mask(a,b,c,d,seq):
                qpos=c+lax.broadcasted_iota(jnp.int32,(1,d-c),1)
                first=seg_start(qpos,b0,b1,b2)
                pt=jnp.where((kpos>=first)&(kpos<=qpos),pt,0.0)
            dpt=lax.dot_general(vv,dom_s[c:d,:],NT,preferred_element_type=F32)
            dst=pt*(dpt-delta_s[0:1,c:d])
            pts.append(pt.astype(BF)); dsts.append(dst.astype(BF))
        pt=jnp.concatenate(pts,axis=1); dst=jnp.concatenate(dsts,axis=1)
        dv=jnp.dot(pt,dom_s[a:stop,:],preferred_element_type=F32)
        dk=jnp.dot(dst,qm_s[a:stop,:],preferred_element_type=F32)
        dv_ref[a:b,:]=jnp.where(mine,dv.astype(BF),dv_ref[a:b,:])
        dk_ref[a:b,:]=jnp.where(mine,dk.astype(BF),dk_ref[a:b,:])
        dqt_s[:,a:stop]+=lax.dot_general(kh,dst,TN,preferred_element_type=F32)
    for a,b in cut(0,seq,128):
        dq=(dqt_s[:,a:b]*HEAD**-0.5).T
        dq_ref[a:b,:]=jnp.where(mine,dq.astype(BF),dq_ref[a:b,:])

def attn_fwd(bounds,q,k,v):
    seq,width=q.shape; H=width//HEAD
    full=pl.BlockSpec((seq,width),lambda h:(0,0))
    return pl.pallas_call(fwd_kernel,grid=(H,),
        in_specs=[pl.BlockSpec(memory_space=pltpu.SMEM),full,full,full],
        out_specs=[full,pl.BlockSpec((1,8,seq),lambda h:(h,0,0))],
        out_shape=[jax.ShapeDtypeStruct((seq,width),BF),jax.ShapeDtypeStruct((H,8,seq),F32)],
        compiler_params=pltpu.CompilerParams(vmem_limit_bytes=56<<20),name="attn_fwd")(bounds,q,k,v)

def attn_bwd(bounds,q,k,v,o,do,lse):
    seq,width=q.shape; H=width//HEAD
    full=pl.BlockSpec((seq,width),lambda h:(0,0))
    sh=jax.ShapeDtypeStruct((seq,width),BF)
    return pl.pallas_call(bwd_kernel,grid=(H,),
        in_specs=[pl.BlockSpec(memory_space=pltpu.SMEM),full,full,full,full,full,pl.BlockSpec((1,8,seq),lambda h:(h,0,0))],
        out_specs=[full,full,full],out_shape=[sh,sh,sh],
        scratch_shapes=[pltpu.VMEM((seq,width),BF),pltpu.VMEM((seq,width),BF),pltpu.VMEM((width,seq),F32),pltpu.VMEM((8,seq),F32)],
        compiler_params=pltpu.CompilerParams(vmem_limit_bytes=56<<20),name="attn_bwd")(bounds,q,k,v,o,do,lse)

eps_norm = 1e-05


def layer_norm(values, gain, shift):
    center = values - jnp.mean(values, axis=-1, keepdims=True)
    spread = jnp.mean(center * center, axis=-1, keepdims=True)
    return center * lax.rsqrt(spread + eps_norm) * gain + shift


def gelu_tanh(values):
    return jax.nn.gelu(values, approximate=True)


def swap(values, axis, mask):
    size = lax.axis_size(axis)
    return lax.ppermute(values, axis, [(i, i ^ mask) for i in range(size)])


def masks_of(axis):
    size = lax.axis_size(axis)
    out = []
    step = size // 2
    while step:
        out.append(step)
        step //= 2
    return out


def gather_rel(block, axis):
    have = {0: block}
    for mask in masks_of(axis):
        have.update({j ^ mask: swap(v, axis, mask) for j, v in list(have.items())})
    return jnp.stack([have[j] for j in range(lax.axis_size(axis))])


def scatter_rel(parts, axis):
    have = {j: parts[j] for j in range(parts.shape[0])}
    for mask in reversed(masks_of(axis)):
        got = {j: swap(have[j].astype(BF), axis, mask) for j in have if j & mask}
        have = {j: have[j] + got[j ^ mask].astype(F32) for j in have if not j & mask}
    return have[0]


def reduce_all(values, axis):
    me = lax.axis_index(axis)
    masks = list(reversed(masks_of(axis)))
    rows = values.shape[0]
    for mask in masks:
        rows //= 2
        bit = (me // mask) % 2
        keep = lax.dynamic_slice_in_dim(values, bit * rows, rows, 0)
        send = lax.dynamic_slice_in_dim(values, (1 - bit) * rows, rows, 0)
        values = keep + swap(send.astype(BF), axis, mask).astype(F32)
    low = values.astype(BF)
    for mask in reversed(masks):
        bit = (me // mask) % 2
        got = swap(low, axis, mask)
        both = jnp.concatenate([low, got], axis=0)
        flipped = jnp.concatenate([got, low], axis=0)
        low = jnp.where(bit == 0, both, flipped)
    return low.astype(F32)


def sum_small(values, axes):
    for axis in axes:
        for mask in masks_of(axis):
            values = values + swap(values, axis, mask)
    return values


def shards_by_ops(
    tokens, caption_len, row_offset, wqkv, qv_bias, wout, out_bias, w1, b1, w2, b2, ln_gain, ln_bias, cotangent,
):
    local_rows, width = tokens.shape
    size = lax.axis_size("mp")
    seq_len = local_rows * size
    head_part = wqkv.shape[2]
    gains = ln_gain.astype(F32)
    shifts = ln_bias.astype(F32)
    me = lax.axis_index("mp")

    def pick(blocks):
        return jnp.concatenate(
            [lax.dynamic_index_in_dim(blocks, me ^ j, 0, keepdims=True) for j in range(size)], axis=0
        )

    first = row_offset[0]
    second = first + caption_len[0, 0] + IMG
    third = second + caption_len[0, 1] + IMG
    bounds = jnp.stack([first, second, third]).astype(jnp.int32)

    def sort(rel):
        return pick(rel).reshape((seq_len,) + rel.shape[2:])

    def rel_of(rows):
        return pick(rows.reshape((size, local_rows) + rows.shape[1:]))

    rows_in = tokens.astype(F32)
    norm_a, pull_a = jax.vjp(layer_norm, rows_in, gains[0], shifts[0])
    attn_full = sort(gather_rel(norm_a.astype(BF), "mp"))
    w_in = wqkv.reshape(width, 3 * head_part)
    projected = jnp.dot(attn_full, w_in, preferred_element_type=F32)
    bias3 = jnp.concatenate([qv_bias[0], jnp.zeros_like(qv_bias[0]), qv_bias[1]]).astype(F32)
    projected = (projected + bias3).astype(BF)
    queries, keys, values = [projected[:, i * head_part:(i + 1) * head_part] for i in range(3)]
    head_low, lse = attn_fwd(bounds, queries, keys, values)
    head_rel = rel_of(head_low)
    grad_out_all = cotangent.astype(F32)
    state = []
    for lo, hi in [(0, local_rows)]:
        rows = hi - lo
        total = size * rows
        attn_out = scatter_rel(
            jnp.dot(head_rel[:, lo:hi], wout, preferred_element_type=F32), "mp"
        ) + out_bias.astype(F32)
        norm_b, pull_b = jax.vjp(layer_norm, attn_out, gains[1], shifts[1])
        hidden_rows = rows_in[lo:hi] + norm_b
        norm_c, pull_c = jax.vjp(layer_norm, hidden_rows, gains[2], shifts[2])
        mlp_full = gather_rel(norm_c.astype(BF), "mp").reshape(total, width)
        pre_act = jnp.dot(mlp_full, w1, preferred_element_type=F32) + b1.astype(F32)
        activated, gelu_pull = jax.vjp(gelu_tanh, pre_act)
        act_low = activated.astype(BF)
        branch = scatter_rel(
            jnp.dot(act_low, w2, preferred_element_type=F32).reshape(size, rows, width), "mp"
        ) + b2.astype(F32)
        norm_d, pull_d = jax.vjp(layer_norm, branch, gains[3], shifts[3])
        mixed = (hidden_rows + norm_d).astype(BF)
        grad_out = grad_out_all[lo:hi]
        grad_branch, gain_d, shift_d = pull_d(grad_out)
        branch_low = grad_branch.astype(BF)
        b2_part = jnp.sum(branch_low.astype(F32), axis=0)
        branch_full = gather_rel(branch_low, "mp").reshape(total, width)
        grad_act = jnp.einsum("td,fd->tf", branch_full, w2, preferred_element_type=F32)
        grad_pre = gelu_pull(grad_act)[0].astype(BF)
        b1_part = jnp.sum(grad_pre.astype(F32), axis=0)
        grad_norm_c = scatter_rel(
            jnp.einsum("tf,df->td", grad_pre, w1, preferred_element_type=F32).reshape(size, rows, width), "mp"
        )
        grad_hidden_c, gain_c, shift_c = pull_c(grad_norm_c)
        grad_hidden = grad_out + grad_hidden_c
        grad_attn, gain_b, shift_b = pull_b(grad_hidden)
        attn_grad_low = grad_attn.astype(BF)
        out_bias_part = jnp.sum(attn_grad_low.astype(F32), axis=0)
        attn_grad_rel = gather_rel(attn_grad_low, "mp")
        state.append(dict(
            mixed=mixed, act=act_low, branch=branch_full, mlp=mlp_full, pre=grad_pre, hidden=grad_hidden,
            attn=attn_grad_rel, heads=head_rel[:, lo:hi].reshape(total, head_part),
            gh=jnp.einsum("jtd,cd->jtc", attn_grad_rel, wout, preferred_element_type=F32).astype(BF),
            sums=jnp.stack([gain_b, gain_c, gain_d, shift_b, shift_c, shift_d, out_bias_part, b2_part]),
            b1=b1_part,
        ))

    def joined(name, axis=0):
        return jnp.concatenate([s[name] for s in state], axis=axis)

    w2_grad = jnp.einsum("tf,td->fd", joined("act"), joined("branch"), preferred_element_type=F32)
    w2_grad = reduce_all(w2_grad, "dp")
    w1_grad = jnp.einsum("td,tf->df", joined("mlp"), joined("pre"), preferred_element_type=F32)
    w1_grad = reduce_all(w1_grad, "dp")
    attn_grad_full = joined("attn", 1).reshape(seq_len, width)
    wout_grad = jnp.einsum(
        "tc,td->cd", head_rel.reshape(seq_len, head_part), attn_grad_full, preferred_element_type=F32
    )
    wout_grad = reduce_all(wout_grad, "dp")
    grad_heads = sort(joined("gh", 1))
    mixed, grad_hidden = joined("mixed"), joined("hidden")
    mid_sums = sum(s["sums"] for s in state)
    b1_grad = sum(s["b1"] for s in state)
    grads = attn_bwd(bounds, queries, keys, values, head_low, grad_heads, lse)
    grad_proj = jnp.concatenate(grads, axis=1)
    part_sums = jnp.sum(grad_proj.astype(F32), axis=0).reshape(3, head_part)
    qv_part = jnp.stack([part_sums[0], part_sums[2]])
    wqkv_grad = jnp.einsum("td,tc->dc", attn_full, grad_proj, preferred_element_type=F32)
    wqkv_grad = reduce_all(wqkv_grad, "dp").reshape(width, 3, head_part)
    grad_rel = rel_of(grad_proj)
    grad_norm_a = scatter_rel(jnp.einsum("jtc,dc->jtd", grad_rel, w_in, preferred_element_type=F32), "mp")
    grad_rows_a, gain_a, shift_a = pull_a(grad_norm_a)
    tokens_grad = (grad_hidden + grad_rows_a).astype(BF)
    own_sums = sum_small(jnp.concatenate([qv_part.reshape(-1), b1_grad]), ("dp",))
    qv_sum = own_sums[: 2 * head_part].reshape(2, head_part)
    b1_sum = own_sums[2 * head_part:]
    stack = jnp.concatenate([gain_a[None], mid_sums[0:3], shift_a[None], mid_sums[3:8]])
    stack = sum_small(stack, ("mp", "dp"))
    return (
        mixed, tokens_grad, wqkv_grad, qv_sum, wout_grad, stack[8], w1_grad, b1_sum, w2_grad, stack[9],
        stack[0:4], stack[4:8],
    )


SLOT = {1: 0, 3: 1, 2: 2, 0: 3}
TILE = 256


def spans_of(rows):
    units = rows // 16
    sizes = [16 * (units // 4 + (1 if i < units % 4 else 0)) for i in range(4)]
    edges = [sum(sizes[:i]) for i in range(5)]
    return [(edges[i], edges[i + 1]) for i in range(4)]


def fold8(values):
    rows, cols = values.shape
    return jnp.sum(values.reshape(rows // 8, 8, cols), axis=0)


def norm_stats(values):
    center = values - jnp.mean(values, axis=-1, keepdims=True)
    inv = lax.rsqrt(jnp.mean(center * center, axis=-1, keepdims=True) + eps_norm)
    return center * inv, inv


def norm_pull(upstream, gain, unit, inv):
    scaled = upstream * gain
    first = jnp.mean(scaled, axis=-1, keepdims=True)
    second = jnp.mean(scaled * unit, axis=-1, keepdims=True)
    return (scaled - first - unit * second) * inv


def dp_place():
    dp, me = lax.axis_index("dp"), lax.axis_index("mp")
    y, low, high = dp % 2, dp // 2 % 2, dp // 4
    return (y, low, high), (
        (dp + 1 - 2 * y, me), (dp + 2 * (1 - 2 * low), me), (dp + 4 * (1 - 2 * high), me)
    )


def by_rows(count, body):
    step = next(t for t in (64, 48, 32, 16) if count % t == 0)

    def trip(i, carry):
        body(pl.multiple_of(i * step, 16), step)
        return carry

    lax.fori_loop(0, count // step, trip, 0)


class Reduction:
    def __init__(self, rows, work, first, held, sbuf, rbuf, full, send, recv, base, order=(0, 1, 2)):
        self.rows, self.work, self.first, self.held, self.full = rows, work, first, held, full
        self.sbuf, self.rbuf, self.send, self.recv, self.base = sbuf, rbuf, send, recv, base
        bits, peers = dp_place()
        self.bits, self.peers = [bits[i] for i in order], [peers[i] for i in order]
        off = [0]
        for k in range(3):
            off.append(off[-1] + self.bits[k] * (rows >> (k + 1)))
        self.off = off
        self.steps = 6

    def copy(self, i):
        if i < 3:
            src, dst, peer = self.sbuf[i], self.rbuf[i], self.peers[i]
        else:
            k = 5 - i
            part = self.full.at[pl.ds(pl.multiple_of(self.off[k + 1], 16), self.rows >> (k + 1))]
            src, dst, peer = part, part, self.peers[k]
        return pltpu.make_async_remote_copy(
            src_ref=src, dst_ref=dst, send_sem=self.send.at[self.base + i], recv_sem=self.recv.at[self.base + i],
            device_id=peer, device_id_type=MESH,
        )

    def copies(self, i):
        return (self.copy(i),)

    def arrive(self, i):
        for copy in self.copies(i):
            copy.wait_recv()

    def leave(self, i):
        for copy in self.copies(i):
            copy.wait_send()

    def depart(self, i):
        for copy in self.copies(i):
            copy.start()

    def at(self, offset, i, step):
        return pl.ds(pl.multiple_of(offset + i - self.off[self.held], 16), step)

    def halve(self, k):
        n = self.rows >> (k + 1)
        bit = self.bits[k]
        give, keep = self.off[k] + (1 - bit) * n, self.off[k] + bit * n
        fresh = k == self.first

        def out(i, step):
            value = self.work[self.at(give, i, step), :]
            if not fresh:
                value = value + self.rbuf[k - 1][pl.ds(pl.multiple_of((1 - bit) * n + i, 16), step), :].astype(F32)
            self.sbuf[k][pl.ds(i, step), :] = value.astype(BF)

        def stay(i, step):
            rows = self.at(keep, i, step)
            self.work[rows, :] += self.rbuf[k - 1][pl.ds(pl.multiple_of(bit * n + i, 16), step), :].astype(F32)

        by_rows(n, out)
        self.depart(k)
        if not fresh:
            by_rows(n, stay)

    def settle(self, dst, at):
        def body(i, step):
            value = self.work[self.at(self.off[3], i, step), :] + self.rbuf[2][pl.ds(i, step), :].astype(F32)
            dst[pl.ds(pl.multiple_of(at + i, 16), step), :] = value.astype(dst.dtype)

        by_rows(self.rows >> 3, body)

    def step(self, i):
        if i > self.first:
            self.arrive(i - 1)
        if i < 3:
            self.halve(i)
        else:
            if i == 3:
                self.settle(self.full, self.off[3])
            self.depart(i)

    def drain(self):
        for i in range(self.first, self.steps):
            self.leave(i)


class Direct(Reduction):
    def __init__(self, rows, work, sbuf, rbuf, full, send, recv, base):
        super().__init__(rows, work, 0, 0, sbuf, rbuf, full, send, recv, base)
        self.steps = 4
        self.z = lax.axis_index("dp") // 2
        self.y = lax.axis_index("dp") % 2

    def copies(self, i):
        me = lax.axis_index("mp")
        n = self.rows >> 3
        half = pl.ds(pl.multiple_of(self.off[1], 16), 4 * n)
        if i in (0, 3):
            part = self.full.at[half]
            pairs = [(self.sbuf[0], self.rbuf[0], self.peers[0])] if i == 0 else [(part, part, self.peers[0])]
        else:
            pairs = []
            own = self.full.at[pl.ds(pl.multiple_of(self.off[1] + self.z * n, 16), n)]
            for j in range(1, 4):
                there = (self.z + j) % 4
                peer = (2 * there + self.y, me)
                if i == 1:
                    src = self.sbuf[1].at[pl.ds(pl.multiple_of(there * n, 16), n)]
                    pairs.append((src, self.rbuf[1].at[pl.ds((j - 1) * n, n)], peer))
                else:
                    pairs.append((own, own, peer))
        first = self.base + (0, 1, 4, 7)[i]
        return [
            pltpu.make_async_remote_copy(
                src_ref=src, dst_ref=dst, send_sem=self.send.at[first + j], recv_sem=self.recv.at[first + j],
                device_id=peer, device_id_type=MESH,
            )
            for j, (src, dst, peer) in enumerate(pairs)
        ]

    def step(self, i):
        n = self.rows >> 3
        if i:
            self.arrive(i - 1)
        if i == 0:
            self.halve(0)
            return
        if i == 1:

            def spread(k, step):
                rows = self.at(self.off[1], k, step)
                value = self.work[rows, :] + self.rbuf[0][pl.ds(k, step), :].astype(F32)
                self.work[rows, :] = value
                self.sbuf[1][pl.ds(k, step), :] = value.astype(BF)

            by_rows(4 * n, spread)
        elif i == 2:

            def body(k, step):
                at = self.off[1] + self.z * n
                value = self.work[self.at(at, k, step), :]
                for j in range(3):
                    value = value + self.rbuf[1][pl.ds(pl.multiple_of(j * n + k, 16), step), :].astype(F32)
                self.full[pl.ds(pl.multiple_of(at + k, 16), step), :] = value.astype(BF)

            by_rows(n, body)
        self.depart(i)


def edges(lengths, offset):
    first = offset[0]
    second = first + lengths[0, 0] + IMG
    return first, second, second + lengths[0, 1] + IMG


def ahead_kernel(
    lengths, offset, tokens, cot, w3, wout, w1, w2, biases, ln_gain, ln_bias, qv_bias,
    xfull, qkv, heads, lse, mixed, ghid, ghead, w2q, w1p, w1q, wog, sums, b1sum,
    vec, b1, mlp, act, dgel, brn, gpre, u1, u2, hid, r1, pbuf, cs, cr, xs, xr, acc, b1acc,
    qkeep, s2y, r2y, r2z, rpy, rqz, rqw, send, recv, dsend, drecv, local_sem,
):
    local, width = tokens.shape
    seq, part = heads.shape
    hidden_units = w1.shape[1]
    spans = spans_of(local)
    count = len(spans)
    dp, me = lax.axis_index("dp"), lax.axis_index("mp")
    mx, mc = me // 2, me % 2
    peer_core = (dp, mx * 2 + 1 - mc)
    peer_x = (dp, (1 - mx) * 2 + mc)
    owner = {0: me, 1: mx * 2 + 1 - mc, 2: (1 - mx) * 2 + mc, 3: (1 - mx) * 2 + 1 - mc}

    barrier = pltpu.get_barrier_semaphore()
    bits, dp_peers = dp_place()
    for peer in (peer_core, peer_x) + dp_peers:
        pl.semaphore_signal(barrier, inc=1, device_id=peer, device_id_type=MESH)
    pl.semaphore_wait(barrier, 5)

    def remote(src, dst, phase, kind, c, device):
        i = (phase * 5 + kind) * count + c
        return pltpu.make_async_remote_copy(
            src_ref=src, dst_ref=dst, send_sem=send.at[i], recv_sem=recv.at[i], device_id=device, device_id_type=MESH
        )

    def core_copy(phase, c):
        lo, hi = spans[c]
        rows = pl.ds(2 * lo, 2 * (hi - lo))
        return remote(cs.at[rows], cr.at[rows], phase, 0, c, peer_core)

    def x_copy(phase, c):
        lo, hi = spans[c]
        rows = pl.ds(lo, hi - lo)
        return remote(xs.at[rows], xr.at[rows], phase, 1, c, peer_x)

    def block(c, j):
        lo, hi = spans[c]
        return pl.ds(4 * lo + SLOT[j] * (hi - lo), hi - lo)

    def gather_copies(full, phase, c):
        own = full.at[block(c, 0)]
        return (
            remote(own, full.at[block(c, 2)], phase, 2, c, peer_x),
            remote(own, full.at[block(c, 1)], phase, 3, c, peer_core),
            remote(full.at[block(c, 2)], full.at[block(c, 3)], phase, 4, c, peer_core),
        )

    def tiles(c):
        lo, hi = spans[c]
        step = next(t for t in (48, 64, 32, 16) if (hi - lo) % t == 0)
        return (hi - lo) // step, step

    def start_gather(full, phase, c):
        first, second, _ = gather_copies(full, phase, c)
        first.start()
        second.start()

    def forward(full, phase, c):
        first, second, third = gather_copies(full, phase, c)
        first.wait_recv()
        third.start()
        second.wait_recv()
        third.wait_recv()

    def partial_products(lhs, rhs, turned, phase, c, half, wide=TILE):
        lo, hi = spans[c]
        r = hi - lo
        rows = pl.ds(4 * lo + half * 2 * r, 2 * r)
        out = pl.ds(2 * lo, 2 * r)

        def body(n, carry):
            cols = pl.ds(pl.multiple_of(n * wide, wide), wide)
            if turned:
                value = lax.dot_general(lhs[rows, :], rhs[cols, :], NT, preferred_element_type=F32)
            else:
                value = jnp.dot(lhs[rows, 0:rhs.shape[0]], rhs[:, cols], preferred_element_type=F32)
            if half == 0:
                cs[out, cols] = value.astype(BF)
            else:
                pbuf[out, cols] = value
            return carry

        lax.fori_loop(0, width // wide, body, 0)

    def pass_on(phase, c):
        lo, hi = spans[c]
        r = hi - lo
        core_copy(phase, c).wait_recv()
        if phase:
            x_copy(phase - 1, c).wait_send()
        xs[lo:hi, :] = (pbuf[2 * lo:2 * lo + r, :] + cr[2 * lo + r:2 * lo + 2 * r, :].astype(F32)).astype(BF)
        x_copy(phase, c).start()

    def own_total(c, i, step):
        lo, hi = spans[c]
        r = hi - lo
        kept = pl.ds(pl.multiple_of(2 * lo + r + i * step, 16), step)
        near = pl.ds(pl.multiple_of(2 * lo + i * step, 16), step)
        far = pl.ds(pl.multiple_of(lo + i * step, 16), step)
        return far, pbuf[kept, :] + cr[near, :].astype(F32) + xr[far, :].astype(F32)

    def row(i):
        return vec[i:i + 1, :]

    wide_biases = biases[...].astype(F32)
    vec[0:2, :] = wide_biases[0:2, :]
    gain, shift = ln_gain[...].astype(F32), ln_bias[...].astype(F32)
    for i in range(4):
        at = 2 * i if i else 8
        vec[at:at + 1, :] = gain[i:i + 1, :]
        vec[at + 1:at + 2, :] = shift[i:i + 1, :]
    b1[...] = wide_biases[2:3, :]
    bias = qv_bias[...].astype(F32)
    acc[...] = jnp.zeros_like(acc)
    b1acc[...] = jnp.zeros_like(b1acc)

    def add(i, values):
        acc[8 * i:8 * i + 8, :] += fold8(values)

    def project(c):
        lo, hi = spans[c]
        for j in (1, 3, 2, 0):
            start = pl.multiple_of(owner[j] * local + lo, 16)
            mlp[block(c, j), 0:part] = heads[pl.ds(start, hi - lo), :]
        partial_products(mlp, wout, False, 0, c, 0)
        core_copy(0, c).start()
        partial_products(mlp, wout, False, 0, c, 1)

    xf = gpre

    def place(j, c):
        lo, hi = spans[c]
        return pl.ds(pl.multiple_of(owner[j] * local + lo, 16), hi - lo)

    def first_copies(c):
        own, across = xf.at[place(0, c)], xf.at[place(2, c)]
        return (
            remote(own, own, 3, 2, c, peer_x),
            remote(own, own, 3, 3, c, peer_core),
            remote(across, across, 3, 4, c, peer_core),
        )

    for c in range(count):
        lo, hi = spans[c]
        trips, step = tiles(c)

        def first_norm(i, carry):
            rows = pl.ds(pl.multiple_of(lo + i * step, 16), step)
            unit, _ = norm_stats(tokens[rows, :].astype(F32))
            dst = pl.ds(pl.multiple_of(me * local + lo + i * step, 16), step)
            xf[dst, :] = (unit * row(8) + row(9)).astype(BF)
            return carry

        lax.fori_loop(0, trips, first_norm, 0)
        for copy in first_copies(c)[:2]:
            copy.start()

    def projections(rows):
        for t in range(3):
            value = jnp.dot(xf[rows, :], w3[t], preferred_element_type=F32)
            if t != 1:
                value = value + bias[t // 2:t // 2 + 1, :]
            act[rows, t * part:(t + 1) * part] = value.astype(BF)

    projections(pl.ds(pl.multiple_of(owner[0] * local, 16), local))
    for c in range(count):
        first_copies(c)[1].wait_recv()
    projections(pl.ds(pl.multiple_of(owner[1] * local, 16), local))
    for c in range(count):
        first_copies(c)[0].wait_recv()
        first_copies(c)[2].start()
        projections(place(2, c))
        if c:
            first_copies(c - 1)[2].wait_recv()
            projections(place(3, c - 1))
    first_copies(count - 1)[2].wait_recv()
    projections(place(3, count - 1))
    keep_x = pltpu.make_async_copy(xf, xfull, local_sem.at[0])
    keep_qkv = pltpu.make_async_copy(act.at[:, 0:3 * part], qkv, local_sem.at[1])
    keep_x.start()
    keep_qkv.start()

    edge0, edge1, edge2 = edges(lengths, offset)
    lo_edge, hi_edge, _, _, cuts = plan(seq)
    pair = 2 * HEAD
    lane = lax.broadcasted_iota(jnp.int32, (1, pair), 1)

    def attend(c):
        lo, hi = spans[c]
        n = hi - lo

        def one_head(h, carry):
            mine = (lane // HEAD) == h % 2
            shift = h // 2 * pair
            qcols, kcols, vcols = (
                pl.ds(pl.multiple_of(t * part + shift, pair), pair) for t in range(3)
            )
            for o in range(4):
                a = o * local + lo
                b = a + n
                start = 0 if a < hi_edge else lo_edge
                stop = -(-b // LANES) * LANES
                qm = jnp.where(mine, act[a:b, qcols].astype(F32) * HEAD**-0.5, 0.0).astype(BF)
                qpos = a + lax.broadcasted_iota(jnp.int32, (n, 1), 0)
                first = seg_start(qpos, edge0, edge1, edge2)
                parts, top = [], None
                for k0, k1 in cuts(start, stop, LANES):
                    s = lax.dot_general(qm, act[k0:k1, kcols], NT, preferred_element_type=F32)
                    if not free_of_mask(k0, k1, a, b, seq):
                        kpos = k0 + lax.broadcasted_iota(jnp.int32, (n, k1 - k0), 1)
                        s = jnp.where((kpos >= first) & (kpos <= qpos), s, -1e9)
                    parts.append(s)
                    top = s if top is None else jnp.maximum(top, s)
                m = jnp.max(top, axis=1, keepdims=True)
                es = [jnp.exp(s - m) for s in parts]
                tot = es[0]
                for e in es[1:]:
                    tot = tot + e
                l = jnp.sum(tot, axis=1, keepdims=True)
                p = jnp.concatenate([e.astype(BF) for e in es], axis=1)
                out = jnp.dot(p, act[start:stop, vcols], preferred_element_type=F32) / l
                hcols = pl.ds(pl.multiple_of(shift, pair), pair)
                heads[a:b, hcols] = jnp.where(mine, out.astype(BF), heads[a:b, hcols])
                log_total = m + jnp.log(l)
                which = lax.broadcasted_iota(jnp.int32, (1, LANES), 1) == h
                at = slice(o * LANES, (o + 1) * LANES)
                u1[lo:hi, at] = jnp.where(which, log_total, u1[lo:hi, at])
            return carry

        lax.fori_loop(0, part // HEAD, one_head, 0)

    for c in range(count):
        attend(c)
        project(c)
        pass_on(0, c)
    keep_lse = [
        pltpu.make_async_copy(u1.at[:, o * LANES:(o + 1) * LANES], lse.at[o], local_sem.at[2 + o]) for o in range(4)
    ]
    for copy in keep_lse:
        copy.start()
    for copy in [keep_qkv, keep_x] + keep_lse:
        copy.wait()
    for c in range(count):
        for copy in first_copies(c):
            copy.wait_send()

    for c in range(count):
        x_copy(0, c).wait_recv()
        lo, hi = spans[c]
        trips, step = tiles(c)

        def norms(i, carry):
            rows, total = own_total(c, i, step)
            unit, inv = norm_stats(total + row(0))
            u1[rows, :] = unit
            r1[rows, 0:HEAD] = jnp.broadcast_to(inv, (step, HEAD))
            hidden = tokens[rows, :].astype(F32) + unit * row(2) + row(3)
            hid[rows, :] = hidden
            unit, inv = norm_stats(hidden)
            u2[rows, :] = unit
            r1[rows, HEAD:LANES] = jnp.broadcast_to(inv, (step, HEAD))
            dst = pl.ds(pl.multiple_of(4 * lo + SLOT[0] * (hi - lo) + i * step, 16), step)
            mlp[dst, :] = (unit * row(4) + row(5)).astype(BF)
            return carry

        lax.fori_loop(0, trips, norms, 0)
        start_gather(mlp, 0, c)

    for c in range(count):
        lo, hi = spans[c]
        r = hi - lo
        forward(mlp, 0, c)
        core_copy(0, c).wait_send()
        for half in range(2):
            rows = pl.ds(4 * lo + half * 2 * r, 2 * r)

            def units(n, carry):
                cols = pl.ds(pl.multiple_of(n * TILE, TILE), TILE)
                pre = jnp.dot(mlp[rows, :], w1[:, cols], preferred_element_type=F32) + b1[:, cols]
                square = pre * pre
                inner = (0.7978845608028654 * pre) * (1.0 + 0.044715 * square)
                tanh = jnp.tanh(inner)
                plus = 0.5 * (1.0 + tanh)
                act[rows, cols] = (pre * plus).astype(BF)
                slope = plus + (0.5 * pre) * (1.0 - tanh * tanh) * (
                    0.7978845608028654 * (1.0 + (3 * 0.044715) * square)
                )
                dgel[rows, cols] = slope.astype(BF)
                return carry

            lax.fori_loop(0, hidden_units // TILE, units, 0)
            partial_products(act, w2, False, 1, c, half)
            if half == 0:
                core_copy(1, c).start()
        pass_on(1, c)

    for c in range(count):
        x_copy(1, c).wait_recv()
        lo, hi = spans[c]
        trips, step = tiles(c)

        def last(i, carry):
            rows, total = own_total(c, i, step)
            unit, inv = norm_stats(total + row(1))
            mixed[rows, :] = (hid[rows, :] + unit * row(6) + row(7)).astype(BF)
            grad = cot[rows, :].astype(F32)
            add(2, grad * unit)
            add(5, grad)
            low = norm_pull(grad, row(6), unit, inv).astype(BF)
            add(7, low.astype(F32))
            dst = pl.ds(pl.multiple_of(4 * lo + SLOT[0] * (hi - lo) + i * step, 16), step)
            brn[dst, :] = low
            return carry

        lax.fori_loop(0, trips, last, 0)
        start_gather(brn, 1, c)

    sum2 = Reduction(hidden_units, hid, 0, 1, (s2y, act.at[512:768]), (r2y, r2z), None, dsend, drecv, 0)
    sump = Reduction(width // 2, w1p, 0, 1, (act.at[0:256],), (rpy,), None, dsend, drecv, 2)
    sumq = Reduction(
        width // 2, qkeep, 0, 1, (act.at[256:512], act.at[768:896]), (rqz, rqw), None, dsend, drecv, 3,
        order=(1, 2, 0),
    )

    def weight_grad(lhs, rhs, first, rows, dst):
        for n in range(rows // TILE):
            cols = pl.ds(pl.multiple_of(first + n * TILE, TILE), TILE)
            value = lax.dot_general(lhs[:, cols], rhs[...], TN, preferred_element_type=F32)
            dst[n * TILE:(n + 1) * TILE, :] = value.astype(dst.dtype)

    half2, half1 = hidden_units // 2, width // 4

    for c in range(count):
        lo, hi = spans[c]
        r = hi - lo
        forward(brn, 1, c)
        if c == count - 1:
            weight_grad(act, brn, (1 - sum2.bits[0]) * half2, half2, s2y)
            sum2.depart(0)
        core_copy(1, c).wait_send()
        for half in range(2):
            rows = pl.ds(4 * lo + half * 2 * r, 2 * r)

            def slopes(n, carry):
                cols = pl.ds(pl.multiple_of(n * TILE, TILE), TILE)
                grad = lax.dot_general(brn[rows, :], w2[cols, :], NT, preferred_element_type=F32)
                low = (grad * dgel[rows, cols].astype(F32)).astype(BF)
                gpre[rows, cols] = low
                b1acc[:, cols] += fold8(low.astype(F32))
                return carry

            lax.fori_loop(0, hidden_units // TILE, slopes, 0)
            partial_products(gpre, w1, True, 2, c, half)
            if half == 0:
                core_copy(2, c).start()
        pass_on(2, c)

    weight_grad(act, brn, sum2.bits[0] * half2, half2, hid)

    for c in range(count):
        x_copy(2, c).wait_recv()
        lo, hi = spans[c]
        trips, step = tiles(c)

        def pulls(i, carry):
            rows, total = own_total(c, i, step)
            unit = u2[rows, :]
            add(1, total * unit)
            add(4, total)
            grad = cot[rows, :].astype(F32) + norm_pull(total, row(4), unit, r1[rows, HEAD:HEAD + 1])
            ghid[rows, :] = grad
            unit = u1[rows, :]
            add(0, grad * unit)
            add(3, grad)
            low = norm_pull(grad, row(2), unit, r1[rows, 0:1]).astype(BF)
            add(6, low.astype(F32))
            dst = pl.ds(pl.multiple_of(4 * lo + SLOT[0] * (hi - lo) + i * step, 16), step)
            dgel[dst, :] = low
            return carry

        lax.fori_loop(0, trips, pulls, 0)
        start_gather(dgel, 2, c)
        if c == 0:
            weight_grad(mlp, gpre, (1 - sump.bits[0]) * half1, half1, act)
            sump.depart(0)
            weight_grad(mlp, gpre, width // 2 + (1 - sumq.bits[0]) * half1, half1, act.at[256:512])
            sumq.depart(0)
        elif c == 2:
            weight_grad(mlp, gpre, width // 2 + sumq.bits[0] * half1, half1, qkeep)

    sum2.step(1)
    weight_grad(mlp, gpre, sump.bits[0] * half1, half1, w1p)
    for c in range(count):
        for copy in gather_copies(brn, 1, c):
            copy.wait_send()
    for c in range(count):
        lo, hi = spans[c]
        forward(dgel, 2, c)
        for j in (1, 3, 2, 0):
            start = pl.multiple_of(owner[j] * local + lo, 16)
            brn[block(c, j), 0:part] = heads[pl.ds(start, hi - lo), :]
            ghead[pl.ds(start, hi - lo), :] = lax.dot_general(
                dgel[block(c, j), :], wout[...], NT, preferred_element_type=F32
            ).astype(BF)
        if c == 0:
            sumq.step(1)
    wog[...] = lax.dot_general(brn[:, 0:part], dgel[...], TN, preferred_element_type=F32)
    for stream, last, work, got, dst in (
        (sump, 0, w1p, rpy, w1p), (sum2, 1, hid, r2z, w2q), (sumq, 1, qkeep, rqw, w1q)
    ):
        stream.arrive(last)

        def join(i, step, stream=stream, last=last, work=work, got=got, dst=dst):
            rows = stream.at(stream.off[last + 1], i, step)
            dst[pl.ds(i, step), :] = work[rows, :] + got[pl.ds(i, step), :].astype(F32)

        by_rows(stream.rows >> (last + 1), join)
        for i in range(last + 1):
            stream.leave(i)

    for i in range(8):
        sums[i:i + 1, :] = jnp.sum(acc[8 * i:8 * i + 8, :], axis=0, keepdims=True)
    b1sum[...] = jnp.sum(b1acc[...], axis=0, keepdims=True)

    for c in range(count):
        core_copy(2, c).wait_send()
        x_copy(2, c).wait_send()
        for phase, full in ((0, mlp), (2, dgel)):
            for copy in gather_copies(full, phase, c):
                copy.wait_send()


def ahead(lengths, offset, tokens, cot, w3, wout, w1, w2, biases, ln_gain, ln_bias, qv_bias):
    local, width = tokens.shape
    seq = 4 * local
    part = w3.shape[2]
    units = w1.shape[1]
    vmem = pl.BlockSpec(memory_space=pltpu.VMEM)
    any_spec = pl.BlockSpec(memory_space=pl.ANY)
    shape = jax.ShapeDtypeStruct
    copies = 20 * 4
    low = lambda *dims: pltpu.VMEM(dims, BF)
    wide = lambda *dims: pltpu.VMEM(dims, F32)
    dma = lambda n: pltpu.SemaphoreType.DMA((n,))
    return pl.pallas_call(
        ahead_kernel,
        in_specs=[pl.BlockSpec(memory_space=pltpu.SMEM)] * 2 + [vmem] * 10,
        out_specs=[any_spec, any_spec, vmem, any_spec] + [vmem] * 9,
        out_shape=[
            shape((seq, width), BF), shape((seq, 3 * part), BF), shape((seq, part), BF), shape((4, local, LANES), F32),
            shape((local, width), BF), shape((local, width), F32), shape((seq, part), BF),
            shape((units // 4, width), F32), shape((width // 4, units), F32), shape((width // 8, units), F32),
            shape((part, width), F32), shape((8, width), F32), shape((1, units), F32),
        ],
        scratch_shapes=[
            wide(16, width), wide(1, units), low(seq, width), low(seq, units), low(seq, units), low(seq, width), low(seq, units),
            wide(local, width), wide(local, width), wide(local, width), wide(local, LANES),
            wide(2 * local, width), low(2 * local, width), low(2 * local, width), low(local, width),
            low(local, width), wide(64, width), wide(8, units),
            wide(width // 4, units), low(units // 2, width), low(units // 2, width), low(units // 4, width),
            low(width // 4, units), low(width // 4, units), low(width // 8, units),
            dma(copies), dma(copies), dma(5), dma(5), dma(6),
        ],
        compiler_params=pltpu.CompilerParams(collective_id=0, has_side_effects=True, vmem_limit_bytes=63 << 20),
        cost_estimate=pl.CostEstimate(
            flops=16 * seq * width * units, bytes_accessed=50 << 20, transcendentals=2 * seq * units
        ),
        name="ahead",
    )(lengths, offset, tokens, cot, w3, wout, w1, w2, biases, ln_gain, ln_bias, qv_bias)


ORDER = {
    "start": (("o", 0), ("2", 2),),
    3: (("q", 2),),
    4: (("o", 1),),
    5: (("p", 1),),
    6: (("2", 3), ("a", 0),),
    8: (("o", 2),),
    9: (("q", 3), ("p", 2),),
    11: (("2", 4),),
    12: (("q", 4), ("o", 3), ("b", 0),),
    "x0": (("p", 3), ("2", 5),),
    "x1": (("a", 1),),
    "x2": (("p", 4), ("b", 1),),
    "x3": (("a", 2),),
    "n0": (("p", 5),),
    "near": (("b", 2),),
    "far": (("a", 3), ("q", 5),),
    "end": (("b", 3),),
}


def back_kernel(
    lengths, offset, qkv_in, o_in, do_in, lse_in, xfull_in, w3, ghid_in, tokens_in, ln_gain, w2q, w1p, w1q, wog_in, sums_in, b1_in,
    tgrad, w2f, w1f, wof, wqt, small_out,
    qkv, o_ref, do_ref, lse_col, xfull, ghid, tokens, lse_s, qm_s, dom_s, dqt_s, delta_s, gp, w_in, wq, wqf, wog, pbuf, cs, cr, xs, xr, gs, acc,
    s2w, r2w, spz, spw, rpz, rpw, s1q, r1q, soy, soz, roy, roz, say, saz, ray, raz, small, near, far,
    send, recv, dsend, drecv, nsend, nrecv, fsend, frecv, lsem,
):
    local, width = tokens.shape
    seq, part = o_ref.shape
    heads = part // HEAD
    spans = spans_of(local)
    count = len(spans)
    pair = part // 2
    moves = [
        pltpu.make_async_copy(src, dst, lsem.at[i])
        for i, (src, dst) in enumerate(
            (
                (qkv_in, qkv), (do_in, do_ref), (o_in, o_ref), (lse_in, lse_col), (xfull_in, xfull), (ghid_in, ghid),
                (tokens_in, tokens),
            )
        )
    ] + [
        pltpu.make_async_copy(
            w3.at[t, :, i * pair:(i + 1) * pair], w_in.at[:, (3 * i + t) * pair:(3 * i + t + 1) * pair],
            lsem.at[7 + 3 * i + t],
        )
        for i in range(2)
        for t in range(3)
    ]
    for move in moves:
        move.start()
    dp, me = lax.axis_index("dp"), lax.axis_index("mp")
    mx, mc = me // 2, me % 2
    owner = {0: me, 1: mx * 2 + 1 - mc, 2: (1 - mx) * 2 + mc, 3: (1 - mx) * 2 + 1 - mc}
    peer_core, peer_x, peer_far = (dp, owner[1]), (dp, owner[2]), (dp, owner[3])
    near_peers = (peer_core, peer_x, peer_far)
    far_peers = tuple(((dp + i) % 8, me) for i in range(1, 8))
    barrier = pltpu.get_barrier_semaphore()
    for peer in near_peers + far_peers:
        pl.semaphore_signal(barrier, inc=1, device_id=peer, device_id_type=MESH)
    pl.semaphore_wait(barrier, 10)

    half = w1f.shape[0] // 2
    streams = {
        "2": Reduction(w2f.shape[0], w2q, 2, 2, (None, None, s2w), (None, None, r2w), w2f, dsend, drecv, 0),
        "p": Reduction(half, w1p, 1, 1, (None, spz, spw), (None, rpz, rpw), w1f.at[0:half], dsend, drecv, 6),
        "q": Reduction(
            half, w1q, 2, 2, (None, None, s1q), (None, None, r1q), w1f.at[half:2 * half], dsend, drecv, 12,
            order=(1, 2, 0),
        ),
        "o": Direct(part, wog, (soy, soz), (roy, roz), wof, dsend, drecv, 18),
        "a": Direct(3 * pair, wq.at[0], (say.at[0], saz.at[0]), (ray.at[0], raz.at[0]), wqf.at[0], dsend, drecv, 26),
        "b": Direct(3 * pair, wq.at[1], (say.at[1], saz.at[1]), (ray.at[1], raz.at[1]), wqf.at[1], dsend, drecv, 34),
    }

    b0, b1, b2 = edges(lengths, offset)
    gain0 = ln_gain[...].astype(F32)[0:1, :]
    lo_edge, hi_edge, _, _, cut = plan(seq)
    lane = lax.broadcasted_iota(jnp.int32, (1, pair), 1)

    def mask_of(h):
        return (lane // HEAD) == h % 2

    def cols_of(h):
        return pl.ds(pl.multiple_of(h // 2 * pair, pair), pair)

    def grad_cols(h, t):
        return pl.ds(pl.multiple_of(h // 2 * 3 * pair + t * pair, pair), pair)

    def prepare(h):
        mine, cols = mask_of(h), cols_of(h)
        qm_s[...] = jnp.where(mine, qkv[:, cols].astype(F32) * HEAD**-0.5, 0.0).astype(BF)
        dom_s[...] = jnp.where(mine, do_ref[:, cols], jnp.zeros((), BF))
        ones = jnp.ones((8, pair), F32)
        for a, b in cut(0, seq, 256):
            prod = dom_s[a:b, :].astype(F32) * o_ref[a:b, cols].astype(F32)
            delta_s[:, a:b] = lax.dot_general(
                ones, prod, NT, preferred_element_type=F32, precision=lax.Precision.HIGHEST
            )
        dqt_s[...] = jnp.zeros_like(dqt_s)

    def key_blocks(h, blocks):
        mine = mask_of(h)
        key_cols, value_cols = (pl.ds(pl.multiple_of(t * part + h // 2 * pair, pair), pair) for t in (1, 2))
        for a, b, stop in blocks:
            n = b - a
            kk = qkv[a:b, key_cols]
            vv = qkv[a:b, value_cols]
            kpos = a + lax.broadcasted_iota(jnp.int32, (n, 1), 0)
            kh = jnp.where(mine, kk, jnp.zeros((), BF))
            pts, dsts = [], []
            for c, d in cut(a, stop, 128):
                st = lax.dot_general(kk, qm_s[c:d, :], NT, preferred_element_type=F32)
                pt = jnp.exp(st - lse_s[h, 0:1, c:d])
                if not free_of_mask(a, b, c, d, seq):
                    qpos = c + lax.broadcasted_iota(jnp.int32, (1, d - c), 1)
                    first = seg_start(qpos, b0, b1, b2)
                    pt = jnp.where((kpos >= first) & (kpos <= qpos), pt, 0.0)
                dpt = lax.dot_general(vv, dom_s[c:d, :], NT, preferred_element_type=F32)
                pts.append(pt.astype(BF))
                dsts.append((pt * (dpt - delta_s[0:1, c:d])).astype(BF))
            pt = jnp.concatenate(pts, axis=1)
            dst = jnp.concatenate(dsts, axis=1)
            dv = jnp.dot(pt, dom_s[a:stop, :], preferred_element_type=F32)
            dk = jnp.dot(dst, qm_s[a:stop, :], preferred_element_type=F32)
            gv, gk = grad_cols(h, 2), grad_cols(h, 1)
            gp[a:b, gv] = jnp.where(mine, dv.astype(BF), gp[a:b, gv])
            gp[a:b, gk] = jnp.where(mine, dk.astype(BF), gp[a:b, gk])
            dqt_s[:, a:stop] += lax.dot_general(kh, dst, TN, preferred_element_type=F32)

    def finish_queries(h):
        mine, gq = mask_of(h), grad_cols(h, 0)
        for a, b in cut(0, seq, 128):
            dq = (dqt_s[:, a:b] * HEAD**-0.5).T
            gp[a:b, gq] = jnp.where(mine, dq.astype(BF), gp[a:b, gq])

    def input_grad(i):
        wq[i] = lax.dot_general(
            gp[:, i * 3 * pair:(i + 1) * 3 * pair], xfull[...], TN, preferred_element_type=F32
        )

    def turn(i):
        for t in range(3):
            wqt[t, :, i * pair:(i + 1) * pair] = wqf[i, t * pair:(t + 1) * pair, :].T

    def run(point):
        for name, step in ORDER.get(point, ()):
            if step == 0 and name in "ab":
                input_grad("ab".index(name))
            streams[name].step(step)

    wog[...] = wog_in[...]
    run("start")
    gp[...] = jnp.zeros_like(gp)
    for move in moves:
        move.wait()
    for a, b in cut(0, seq, LANES):
        turned = lse_col[a:b, :].T
        for h in range(heads):
            lse_s[h, 0:1, a:b] = turned[h:h + 1, :]

    groups = (
        [(a, b, hi_edge) for a, b in cut(0, lo_edge, 256)][:2],
        [(a, b, hi_edge) for a, b in cut(0, lo_edge, 256)][2:] + [(a, b, seq) for a, b in cut(lo_edge, hi_edge, 256)],
        [(a, b, seq) for a, b in cut(hi_edge, seq, 256)],
    )

    def one_head(h, carry):
        prepare(h)
        for g, blocks in enumerate(groups):
            key_blocks(h, blocks)
            if g == 2:
                finish_queries(h)
            for k in range(heads):
                if (3 * k + g + 1) in ORDER:

                    @pl.when(h == k)
                    def _(k=k, g=g):
                        run(3 * k + g + 1)

        return carry

    lax.fori_loop(0, heads, one_head, 0)

    def remote(src, dst, kind, c, device):
        i = kind * count + c
        return pltpu.make_async_remote_copy(
            src_ref=src, dst_ref=dst, send_sem=send.at[i], recv_sem=recv.at[i], device_id=device, device_id_type=MESH
        )

    def core_copy(c):
        lo, hi = spans[c]
        rows = pl.ds(2 * lo, 2 * (hi - lo))
        return remote(cs.at[rows], cr.at[rows], 0, c, peer_core)

    def x_copy(c):
        lo, hi = spans[c]
        rows = pl.ds(lo, hi - lo)
        return remote(xs.at[rows], xr.at[rows], 1, c, peer_x)

    def project(c):
        lo, hi = spans[c]
        r = hi - lo
        for half in range(2):
            out = pl.ds(2 * lo, 2 * r)
            for s, j in enumerate(((1, 3), (2, 0))[half]):
                src = pl.ds(pl.multiple_of(owner[j] * local + lo, 16), r)
                gs[s * r:(s + 1) * r, :] = gp[src, :]

            def body(n, carry):
                cols = pl.ds(pl.multiple_of(n * TILE, TILE), TILE)
                value = lax.dot_general(gs[0:2 * r, :], w_in[cols, :], NT, preferred_element_type=F32)
                if half == 0:
                    cs[out, cols] = value.astype(BF)
                else:
                    pbuf[out, cols] = value
                return carry

            lax.fori_loop(0, width // TILE, body, 0)
            if half == 0:
                core_copy(c).start()

    def pass_on(c):
        lo, hi = spans[c]
        r = hi - lo
        core_copy(c).wait_recv()
        xs[lo:hi, :] = (pbuf[2 * lo:2 * lo + r, :] + cr[2 * lo + r:2 * lo + 2 * r, :].astype(F32)).astype(BF)
        x_copy(c).start()

    project(0)
    for c in range(count):
        if c + 1 < count:
            project(c + 1)
        pass_on(c)
        run("x%d" % c)

    acc[...] = jnp.zeros_like(acc)
    for c in range(count):
        x_copy(c).wait_recv()
        lo, hi = spans[c]
        r = hi - lo
        step = next(t for t in (48, 64, 32, 16) if r % t == 0)

        def pulls(i, carry):
            kept = pl.ds(pl.multiple_of(2 * lo + r + i * step, 16), step)
            close = pl.ds(pl.multiple_of(2 * lo + i * step, 16), step)
            rows = pl.ds(pl.multiple_of(lo + i * step, 16), step)
            total = pbuf[kept, :] + cr[close, :].astype(F32) + xr[rows, :].astype(F32)
            unit, inv = norm_stats(tokens[rows, :].astype(F32))
            acc[0:8, :] += fold8(total * unit)
            acc[8:16, :] += fold8(total)
            tgrad[rows, :] = (ghid[rows, :] + norm_pull(total, gain0, unit, inv)).astype(BF)
            return carry

        lax.fori_loop(0, r // step, pulls, 0)
        run("n%d" % c)

    small[...] = jnp.zeros_like(small)
    small[2:10, :] = sums_in[...]
    small[10:11, :] = b1_in[...]
    small[0:1, :] = jnp.sum(acc[0:8, :], axis=0, keepdims=True)
    small[1:2, :] = jnp.sum(acc[8:16, :], axis=0, keepdims=True)
    bias = jnp.sum(gp[...].astype(F32), axis=0, keepdims=True)
    for i in range(2):
        for t in range(2):
            at = (3 * i + 2 * t) * pair
            small[11:12, t * part + i * pair:t * part + (i + 1) * pair] = bias[:, at:at + pair]

    def near_copy(i):
        return pltpu.make_async_remote_copy(
            src_ref=small, dst_ref=near.at[me], send_sem=nsend.at[i], recv_sem=nrecv.at[i], device_id=near_peers[i],
            device_id_type=MESH,
        )

    def far_copy(i):
        return pltpu.make_async_remote_copy(
            src_ref=small_out, dst_ref=far.at[dp], send_sem=fsend.at[i], recv_sem=frecv.at[i], device_id=far_peers[i],
            device_id_type=MESH,
        )

    for i in range(3):
        near_copy(i).start()
    run("near")
    for i in range(3):
        near_copy(i).wait_recv()
    own = lax.broadcasted_iota(jnp.int32, (16, 1), 0) >= 10
    near[me] = small[...]
    small_out[...] = jnp.where(own, small[...], ((near[0] + near[1]) + near[2]) + near[3])
    for i in range(7):
        far_copy(i).start()
    run("far")
    for i in range(7):
        far_copy(i).wait_recv()
    for i in range(7):
        far_copy(i).wait_send()
    far[dp] = small_out[...]
    total = far[0]
    for i in range(1, 8):
        total = total + far[i]
    small_out[...] = total
    run("end")
    for name in ("a", "b"):
        streams[name].arrive(3)
        turn("ab".index(name))

    for name in ("2", "p", "q", "o"):
        streams[name].arrive(streams[name].steps - 1)
    for stream in streams.values():
        stream.drain()
    for i in range(3):
        near_copy(i).wait_send()
    for c in range(count):
        core_copy(c).wait_send()
        x_copy(c).wait_send()


def back(lengths, offset, qkv, o, do, lse, xfull, w3, ghid, tokens, ln_gain, w2q, w1p, w1q, wog, sums, b1_part):
    seq, part = o.shape
    local, width = tokens.shape
    units = w1p.shape[1]
    pair = part // 2
    vmem = pl.BlockSpec(memory_space=pltpu.VMEM)
    shape = jax.ShapeDtypeStruct
    low = lambda *dims: pltpu.VMEM(dims, BF)
    wide = lambda *dims: pltpu.VMEM(dims, F32)
    dma = lambda n: pltpu.SemaphoreType.DMA((n,))
    return pl.pallas_call(
        back_kernel,
        in_specs=[pl.BlockSpec(memory_space=pltpu.SMEM)] * 2 + [pl.BlockSpec(memory_space=pl.ANY)] * 8 + [vmem] * 7,
        out_specs=[vmem] * 6,
        out_shape=[
            shape((local, width), BF), shape((4 * w2q.shape[0], width), BF), shape((width, units), BF),
            shape((part, width), BF), shape((3, width, part), BF), shape((16, width), F32),
        ],
        scratch_shapes=[
            low(seq, 3 * part), low(seq, part), low(seq, part), wide(seq, LANES), low(seq, width),
            wide(local, width), low(local, width), wide(part // HEAD, 8, seq), low(seq, pair), low(seq, pair), wide(pair, seq), wide(8, seq), low(seq, 3 * part), low(width, 3 * part),
            wide(2, 3 * pair, width), low(2, 3 * pair, width), wide(part, width), wide(2 * local, width), low(2 * local, width),
            low(2 * local, width), low(local, width), low(local, width), low(seq // 6 // 16 * 16, 3 * part), wide(16, width),
            low(units // 8, width), low(units // 8, width), low(width // 8, units), low(width // 16, units),
            low(width // 8, units), low(width // 16, units), low(width // 16, units), low(width // 16, units),
            low(part // 2, width), low(part // 2, width), low(part // 2, width), low(3 * part // 8, width),
            low(2, 3 * pair // 2, width), low(2, 3 * pair // 2, width), low(2, 3 * pair // 2, width),
            low(2, 9 * pair // 8, width),
            wide(16, width), wide(4, 16, width), wide(8, 16, width),
            dma(8), dma(8), dma(42), dma(42), dma(3), dma(3), dma(7), dma(7), dma(13),
        ],
        compiler_params=pltpu.CompilerParams(collective_id=1, has_side_effects=True, vmem_limit_bytes=63 << 20),
        cost_estimate=pl.CostEstimate(flops=20 << 30, bytes_accessed=40 << 20, transcendentals=8 << 20),
        name="back",
    )(lengths, offset, qkv, o, do, lse, xfull, w3, ghid, tokens, ln_gain, w2q, w1p, w1q, wog, sums, b1_part)


def finish_kernel(
    w2f, w1f, wof, wqt, small, tgrad_in, mixed_in, w2o, w1o, woo, wqo, gains, shifts, out_bias, b2, b1, qv, tgrad,
    mixed,
):
    tgrad[...] = tgrad_in[...]
    mixed[...] = mixed_in[...]
    w2o[...] = w2f[...].astype(F32)
    w1o[...] = w1f[...].astype(F32)
    woo[...] = wof[...].astype(F32)
    wqo[...] = wqt[...].astype(F32)
    part = qv.shape[1]
    gains[0:1, :] = small[0:1, :]
    gains[1:4, :] = small[2:5, :]
    shifts[0:1, :] = small[1:2, :]
    shifts[1:4, :] = small[5:8, :]
    out_bias[...] = small[8:9, :]
    b2[...] = small[9:10, :]
    b1[...] = small[10:11, :]
    qv[0:1, :] = small[11:12, 0:part]
    qv[1:2, :] = small[11:12, part:2 * part]


def finish(w2f, w1f, wof, wqt, small, tgrad, mixed):
    parts = 4
    shape = jax.ShapeDtypeStruct
    part = wof.shape[0]
    halves = pl.BlockSpec((tgrad.shape[0] // 2, tgrad.shape[1]), lambda i: (i * 2 // parts, 0))
    rows = lambda a: pl.BlockSpec((a.shape[0] // parts, a.shape[1]), lambda i: (i, 0))
    turned = pl.BlockSpec((3, wqt.shape[1] // parts, part), lambda i: (0, i, 0))
    fixed = lambda n, m: pl.BlockSpec((n, m), lambda i: (0, 0))
    width, units = w2f.shape[1], w1f.shape[1]
    return pl.pallas_call(
        finish_kernel,
        grid=(parts,),
        in_specs=[rows(w2f), rows(w1f), rows(wof), turned, fixed(*small.shape), halves, halves],
        out_specs=[
            rows(w2f), rows(w1f), rows(wof), turned, fixed(4, width), fixed(4, width), fixed(1, width),
            fixed(1, width), fixed(1, units), fixed(2, part), halves, halves,
        ],
        out_shape=[
            shape(w2f.shape, F32), shape(w1f.shape, F32), shape(wof.shape, F32), shape(wqt.shape, F32),
            shape((4, width), F32), shape((4, width), F32), shape((1, width), F32), shape((1, width), F32),
            shape((1, units), F32), shape((2, part), F32), shape(tgrad.shape, BF), shape(mixed.shape, BF),
        ],
        compiler_params=pltpu.CompilerParams(vmem_limit_bytes=56 << 20),
        name="finish",
    )(w2f, w1f, wof, wqt, small, tgrad, mixed)


def shards(
    tokens, caption_len, row_offset, wqkv, qv_bias, wout, out_bias, w1, b1, w2, b2, ln_gain, ln_bias, cotangent,
):
    local_rows, width = tokens.shape
    head_part = wqkv.shape[2]
    here = lax.axis_size("dp") == 8 and lax.axis_size("mp") == 4 and head_part == TILE
    if not (here and width == w1.shape[1] == 1024 and local_rows % 32 == 0):
        return shards_by_ops(
            tokens, caption_len, row_offset, wqkv, qv_bias, wout, out_bias, w1, b1, w2, b2, ln_gain, ln_bias,
            cotangent,
        )
    w3 = wqkv.transpose(1, 0, 2)
    (
        xfull, qkv, heads, lse, mixed, grad_hidden, grad_heads, w2_part, w1_first, w1_last, wout_part, sums, b1_part,
    ) = ahead(
        caption_len, row_offset, tokens, cotangent, w3, wout, w1, w2,
        jnp.concatenate([out_bias, b2, b1]).reshape(3, width), ln_gain, ln_bias, qv_bias,
    )
    tokens_grad, w2_grad, w1_grad, wout_grad, wqkv_grad, small = back(
        caption_len, row_offset, qkv, heads, grad_heads, lse.reshape(-1, LANES), xfull, w3, grad_hidden, tokens,
        ln_gain, w2_part, w1_first, w1_last, wout_part, sums, b1_part,
    )
    (
        w2_grad, w1_grad, wout_grad, wqkv_grad, gain_grad, shift_grad, out_bias_grad, b2_grad, b1_grad, qv_grad,
        tokens_grad, mixed,
    ) = finish(w2_grad, w1_grad, wout_grad, wqkv_grad, small, tokens_grad, mixed)
    return (
        mixed, tokens_grad, wqkv_grad.transpose(1, 0, 2), qv_grad, wout_grad, out_bias_grad[0], w1_grad, b1_grad[0],
        w2_grad, b2_grad[0], gain_grad, shift_grad,
    )


def solution(mesh):
    rows = P(("dp", "mp"), None)
    placed = (
        rows, P("dp", None), P("dp"), P(None, None, "mp"), P(None, "mp"), P("mp", None), P(), P(None, "mp"),
        P("mp"), P("mp", None), P(), P(), P(), rows,
    )
    return jax.shard_map(
        shards,
        mesh=mesh,
        in_specs=placed,
        out_specs=(
            rows, rows, P(None, None, "mp"), P(None, "mp"), P("mp", None), P(), P(None, "mp"), P("mp"),
            P("mp", None), P(), P(), P(),
        ),
        check_vma=False,
    )
```

```python
import functools
import jax, jax.numpy as jnp
from jax import lax
from jax.experimental import pallas as pl
from jax.experimental.pallas import tpu as pltpu
from jax.sharding import PartitionSpec as P
HEAD=64; IMG=1024; CAP_MIN=5; LANES=128
F32=jnp.float32; BF=jnp.bfloat16
MESH=pl.DeviceIdType.MESH
NT=(((1,),(1,)),((),()))
TN=(((0,),(0,)),((),()))

def plan(seq):
    least=IMG+CAP_MIN
    slack=seq-2*least
    lo=least//LANES*LANES
    hi=-(-(seq-least)//LANES)*LANES
    head_pad=-(-slack//LANES)*LANES
    tail_pad=(2*least)//LANES*LANES
    def cut(a,b,step):
        out=[]
        while a<b:
            out.append((a,min(a+step,b))); a=min(a+step,b)
        return out
    return lo,hi,head_pad,tail_pad,cut

def free_of_mask(k0,k1,q0,q1,seq):
    lo,hi,head_pad,tail_pad,_=plan(seq)
    if k1>q0: return False
    if q1<=lo: return k0>=head_pad
    if q0>=hi: return k0>=hi and q1<=tail_pad
    return False

def seg_start(pos,b0,b1,b2):
    return jnp.where(pos>=b2,b2,jnp.where(pos>=b1,b1,jnp.where(pos>=b0,b0,0)))

def fwd_kernel(bounds,q_ref,k_ref,v_ref,o_ref,lse_ref):
    seq,width=q_ref.shape
    h=pl.program_id(0)
    b0,b1,b2=bounds[0],bounds[1],bounds[2]
    lo,hi,_,_,cut=plan(seq)
    lane=lax.broadcasted_iota(jnp.int32,(1,width),1)
    mine=(lane//HEAD)==h
    blocks=[(a,b,0) for a,b in cut(0,lo,256)]+[(a,b,0) for a,b in cut(lo,hi,256)]+[(a,b,lo) for a,b in cut(hi,seq,256)]
    for a,b,start in blocks:
        n=b-a
        qm=jnp.where(mine,q_ref[a:b,:].astype(F32)*HEAD**-0.5,0.0).astype(BF)
        qpos=a+lax.broadcasted_iota(jnp.int32,(n,1),0)
        first=seg_start(qpos,b0,b1,b2)
        parts=[]
        top=None
        for c,d in cut(start,b,128):
            s=lax.dot_general(qm,k_ref[c:d,:],NT,preferred_element_type=F32)
            if not free_of_mask(c,d,a,b,seq):
                kpos=c+lax.broadcasted_iota(jnp.int32,(n,d-c),1)
                s=jnp.where((kpos>=first)&(kpos<=qpos),s,-1e9)
            parts.append(s)
            top=s if top is None else jnp.maximum(top,s)
        m=jnp.max(top,axis=1,keepdims=True)
        es=[jnp.exp(s-m) for s in parts]
        tot=es[0]
        for e in es[1:]: tot=tot+e
        l=jnp.sum(tot,axis=1,keepdims=True)
        p=jnp.concatenate([e.astype(BF) for e in es],axis=1)
        o=jnp.dot(p,v_ref[start:b,:],preferred_element_type=F32)/l
        o_ref[a:b,:]=jnp.where(mine,o.astype(BF),o_ref[a:b,:])
        lse=m+jnp.log(l)
        lse_ref[0,:,a:b]=jnp.broadcast_to(lse,(n,128)).T[0:8,:]

def bwd_kernel(bounds,q_ref,k_ref,v_ref,o_ref,do_ref,lse_ref,dq_ref,dk_ref,dv_ref,qm_s,dom_s,dqt_s,delta_s):
    seq,width=q_ref.shape
    h=pl.program_id(0)
    b0,b1,b2=bounds[0],bounds[1],bounds[2]
    lo,hi,_,_,cut=plan(seq)
    lane=lax.broadcasted_iota(jnp.int32,(1,width),1)
    mine=(lane//HEAD)==h
    qm_s[...]=jnp.where(mine,q_ref[...].astype(F32)*HEAD**-0.5,0.0).astype(BF)
    dom_s[...]=jnp.where(mine,do_ref[...],jnp.zeros((),BF))
    ones=jnp.ones((8,width),F32)
    for a,b in cut(0,seq,256):
        prod=dom_s[a:b,:].astype(F32)*o_ref[a:b,:].astype(F32)
        delta_s[:,a:b]=lax.dot_general(ones,prod,NT,preferred_element_type=F32,precision=lax.Precision.HIGHEST)
    dqt_s[...]=jnp.zeros_like(dqt_s)
    blocks=[(a,b,hi) for a,b in cut(0,lo,256)]+[(a,b,seq) for a,b in cut(lo,hi,256)]+[(a,b,seq) for a,b in cut(hi,seq,256)]
    for a,b,stop in blocks:
        n=b-a
        kk=k_ref[a:b,:]; vv=v_ref[a:b,:]
        kpos=a+lax.broadcasted_iota(jnp.int32,(n,1),0)
        kh=jnp.where(mine,kk,jnp.zeros((),BF))
        pts=[];dsts=[]
        for c,d in cut(a,stop,128):
            st=lax.dot_general(kk,qm_s[c:d,:],NT,preferred_element_type=F32)
            pt=jnp.exp(st-lse_ref[0,0:1,c:d])
            if not free_of_mask(a,b,c,d,seq):
                qpos=c+lax.broadcasted_iota(jnp.int32,(1,d-c),1)
                first=seg_start(qpos,b0,b1,b2)
                pt=jnp.where((kpos>=first)&(kpos<=qpos),pt,0.0)
            dpt=lax.dot_general(vv,dom_s[c:d,:],NT,preferred_element_type=F32)
            dst=pt*(dpt-delta_s[0:1,c:d])
            pts.append(pt.astype(BF)); dsts.append(dst.astype(BF))
        pt=jnp.concatenate(pts,axis=1); dst=jnp.concatenate(dsts,axis=1)
        dv=jnp.dot(pt,dom_s[a:stop,:],preferred_element_type=F32)
        dk=jnp.dot(dst,qm_s[a:stop,:],preferred_element_type=F32)
        dv_ref[a:b,:]=jnp.where(mine,dv.astype(BF),dv_ref[a:b,:])
        dk_ref[a:b,:]=jnp.where(mine,dk.astype(BF),dk_ref[a:b,:])
        dqt_s[:,a:stop]+=lax.dot_general(kh,dst,TN,preferred_element_type=F32)
    for a,b in cut(0,seq,128):
        dq=(dqt_s[:,a:b]*HEAD**-0.5).T
        dq_ref[a:b,:]=jnp.where(mine,dq.astype(BF),dq_ref[a:b,:])

def attn_fwd(bounds,q,k,v):
    seq,width=q.shape; H=width//HEAD
    full=pl.BlockSpec((seq,width),lambda h:(0,0))
    return pl.pallas_call(fwd_kernel,grid=(H,),
        in_specs=[pl.BlockSpec(memory_space=pltpu.SMEM),full,full,full],
        out_specs=[full,pl.BlockSpec((1,8,seq),lambda h:(h,0,0))],
        out_shape=[jax.ShapeDtypeStruct((seq,width),BF),jax.ShapeDtypeStruct((H,8,seq),F32)],
        compiler_params=pltpu.CompilerParams(vmem_limit_bytes=56<<20),name="attn_fwd")(bounds,q,k,v)

def attn_bwd(bounds,q,k,v,o,do,lse):
    seq,width=q.shape; H=width//HEAD
    full=pl.BlockSpec((seq,width),lambda h:(0,0))
    sh=jax.ShapeDtypeStruct((seq,width),BF)
    return pl.pallas_call(bwd_kernel,grid=(H,),
        in_specs=[pl.BlockSpec(memory_space=pltpu.SMEM),full,full,full,full,full,pl.BlockSpec((1,8,seq),lambda h:(h,0,0))],
        out_specs=[full,full,full],out_shape=[sh,sh,sh],
        scratch_shapes=[pltpu.VMEM((seq,width),BF),pltpu.VMEM((seq,width),BF),pltpu.VMEM((width,seq),F32),pltpu.VMEM((8,seq),F32)],
        compiler_params=pltpu.CompilerParams(vmem_limit_bytes=56<<20),name="attn_bwd")(bounds,q,k,v,o,do,lse)

eps_norm = 1e-05


def layer_norm(values, gain, shift):
    center = values - jnp.mean(values, axis=-1, keepdims=True)
    spread = jnp.mean(center * center, axis=-1, keepdims=True)
    return center * lax.rsqrt(spread + eps_norm) * gain + shift


def gelu_tanh(values):
    return jax.nn.gelu(values, approximate=True)


def swap(values, axis, mask):
    size = lax.axis_size(axis)
    return lax.ppermute(values, axis, [(i, i ^ mask) for i in range(size)])


def masks_of(axis):
    size = lax.axis_size(axis)
    out = []
    step = size // 2
    while step:
        out.append(step)
        step //= 2
    return out


def gather_rel(block, axis):
    have = {0: block}
    for mask in masks_of(axis):
        have.update({j ^ mask: swap(v, axis, mask) for j, v in list(have.items())})
    return jnp.stack([have[j] for j in range(lax.axis_size(axis))])


def scatter_rel(parts, axis):
    have = {j: parts[j] for j in range(parts.shape[0])}
    for mask in reversed(masks_of(axis)):
        got = {j: swap(have[j].astype(BF), axis, mask) for j in have if j & mask}
        have = {j: have[j] + got[j ^ mask].astype(F32) for j in have if not j & mask}
    return have[0]


def reduce_all(values, axis):
    me = lax.axis_index(axis)
    masks = list(reversed(masks_of(axis)))
    rows = values.shape[0]
    for mask in masks:
        rows //= 2
        bit = (me // mask) % 2
        keep = lax.dynamic_slice_in_dim(values, bit * rows, rows, 0)
        send = lax.dynamic_slice_in_dim(values, (1 - bit) * rows, rows, 0)
        values = keep + swap(send.astype(BF), axis, mask).astype(F32)
    low = values.astype(BF)
    for mask in reversed(masks):
        bit = (me // mask) % 2
        got = swap(low, axis, mask)
        both = jnp.concatenate([low, got], axis=0)
        flipped = jnp.concatenate([got, low], axis=0)
        low = jnp.where(bit == 0, both, flipped)
    return low.astype(F32)


def sum_small(values, axes):
    for axis in axes:
        for mask in masks_of(axis):
            values = values + swap(values, axis, mask)
    return values


def shards_by_ops(
    tokens, caption_len, row_offset, wqkv, qv_bias, wout, out_bias, w1, b1, w2, b2, ln_gain, ln_bias, cotangent,
):
    local_rows, width = tokens.shape
    size = lax.axis_size("mp")
    seq_len = local_rows * size
    head_part = wqkv.shape[2]
    gains = ln_gain.astype(F32)
    shifts = ln_bias.astype(F32)
    me = lax.axis_index("mp")

    def pick(blocks):
        return jnp.concatenate(
            [lax.dynamic_index_in_dim(blocks, me ^ j, 0, keepdims=True) for j in range(size)], axis=0
        )

    first = row_offset[0]
    second = first + caption_len[0, 0] + IMG
    third = second + caption_len[0, 1] + IMG
    bounds = jnp.stack([first, second, third]).astype(jnp.int32)

    def sort(rel):
        return pick(rel).reshape((seq_len,) + rel.shape[2:])

    def rel_of(rows):
        return pick(rows.reshape((size, local_rows) + rows.shape[1:]))

    rows_in = tokens.astype(F32)
    norm_a, pull_a = jax.vjp(layer_norm, rows_in, gains[0], shifts[0])
    attn_full = sort(gather_rel(norm_a.astype(BF), "mp"))
    w_in = wqkv.reshape(width, 3 * head_part)
    projected = jnp.dot(attn_full, w_in, preferred_element_type=F32)
    bias3 = jnp.concatenate([qv_bias[0], jnp.zeros_like(qv_bias[0]), qv_bias[1]]).astype(F32)
    projected = (projected + bias3).astype(BF)
    queries, keys, values = [projected[:, i * head_part:(i + 1) * head_part] for i in range(3)]
    head_low, lse = attn_fwd(bounds, queries, keys, values)
    head_rel = rel_of(head_low)
    grad_out_all = cotangent.astype(F32)
    state = []
    for lo, hi in [(0, local_rows)]:
        rows = hi - lo
        total = size * rows
        attn_out = scatter_rel(
            jnp.dot(head_rel[:, lo:hi], wout, preferred_element_type=F32), "mp"
        ) + out_bias.astype(F32)
        norm_b, pull_b = jax.vjp(layer_norm, attn_out, gains[1], shifts[1])
        hidden_rows = rows_in[lo:hi] + norm_b
        norm_c, pull_c = jax.vjp(layer_norm, hidden_rows, gains[2], shifts[2])
        mlp_full = gather_rel(norm_c.astype(BF), "mp").reshape(total, width)
        pre_act = jnp.dot(mlp_full, w1, preferred_element_type=F32) + b1.astype(F32)
        activated, gelu_pull = jax.vjp(gelu_tanh, pre_act)
        act_low = activated.astype(BF)
        branch = scatter_rel(
            jnp.dot(act_low, w2, preferred_element_type=F32).reshape(size, rows, width), "mp"
        ) + b2.astype(F32)
        norm_d, pull_d = jax.vjp(layer_norm, branch, gains[3], shifts[3])
        mixed = (hidden_rows + norm_d).astype(BF)
        grad_out = grad_out_all[lo:hi]
        grad_branch, gain_d, shift_d = pull_d(grad_out)
        branch_low = grad_branch.astype(BF)
        b2_part = jnp.sum(branch_low.astype(F32), axis=0)
        branch_full = gather_rel(branch_low, "mp").reshape(total, width)
        grad_act = jnp.einsum("td,fd->tf", branch_full, w2, preferred_element_type=F32)
        grad_pre = gelu_pull(grad_act)[0].astype(BF)
        b1_part = jnp.sum(grad_pre.astype(F32), axis=0)
        grad_norm_c = scatter_rel(
            jnp.einsum("tf,df->td", grad_pre, w1, preferred_element_type=F32).reshape(size, rows, width), "mp"
        )
        grad_hidden_c, gain_c, shift_c = pull_c(grad_norm_c)
        grad_hidden = grad_out + grad_hidden_c
        grad_attn, gain_b, shift_b = pull_b(grad_hidden)
        attn_grad_low = grad_attn.astype(BF)
        out_bias_part = jnp.sum(attn_grad_low.astype(F32), axis=0)
        attn_grad_rel = gather_rel(attn_grad_low, "mp")
        state.append(dict(
            mixed=mixed, act=act_low, branch=branch_full, mlp=mlp_full, pre=grad_pre, hidden=grad_hidden,
            attn=attn_grad_rel, heads=head_rel[:, lo:hi].reshape(total, head_part),
            gh=jnp.einsum("jtd,cd->jtc", attn_grad_rel, wout, preferred_element_type=F32).astype(BF),
            sums=jnp.stack([gain_b, gain_c, gain_d, shift_b, shift_c, shift_d, out_bias_part, b2_part]),
            b1=b1_part,
        ))

    def joined(name, axis=0):
        return jnp.concatenate([s[name] for s in state], axis=axis)

    w2_grad = jnp.einsum("tf,td->fd", joined("act"), joined("branch"), preferred_element_type=F32)
    w2_grad = reduce_all(w2_grad, "dp")
    w1_grad = jnp.einsum("td,tf->df", joined("mlp"), joined("pre"), preferred_element_type=F32)
    w1_grad = reduce_all(w1_grad, "dp")
    attn_grad_full = joined("attn", 1).reshape(seq_len, width)
    wout_grad = jnp.einsum(
        "tc,td->cd", head_rel.reshape(seq_len, head_part), attn_grad_full, preferred_element_type=F32
    )
    wout_grad = reduce_all(wout_grad, "dp")
    grad_heads = sort(joined("gh", 1))
    mixed, grad_hidden = joined("mixed"), joined("hidden")
    mid_sums = sum(s["sums"] for s in state)
    b1_grad = sum(s["b1"] for s in state)
    grads = attn_bwd(bounds, queries, keys, values, head_low, grad_heads, lse)
    grad_proj = jnp.concatenate(grads, axis=1)
    part_sums = jnp.sum(grad_proj.astype(F32), axis=0).reshape(3, head_part)
    qv_part = jnp.stack([part_sums[0], part_sums[2]])
    wqkv_grad = jnp.einsum("td,tc->dc", attn_full, grad_proj, preferred_element_type=F32)
    wqkv_grad = reduce_all(wqkv_grad, "dp").reshape(width, 3, head_part)
    grad_rel = rel_of(grad_proj)
    grad_norm_a = scatter_rel(jnp.einsum("jtc,dc->jtd", grad_rel, w_in, preferred_element_type=F32), "mp")
    grad_rows_a, gain_a, shift_a = pull_a(grad_norm_a)
    tokens_grad = (grad_hidden + grad_rows_a).astype(BF)
    own_sums = sum_small(jnp.concatenate([qv_part.reshape(-1), b1_grad]), ("dp",))
    qv_sum = own_sums[: 2 * head_part].reshape(2, head_part)
    b1_sum = own_sums[2 * head_part:]
    stack = jnp.concatenate([gain_a[None], mid_sums[0:3], shift_a[None], mid_sums[3:8]])
    stack = sum_small(stack, ("mp", "dp"))
    return (
        mixed, tokens_grad, wqkv_grad, qv_sum, wout_grad, stack[8], w1_grad, b1_sum, w2_grad, stack[9],
        stack[0:4], stack[4:8],
    )


SLOT = {1: 0, 3: 1, 2: 2, 0: 3}
TILE = 256
AHEAD = 2


def spans_of(rows):
    units = rows // 16
    sizes = [16 * (units // 4 + (1 if i < units % 4 else 0)) for i in range(4)]
    edges = [sum(sizes[:i]) for i in range(5)]
    return [(edges[i], edges[i + 1]) for i in range(4)]


def fold8(values):
    rows, cols = values.shape
    return jnp.sum(values.reshape(rows // 8, 8, cols), axis=0)


def norm_stats(values):
    center = values - jnp.mean(values, axis=-1, keepdims=True)
    inv = lax.rsqrt(jnp.mean(center * center, axis=-1, keepdims=True) + eps_norm)
    return center * inv, inv


def norm_pull(upstream, gain, unit, inv):
    scaled = upstream * gain
    first = jnp.mean(scaled, axis=-1, keepdims=True)
    second = jnp.mean(scaled * unit, axis=-1, keepdims=True)
    return (scaled - first - unit * second) * inv


def dp_place():
    dp, me = lax.axis_index("dp"), lax.axis_index("mp")
    y, low, high = dp % 2, dp // 2 % 2, dp // 4
    return (y, low, high), (
        (dp + 1 - 2 * y, me), (dp + 2 * (1 - 2 * low), me), (dp + 4 * (1 - 2 * high), me)
    )


def by_rows(count, body):
    step = next(t for t in (64, 48, 32, 16) if count % t == 0)

    def trip(i, carry):
        body(pl.multiple_of(i * step, 16), step)
        return carry

    lax.fori_loop(0, count // step, trip, 0)


class Reduction:
    def __init__(self, rows, work, first, held, sbuf, rbuf, full, send, recv, base, order=(0, 1, 2)):
        self.rows, self.work, self.first, self.held, self.full = rows, work, first, held, full
        self.sbuf, self.rbuf, self.send, self.recv, self.base = sbuf, rbuf, send, recv, base
        bits, peers = dp_place()
        self.bits, self.peers = [bits[i] for i in order], [peers[i] for i in order]
        off = [0]
        for k in range(3):
            off.append(off[-1] + self.bits[k] * (rows >> (k + 1)))
        self.off = off
        self.steps = 6

    def copy(self, i):
        if i < 3:
            src, dst, peer = self.sbuf[i], self.rbuf[i], self.peers[i]
        else:
            k = 5 - i
            part = self.full.at[pl.ds(pl.multiple_of(self.off[k + 1], 16), self.rows >> (k + 1))]
            src, dst, peer = part, part, self.peers[k]
        return pltpu.make_async_remote_copy(
            src_ref=src, dst_ref=dst, send_sem=self.send.at[self.base + i], recv_sem=self.recv.at[self.base + i],
            device_id=peer, device_id_type=MESH,
        )

    def copies(self, i):
        return (self.copy(i),)

    def arrive(self, i):
        for copy in self.copies(i):
            copy.wait_recv()

    def leave(self, i):
        for copy in self.copies(i):
            copy.wait_send()

    def depart(self, i):
        for copy in self.copies(i):
            copy.start()

    def at(self, offset, i, step):
        return pl.ds(pl.multiple_of(offset + i - self.off[self.held], 16), step)

    def halve(self, k):
        n = self.rows >> (k + 1)
        bit = self.bits[k]
        give, keep = self.off[k] + (1 - bit) * n, self.off[k] + bit * n
        fresh = k == self.first

        def out(i, step):
            value = self.work[self.at(give, i, step), :]
            if not fresh:
                value = value + self.rbuf[k - 1][pl.ds(pl.multiple_of((1 - bit) * n + i, 16), step), :].astype(F32)
            self.sbuf[k][pl.ds(i, step), :] = value.astype(BF)

        def stay(i, step):
            rows = self.at(keep, i, step)
            self.work[rows, :] += self.rbuf[k - 1][pl.ds(pl.multiple_of(bit * n + i, 16), step), :].astype(F32)

        by_rows(n, out)
        self.depart(k)
        if not fresh:
            by_rows(n, stay)

    def settle(self, dst, at):
        def body(i, step):
            value = self.work[self.at(self.off[3], i, step), :] + self.rbuf[2][pl.ds(i, step), :].astype(F32)
            dst[pl.ds(pl.multiple_of(at + i, 16), step), :] = value.astype(dst.dtype)

        by_rows(self.rows >> 3, body)

    def step(self, i):
        if i > self.first:
            self.arrive(i - 1)
        if i < 3:
            self.halve(i)
        else:
            if i == 3:
                self.settle(self.full, self.off[3])
            self.depart(i)

    def drain(self):
        for i in range(self.first, self.steps):
            self.leave(i)


class Direct(Reduction):
    def __init__(self, rows, work, sbuf, rbuf, full, send, recv, base):
        super().__init__(rows, work, 0, 0, sbuf, rbuf, full, send, recv, base)
        self.steps = 4
        self.z = lax.axis_index("dp") // 2
        self.y = lax.axis_index("dp") % 2

    def copies(self, i):
        me = lax.axis_index("mp")
        n = self.rows >> 3
        half = pl.ds(pl.multiple_of(self.off[1], 16), 4 * n)
        if i in (0, 3):
            part = self.full.at[half]
            pairs = [(self.sbuf[0], self.rbuf[0], self.peers[0])] if i == 0 else [(part, part, self.peers[0])]
        else:
            pairs = []
            own = self.full.at[pl.ds(pl.multiple_of(self.off[1] + self.z * n, 16), n)]
            for j in range(1, 4):
                there = (self.z + j) % 4
                peer = (2 * there + self.y, me)
                if i == 1:
                    src = self.sbuf[1].at[pl.ds(pl.multiple_of(there * n, 16), n)]
                    pairs.append((src, self.rbuf[1].at[pl.ds((j - 1) * n, n)], peer))
                else:
                    pairs.append((own, own, peer))
        first = self.base + (0, 1, 4, 7)[i]
        return [
            pltpu.make_async_remote_copy(
                src_ref=src, dst_ref=dst, send_sem=self.send.at[first + j], recv_sem=self.recv.at[first + j],
                device_id=peer, device_id_type=MESH,
            )
            for j, (src, dst, peer) in enumerate(pairs)
        ]

    def step(self, i):
        n = self.rows >> 3
        if i:
            self.arrive(i - 1)
        if i == 0:
            self.halve(0)
            return
        if i == 1:

            def spread(k, step):
                rows = self.at(self.off[1], k, step)
                value = self.work[rows, :] + self.rbuf[0][pl.ds(k, step), :].astype(F32)
                self.work[rows, :] = value
                self.sbuf[1][pl.ds(k, step), :] = value.astype(BF)

            by_rows(4 * n, spread)
        elif i == 2:

            def body(k, step):
                at = self.off[1] + self.z * n
                value = self.work[self.at(at, k, step), :]
                for j in range(3):
                    value = value + self.rbuf[1][pl.ds(pl.multiple_of(j * n + k, 16), step), :].astype(F32)
                self.full[pl.ds(pl.multiple_of(at + k, 16), step), :] = value.astype(BF)

            by_rows(n, body)
        self.depart(i)


def edges(lengths, offset):
    first = offset[0]
    second = first + lengths[0, 0] + IMG
    return first, second, second + lengths[0, 1] + IMG


def ahead_kernel(
    lengths, offset, tokens, cot, w3, wout, w1, w2, biases, ln_gain, ln_bias, qv_bias,
    xfull, qkv, heads, lse, mixed, ghid, ghead, w2q, w1p, w1q, wog, sums, b1sum,
    vec, b1, mlp, act, dgel, brn, gpre, u1, u2, hid, r1, pbuf, cs, cr, xs, xr, acc, b1acc,
    qkeep, s2y, r2y, r2z, rpy, rqz, rqw, send, recv, dsend, drecv, local_sem,
):
    local, width = tokens.shape
    seq, part = heads.shape
    hidden_units = w1.shape[1]
    spans = spans_of(local)
    count = len(spans)
    dp, me = lax.axis_index("dp"), lax.axis_index("mp")
    mx, mc = me // 2, me % 2
    peer_core = (dp, mx * 2 + 1 - mc)
    peer_x = (dp, (1 - mx) * 2 + mc)
    owner = {0: me, 1: mx * 2 + 1 - mc, 2: (1 - mx) * 2 + mc, 3: (1 - mx) * 2 + 1 - mc}

    barrier = pltpu.get_barrier_semaphore()
    bits, dp_peers = dp_place()
    for peer in (peer_core, peer_x) + dp_peers:
        pl.semaphore_signal(barrier, inc=1, device_id=peer, device_id_type=MESH)
    pl.semaphore_wait(barrier, 5)

    def remote(src, dst, phase, kind, c, device):
        i = (phase * 5 + kind) * count + c
        return pltpu.make_async_remote_copy(
            src_ref=src, dst_ref=dst, send_sem=send.at[i], recv_sem=recv.at[i], device_id=device, device_id_type=MESH
        )

    def core_copy(phase, c):
        lo, hi = spans[c]
        rows = pl.ds(2 * lo, 2 * (hi - lo))
        return remote(cs.at[rows], cr.at[rows], phase, 0, c, peer_core)

    def x_copy(phase, c):
        lo, hi = spans[c]
        rows = pl.ds(lo, hi - lo)
        return remote(xs.at[rows], xr.at[rows], phase, 1, c, peer_x)

    def block(c, j):
        lo, hi = spans[c]
        return pl.ds(4 * lo + SLOT[j] * (hi - lo), hi - lo)

    def gather_copies(full, phase, c):
        own = full.at[block(c, 0)]
        return (
            remote(own, full.at[block(c, 2)], phase, 2, c, peer_x),
            remote(own, full.at[block(c, 1)], phase, 3, c, peer_core),
            remote(full.at[block(c, 2)], full.at[block(c, 3)], phase, 4, c, peer_core),
        )

    def tiles(c):
        lo, hi = spans[c]
        step = next(t for t in (48, 64, 32, 16) if (hi - lo) % t == 0)
        return (hi - lo) // step, step

    def start_gather(full, phase, c):
        first, second, _ = gather_copies(full, phase, c)
        first.start()
        second.start()

    def forward(full, phase, c):
        first, second, third = gather_copies(full, phase, c)
        first.wait_recv()
        third.start()
        second.wait_recv()
        third.wait_recv()

    def partial_products(lhs, rhs, turned, phase, c, half, wide=TILE):
        lo, hi = spans[c]
        r = hi - lo
        rows = pl.ds(4 * lo + half * 2 * r, 2 * r)
        out = pl.ds(2 * lo, 2 * r)

        def body(n, carry):
            cols = pl.ds(pl.multiple_of(n * wide, wide), wide)
            if turned:
                value = lax.dot_general(lhs[rows, :], rhs[cols, :], NT, preferred_element_type=F32)
            else:
                value = jnp.dot(lhs[rows, 0:rhs.shape[0]], rhs[:, cols], preferred_element_type=F32)
            if half == 0:
                cs[out, cols] = value.astype(BF)
            else:
                pbuf[out, cols] = value
            return carry

        lax.fori_loop(0, width // wide, body, 0)

    def pass_on(phase, c):
        lo, hi = spans[c]
        r = hi - lo
        core_copy(phase, c).wait_recv()
        if phase:
            x_copy(phase - 1, c).wait_send()
        xs[lo:hi, :] = (pbuf[2 * lo:2 * lo + r, :] + cr[2 * lo + r:2 * lo + 2 * r, :].astype(F32)).astype(BF)
        x_copy(phase, c).start()

    def own_total(c, i, step):
        lo, hi = spans[c]
        r = hi - lo
        kept = pl.ds(pl.multiple_of(2 * lo + r + i * step, 16), step)
        near = pl.ds(pl.multiple_of(2 * lo + i * step, 16), step)
        far = pl.ds(pl.multiple_of(lo + i * step, 16), step)
        return far, pbuf[kept, :] + cr[near, :].astype(F32) + xr[far, :].astype(F32)

    def row(i):
        return vec[i:i + 1, :]

    wide_biases = biases[...].astype(F32)
    vec[0:2, :] = wide_biases[0:2, :]
    gain, shift = ln_gain[...].astype(F32), ln_bias[...].astype(F32)
    for i in range(4):
        at = 2 * i if i else 8
        vec[at:at + 1, :] = gain[i:i + 1, :]
        vec[at + 1:at + 2, :] = shift[i:i + 1, :]
    b1[...] = wide_biases[2:3, :]
    bias = qv_bias[...].astype(F32)
    acc[...] = jnp.zeros_like(acc)
    b1acc[...] = jnp.zeros_like(b1acc)

    def add(i, values):
        acc[8 * i:8 * i + 8, :] += fold8(values)

    def project(c):
        lo, hi = spans[c]
        for j in (1, 3, 2, 0):
            start = pl.multiple_of(owner[j] * local + lo, 16)
            mlp[block(c, j), 0:part] = heads[pl.ds(start, hi - lo), :]
        partial_products(mlp, wout, False, 0, c, 0)
        core_copy(0, c).start()
        partial_products(mlp, wout, False, 0, c, 1)

    xf = gpre

    def place(j, c):
        lo, hi = spans[c]
        return pl.ds(pl.multiple_of(owner[j] * local + lo, 16), hi - lo)

    def first_copies(c):
        own, across = xf.at[place(0, c)], xf.at[place(2, c)]
        return (
            remote(own, own, 3, 2, c, peer_x),
            remote(own, own, 3, 3, c, peer_core),
            remote(across, across, 3, 4, c, peer_core),
        )

    for c in range(count):
        lo, hi = spans[c]
        trips, step = tiles(c)

        def first_norm(i, carry):
            rows = pl.ds(pl.multiple_of(lo + i * step, 16), step)
            unit, _ = norm_stats(tokens[rows, :].astype(F32))
            dst = pl.ds(pl.multiple_of(me * local + lo + i * step, 16), step)
            xf[dst, :] = (unit * row(8) + row(9)).astype(BF)
            return carry

        lax.fori_loop(0, trips, first_norm, 0)
        for copy in first_copies(c)[:2]:
            copy.start()

    def projections(rows):
        for t in range(3):
            value = jnp.dot(xf[rows, :], w3[t], preferred_element_type=F32)
            if t != 1:
                value = value + bias[t // 2:t // 2 + 1, :]
            act[rows, t * part:(t + 1) * part] = value.astype(BF)

    projections(pl.ds(pl.multiple_of(owner[0] * local, 16), local))
    for c in range(count):
        first_copies(c)[1].wait_recv()
    projections(pl.ds(pl.multiple_of(owner[1] * local, 16), local))
    for c in range(count):
        first_copies(c)[0].wait_recv()
        first_copies(c)[2].start()
        projections(place(2, c))
        if c:
            first_copies(c - 1)[2].wait_recv()
            projections(place(3, c - 1))
    first_copies(count - 1)[2].wait_recv()
    projections(place(3, count - 1))
    keep_x = pltpu.make_async_copy(xf, xfull, local_sem.at[0])
    keep_qkv = pltpu.make_async_copy(act.at[:, 0:3 * part], qkv, local_sem.at[1])
    keep_x.start()
    keep_qkv.start()

    edge0, edge1, edge2 = edges(lengths, offset)
    lo_edge, hi_edge, _, _, cuts = plan(seq)
    pair = 2 * HEAD
    lane = lax.broadcasted_iota(jnp.int32, (1, pair), 1)

    def attend(c):
        lo, hi = spans[c]
        n = hi - lo

        def one_head(h, carry):
            mine = (lane // HEAD) == h % 2
            shift = h // 2 * pair
            qcols, kcols, vcols = (
                pl.ds(pl.multiple_of(t * part + shift, pair), pair) for t in range(3)
            )
            for o in range(4):
                a = o * local + lo
                b = a + n
                start = 0 if a < hi_edge else lo_edge
                stop = -(-b // LANES) * LANES
                qm = jnp.where(mine, act[a:b, qcols].astype(F32) * HEAD**-0.5, 0.0).astype(BF)
                qpos = a + lax.broadcasted_iota(jnp.int32, (n, 1), 0)
                first = seg_start(qpos, edge0, edge1, edge2)
                parts, top = [], None
                for k0, k1 in cuts(start, stop, LANES):
                    s = lax.dot_general(qm, act[k0:k1, kcols], NT, preferred_element_type=F32)
                    if not free_of_mask(k0, k1, a, b, seq):
                        kpos = k0 + lax.broadcasted_iota(jnp.int32, (n, k1 - k0), 1)
                        s = jnp.where((kpos >= first) & (kpos <= qpos), s, -1e9)
                    parts.append(s)
                    top = s if top is None else jnp.maximum(top, s)
                m = jnp.max(top, axis=1, keepdims=True)
                es = [jnp.exp(s - m) for s in parts]
                tot = es[0]
                for e in es[1:]:
                    tot = tot + e
                l = jnp.sum(tot, axis=1, keepdims=True)
                p = jnp.concatenate([e.astype(BF) for e in es], axis=1)
                out = jnp.dot(p, act[start:stop, vcols], preferred_element_type=F32) / l
                hcols = pl.ds(pl.multiple_of(shift, pair), pair)
                heads[a:b, hcols] = jnp.where(mine, out.astype(BF), heads[a:b, hcols])
                log_total = m + jnp.log(l)
                which = lax.broadcasted_iota(jnp.int32, (1, LANES), 1) == h
                at = slice(o * LANES, (o + 1) * LANES)
                ghid[lo:hi, at] = jnp.where(which, log_total, ghid[lo:hi, at])
            return carry

        lax.fori_loop(0, part // HEAD, one_head, 0)

    def two_norms(c):
        x_copy(0, c).wait_recv()
        lo, hi = spans[c]
        trips, step = tiles(c)

        def norms(i, carry):
            rows, total = own_total(c, i, step)
            unit, inv = norm_stats(total + row(0))
            u1[rows, :] = unit
            r1[rows, 0:HEAD] = jnp.broadcast_to(inv, (step, HEAD))
            hidden = tokens[rows, :].astype(F32) + unit * row(2) + row(3)
            hid[rows, :] = hidden
            unit, inv = norm_stats(hidden)
            u2[rows, :] = unit
            r1[rows, HEAD:LANES] = jnp.broadcast_to(inv, (step, HEAD))
            dst = pl.ds(pl.multiple_of(4 * lo + SLOT[0] * (hi - lo) + i * step, 16), step)
            mlp[dst, :] = (unit * row(4) + row(5)).astype(BF)
            return carry

        lax.fori_loop(0, trips, norms, 0)
        start_gather(mlp, 0, c)

    for c in range(count):
        attend(c)
        project(c)
        pass_on(0, c)
        if c >= AHEAD:
            two_norms(c - AHEAD)
    for c in range(count - AHEAD, count):
        two_norms(c)
    keep_lse = [
        pltpu.make_async_copy(ghid.at[:, o * LANES:(o + 1) * LANES], lse.at[o], local_sem.at[2 + o]) for o in range(4)
    ]
    for copy in keep_lse:
        copy.start()
    for copy in [keep_qkv, keep_x] + keep_lse:
        copy.wait()
    for c in range(count):
        for copy in first_copies(c):
            copy.wait_send()

    for c in range(count):
        lo, hi = spans[c]
        r = hi - lo
        forward(mlp, 0, c)
        core_copy(0, c).wait_send()
        for half in range(2):
            rows = pl.ds(4 * lo + half * 2 * r, 2 * r)

            def units(n, carry):
                cols = pl.ds(pl.multiple_of(n * TILE, TILE), TILE)
                pre = jnp.dot(mlp[rows, :], w1[:, cols], preferred_element_type=F32) + b1[:, cols]
                square = pre * pre
                inner = (0.7978845608028654 * pre) * (1.0 + 0.044715 * square)
                tanh = jnp.tanh(inner)
                plus = 0.5 * (1.0 + tanh)
                act[rows, cols] = (pre * plus).astype(BF)
                slope = plus + (0.5 * pre) * (1.0 - tanh * tanh) * (
                    0.7978845608028654 * (1.0 + (3 * 0.044715) * square)
                )
                dgel[rows, cols] = slope.astype(BF)
                return carry

            lax.fori_loop(0, hidden_units // TILE, units, 0)
            partial_products(act, w2, False, 1, c, half)
            if half == 0:
                core_copy(1, c).start()
        pass_on(1, c)

    for c in range(count):
        x_copy(1, c).wait_recv()
        lo, hi = spans[c]
        trips, step = tiles(c)

        def last(i, carry):
            rows, total = own_total(c, i, step)
            unit, inv = norm_stats(total + row(1))
            mixed[rows, :] = (hid[rows, :] + unit * row(6) + row(7)).astype(BF)
            grad = cot[rows, :].astype(F32)
            add(2, grad * unit)
            add(5, grad)
            low = norm_pull(grad, row(6), unit, inv).astype(BF)
            add(7, low.astype(F32))
            dst = pl.ds(pl.multiple_of(4 * lo + SLOT[0] * (hi - lo) + i * step, 16), step)
            brn[dst, :] = low
            return carry

        lax.fori_loop(0, trips, last, 0)
        start_gather(brn, 1, c)

    sum2 = Reduction(hidden_units, hid, 0, 1, (s2y, act.at[512:768]), (r2y, r2z), None, dsend, drecv, 0)
    sump = Reduction(width // 2, w1p, 0, 1, (act.at[0:256],), (rpy,), None, dsend, drecv, 2)
    sumq = Reduction(
        width // 2, qkeep, 0, 1, (act.at[256:512], act.at[768:896]), (rqz, rqw), None, dsend, drecv, 3,
        order=(1, 2, 0),
    )

    def weight_grad(lhs, rhs, first, rows, dst):
        for n in range(rows // TILE):
            cols = pl.ds(pl.multiple_of(first + n * TILE, TILE), TILE)
            value = lax.dot_general(lhs[:, cols], rhs[...], TN, preferred_element_type=F32)
            dst[n * TILE:(n + 1) * TILE, :] = value.astype(dst.dtype)

    half2, half1 = hidden_units // 2, width // 4

    for c in range(count):
        lo, hi = spans[c]
        r = hi - lo
        forward(brn, 1, c)
        if c == count - 1:
            weight_grad(act, brn, (1 - sum2.bits[0]) * half2, half2, s2y)
            sum2.depart(0)
        core_copy(1, c).wait_send()
        for half in range(2):
            rows = pl.ds(4 * lo + half * 2 * r, 2 * r)

            def slopes(n, carry):
                cols = pl.ds(pl.multiple_of(n * TILE, TILE), TILE)
                grad = lax.dot_general(brn[rows, :], w2[cols, :], NT, preferred_element_type=F32)
                low = (grad * dgel[rows, cols].astype(F32)).astype(BF)
                gpre[rows, cols] = low
                b1acc[:, cols] += fold8(low.astype(F32))
                return carry

            lax.fori_loop(0, hidden_units // TILE, slopes, 0)
            partial_products(gpre, w1, True, 2, c, half)
            if half == 0:
                core_copy(2, c).start()
        pass_on(2, c)

    weight_grad(act, brn, sum2.bits[0] * half2, half2, hid)

    for c in range(count):
        x_copy(2, c).wait_recv()
        lo, hi = spans[c]
        trips, step = tiles(c)

        def pulls(i, carry):
            rows, total = own_total(c, i, step)
            unit = u2[rows, :]
            add(1, total * unit)
            add(4, total)
            grad = cot[rows, :].astype(F32) + norm_pull(total, row(4), unit, r1[rows, HEAD:HEAD + 1])
            ghid[rows, :] = grad
            unit = u1[rows, :]
            add(0, grad * unit)
            add(3, grad)
            low = norm_pull(grad, row(2), unit, r1[rows, 0:1]).astype(BF)
            add(6, low.astype(F32))
            dst = pl.ds(pl.multiple_of(4 * lo + SLOT[0] * (hi - lo) + i * step, 16), step)
            dgel[dst, :] = low
            return carry

        lax.fori_loop(0, trips, pulls, 0)
        start_gather(dgel, 2, c)
        if c == 0:
            weight_grad(mlp, gpre, (1 - sump.bits[0]) * half1, half1, act)
            sump.depart(0)
            weight_grad(mlp, gpre, width // 2 + (1 - sumq.bits[0]) * half1, half1, act.at[256:512])
            sumq.depart(0)
        elif c == 2:
            weight_grad(mlp, gpre, width // 2 + sumq.bits[0] * half1, half1, qkeep)

    sum2.step(1)
    weight_grad(mlp, gpre, sump.bits[0] * half1, half1, w1p)
    for c in range(count):
        for copy in gather_copies(brn, 1, c):
            copy.wait_send()
    for c in range(count):
        lo, hi = spans[c]
        forward(dgel, 2, c)
        for j in (1, 3, 2, 0):
            start = pl.multiple_of(owner[j] * local + lo, 16)
            brn[block(c, j), 0:part] = heads[pl.ds(start, hi - lo), :]
            ghead[pl.ds(start, hi - lo), :] = lax.dot_general(
                dgel[block(c, j), :], wout[...], NT, preferred_element_type=F32
            ).astype(BF)
        rows = pl.ds(4 * lo, 4 * (hi - lo))
        share = lax.dot_general(brn[rows, 0:part], dgel[rows, :], TN, preferred_element_type=F32)
        wog[...] = wog[...] + share if c else share
        if c == 0:
            sumq.step(1)
    for stream, last, work, got, dst in (
        (sump, 0, w1p, rpy, w1p), (sum2, 1, hid, r2z, w2q), (sumq, 1, qkeep, rqw, w1q)
    ):
        stream.arrive(last)

        def join(i, step, stream=stream, last=last, work=work, got=got, dst=dst):
            rows = stream.at(stream.off[last + 1], i, step)
            dst[pl.ds(i, step), :] = work[rows, :] + got[pl.ds(i, step), :].astype(F32)

        by_rows(stream.rows >> (last + 1), join)
        for i in range(last + 1):
            stream.leave(i)

    for i in range(8):
        sums[i:i + 1, :] = jnp.sum(acc[8 * i:8 * i + 8, :], axis=0, keepdims=True)
    b1sum[...] = jnp.sum(b1acc[...], axis=0, keepdims=True)

    for c in range(count):
        core_copy(2, c).wait_send()
        x_copy(2, c).wait_send()
        for phase, full in ((0, mlp), (2, dgel)):
            for copy in gather_copies(full, phase, c):
                copy.wait_send()


def ahead(lengths, offset, tokens, cot, w3, wout, w1, w2, biases, ln_gain, ln_bias, qv_bias):
    local, width = tokens.shape
    seq = 4 * local
    part = w3.shape[2]
    units = w1.shape[1]
    vmem = pl.BlockSpec(memory_space=pltpu.VMEM)
    any_spec = pl.BlockSpec(memory_space=pl.ANY)
    shape = jax.ShapeDtypeStruct
    copies = 20 * 4
    low = lambda *dims: pltpu.VMEM(dims, BF)
    wide = lambda *dims: pltpu.VMEM(dims, F32)
    dma = lambda n: pltpu.SemaphoreType.DMA((n,))
    return pl.pallas_call(
        ahead_kernel,
        in_specs=[pl.BlockSpec(memory_space=pltpu.SMEM)] * 2 + [vmem] * 10,
        out_specs=[any_spec, any_spec, vmem, any_spec] + [vmem] * 9,
        out_shape=[
            shape((seq, width), BF), shape((seq, 3 * part), BF), shape((seq, part), BF), shape((4, local, LANES), F32),
            shape((local, width), BF), shape((local, width), F32), shape((seq, part), BF),
            shape((units // 4, width), F32), shape((width // 4, units), F32), shape((width // 8, units), F32),
            shape((part, width), F32), shape((8, width), F32), shape((1, units), F32),
        ],
        scratch_shapes=[
            wide(16, width), wide(1, units), low(seq, width), low(seq, units), low(seq, units), low(seq, width), low(seq, units),
            wide(local, width), wide(local, width), wide(local, width), wide(local, LANES),
            wide(2 * local, width), low(2 * local, width), low(2 * local, width), low(local, width),
            low(local, width), wide(64, width), wide(8, units),
            wide(width // 4, units), low(units // 2, width), low(units // 2, width), low(units // 4, width),
            low(width // 4, units), low(width // 4, units), low(width // 8, units),
            dma(copies), dma(copies), dma(5), dma(5), dma(6),
        ],
        compiler_params=pltpu.CompilerParams(collective_id=0, has_side_effects=True, vmem_limit_bytes=63 << 20),
        cost_estimate=pl.CostEstimate(
            flops=16 * seq * width * units, bytes_accessed=50 << 20, transcendentals=2 * seq * units
        ),
        name="ahead",
    )(lengths, offset, tokens, cot, w3, wout, w1, w2, biases, ln_gain, ln_bias, qv_bias)


ORDER = {
    "start": (("o", 0), ("2", 2),),
    3: (("q", 2),),
    4: (("o", 1),),
    5: (("p", 1),),
    6: (("2", 3), ("a", 0),),
    8: (("o", 2),),
    9: (("q", 3), ("p", 2),),
    11: (("2", 4),),
    12: (("q", 4), ("o", 3), ("b", 0),),
    "x0": (("p", 3), ("2", 5),),
    "x1": (("a", 1),),
    "x2": (("p", 4), ("b", 1),),
    "x3": (("a", 2),),
    "n0": (("p", 5),),
    "near": (("b", 2),),
    "far": (("a", 3), ("q", 5),),
    "end": (("b", 3),),
}


def back_kernel(
    lengths, offset, qkv_in, o_in, do_in, lse_in, xfull_in, w3, ghid_in, tokens_in, ln_gain, w2q, w1p, w1q, wog_in, sums_in, b1_in,
    tgrad, w2f, w1f, wof, wqt, small_out,
    qkv, o_ref, do_ref, lse_col, xfull, ghid, tokens, lse_s, qm_s, dom_s, dqt_s, delta_s, gp, w_in, wq, wqf, wog, pbuf, cs, cr, xs, xr, gs, acc,
    s2w, r2w, spz, spw, rpz, rpw, s1q, r1q, soy, soz, roy, roz, say, saz, ray, raz, small, near, far,
    send, recv, dsend, drecv, nsend, nrecv, fsend, frecv, lsem,
):
    local, width = tokens.shape
    seq, part = o_ref.shape
    heads = part // HEAD
    spans = spans_of(local)
    count = len(spans)
    pair = part // 2
    moves = [
        pltpu.make_async_copy(src, dst, lsem.at[i])
        for i, (src, dst) in enumerate(
            (
                (qkv_in, qkv), (do_in, do_ref), (o_in, o_ref), (lse_in, lse_col), (xfull_in, xfull), (ghid_in, ghid),
                (tokens_in, tokens),
            )
        )
    ] + [
        pltpu.make_async_copy(
            w3.at[t, :, i * pair:(i + 1) * pair], w_in.at[:, (3 * i + t) * pair:(3 * i + t + 1) * pair],
            lsem.at[7 + 3 * i + t],
        )
        for i in range(2)
        for t in range(3)
    ]
    for move in moves:
        move.start()
    dp, me = lax.axis_index("dp"), lax.axis_index("mp")
    mx, mc = me // 2, me % 2
    owner = {0: me, 1: mx * 2 + 1 - mc, 2: (1 - mx) * 2 + mc, 3: (1 - mx) * 2 + 1 - mc}
    peer_core, peer_x, peer_far = (dp, owner[1]), (dp, owner[2]), (dp, owner[3])
    near_peers = (peer_core, peer_x, peer_far)
    far_peers = tuple(((dp + i) % 8, me) for i in range(1, 8))
    barrier = pltpu.get_barrier_semaphore()
    for peer in near_peers + far_peers:
        pl.semaphore_signal(barrier, inc=1, device_id=peer, device_id_type=MESH)
    pl.semaphore_wait(barrier, 10)

    half = w1f.shape[0] // 2
    streams = {
        "2": Reduction(w2f.shape[0], w2q, 2, 2, (None, None, s2w), (None, None, r2w), w2f, dsend, drecv, 0),
        "p": Reduction(half, w1p, 1, 1, (None, spz, spw), (None, rpz, rpw), w1f.at[0:half], dsend, drecv, 6),
        "q": Reduction(
            half, w1q, 2, 2, (None, None, s1q), (None, None, r1q), w1f.at[half:2 * half], dsend, drecv, 12,
            order=(1, 2, 0),
        ),
        "o": Direct(part, wog, (soy, soz), (roy, roz), wof, dsend, drecv, 18),
        "a": Direct(3 * pair, wq.at[0], (say.at[0], saz.at[0]), (ray.at[0], raz.at[0]), wqf.at[0], dsend, drecv, 26),
        "b": Direct(3 * pair, wq.at[1], (say.at[1], saz.at[1]), (ray.at[1], raz.at[1]), wqf.at[1], dsend, drecv, 34),
    }

    b0, b1, b2 = edges(lengths, offset)
    gain0 = ln_gain[...].astype(F32)[0:1, :]
    lo_edge, hi_edge, _, _, cut = plan(seq)
    lane = lax.broadcasted_iota(jnp.int32, (1, pair), 1)

    def mask_of(h):
        return (lane // HEAD) == h % 2

    def cols_of(h):
        return pl.ds(pl.multiple_of(h // 2 * pair, pair), pair)

    def grad_cols(h, t):
        return pl.ds(pl.multiple_of(h // 2 * 3 * pair + t * pair, pair), pair)

    def prepare(h):
        mine, cols = mask_of(h), cols_of(h)
        qm_s[...] = jnp.where(mine, qkv[:, cols].astype(F32) * HEAD**-0.5, 0.0).astype(BF)
        dom_s[...] = jnp.where(mine, do_ref[:, cols], jnp.zeros((), BF))
        ones = jnp.ones((8, pair), F32)
        for a, b in cut(0, seq, 256):
            prod = dom_s[a:b, :].astype(F32) * o_ref[a:b, cols].astype(F32)
            delta_s[:, a:b] = lax.dot_general(
                ones, prod, NT, preferred_element_type=F32, precision=lax.Precision.HIGHEST
            )
        dqt_s[...] = jnp.zeros_like(dqt_s)

    def key_blocks(h, blocks):
        mine = mask_of(h)
        key_cols, value_cols = (pl.ds(pl.multiple_of(t * part + h // 2 * pair, pair), pair) for t in (1, 2))
        for a, b, stop in blocks:
            n = b - a
            kk = qkv[a:b, key_cols]
            vv = qkv[a:b, value_cols]
            kpos = a + lax.broadcasted_iota(jnp.int32, (n, 1), 0)
            kh = jnp.where(mine, kk, jnp.zeros((), BF))
            pts, dsts = [], []
            for c, d in cut(a, stop, 128):
                st = lax.dot_general(kk, qm_s[c:d, :], NT, preferred_element_type=F32)
                pt = jnp.exp(st - lse_s[h, 0:1, c:d])
                if not free_of_mask(a, b, c, d, seq):
                    qpos = c + lax.broadcasted_iota(jnp.int32, (1, d - c), 1)
                    first = seg_start(qpos, b0, b1, b2)
                    pt = jnp.where((kpos >= first) & (kpos <= qpos), pt, 0.0)
                dpt = lax.dot_general(vv, dom_s[c:d, :], NT, preferred_element_type=F32)
                pts.append(pt.astype(BF))
                dsts.append((pt * (dpt - delta_s[0:1, c:d])).astype(BF))
            pt = jnp.concatenate(pts, axis=1)
            dst = jnp.concatenate(dsts, axis=1)
            dv = jnp.dot(pt, dom_s[a:stop, :], preferred_element_type=F32)
            dk = jnp.dot(dst, qm_s[a:stop, :], preferred_element_type=F32)
            gv, gk = grad_cols(h, 2), grad_cols(h, 1)
            gp[a:b, gv] = jnp.where(mine, dv.astype(BF), gp[a:b, gv])
            gp[a:b, gk] = jnp.where(mine, dk.astype(BF), gp[a:b, gk])
            dqt_s[:, a:stop] += lax.dot_general(kh, dst, TN, preferred_element_type=F32)

    def finish_queries(h):
        mine, gq = mask_of(h), grad_cols(h, 0)
        for a, b in cut(0, seq, 128):
            dq = (dqt_s[:, a:b] * HEAD**-0.5).T
            gp[a:b, gq] = jnp.where(mine, dq.astype(BF), gp[a:b, gq])

    def input_grad(i):
        wq[i] = lax.dot_general(
            gp[:, i * 3 * pair:(i + 1) * 3 * pair], xfull[...], TN, preferred_element_type=F32
        )

    def turn(i):
        for t in range(3):
            wqt[t, :, i * pair:(i + 1) * pair] = wqf[i, t * pair:(t + 1) * pair, :].T

    def run(point):
        for name, step in ORDER.get(point, ()):
            if step == 0 and name in "ab":
                input_grad("ab".index(name))
            streams[name].step(step)

    wog[...] = wog_in[...]
    run("start")
    gp[...] = jnp.zeros_like(gp)
    for move in moves:
        move.wait()
    for a, b in cut(0, seq, LANES):
        turned = lse_col[a:b, :].T
        for h in range(heads):
            lse_s[h, 0:1, a:b] = turned[h:h + 1, :]

    groups = (
        [(a, b, hi_edge) for a, b in cut(0, lo_edge, 256)][:2],
        [(a, b, hi_edge) for a, b in cut(0, lo_edge, 256)][2:] + [(a, b, seq) for a, b in cut(lo_edge, hi_edge, 256)],
        [(a, b, seq) for a, b in cut(hi_edge, seq, 256)],
    )

    def one_head(h, carry):
        prepare(h)
        for g, blocks in enumerate(groups):
            key_blocks(h, blocks)
            if g == 2:
                finish_queries(h)
            for k in range(heads):
                if (3 * k + g + 1) in ORDER:

                    @pl.when(h == k)
                    def _(k=k, g=g):
                        run(3 * k + g + 1)

        return carry

    lax.fori_loop(0, heads, one_head, 0)

    def remote(src, dst, kind, c, device):
        i = kind * count + c
        return pltpu.make_async_remote_copy(
            src_ref=src, dst_ref=dst, send_sem=send.at[i], recv_sem=recv.at[i], device_id=device, device_id_type=MESH
        )

    def core_copy(c):
        lo, hi = spans[c]
        rows = pl.ds(2 * lo, 2 * (hi - lo))
        return remote(cs.at[rows], cr.at[rows], 0, c, peer_core)

    def x_copy(c):
        lo, hi = spans[c]
        rows = pl.ds(lo, hi - lo)
        return remote(xs.at[rows], xr.at[rows], 1, c, peer_x)

    def project(c):
        lo, hi = spans[c]
        r = hi - lo
        for half in range(2):
            out = pl.ds(2 * lo, 2 * r)
            for s, j in enumerate(((1, 3), (2, 0))[half]):
                src = pl.ds(pl.multiple_of(owner[j] * local + lo, 16), r)
                gs[s * r:(s + 1) * r, :] = gp[src, :]

            def body(n, carry):
                cols = pl.ds(pl.multiple_of(n * TILE, TILE), TILE)
                value = lax.dot_general(gs[0:2 * r, :], w_in[cols, :], NT, preferred_element_type=F32)
                if half == 0:
                    cs[out, cols] = value.astype(BF)
                else:
                    pbuf[out, cols] = value
                return carry

            lax.fori_loop(0, width // TILE, body, 0)
            if half == 0:
                core_copy(c).start()

    def pass_on(c):
        lo, hi = spans[c]
        r = hi - lo
        core_copy(c).wait_recv()
        xs[lo:hi, :] = (pbuf[2 * lo:2 * lo + r, :] + cr[2 * lo + r:2 * lo + 2 * r, :].astype(F32)).astype(BF)
        x_copy(c).start()

    project(0)
    for c in range(count):
        if c + 1 < count:
            project(c + 1)
        pass_on(c)
        run("x%d" % c)

    acc[...] = jnp.zeros_like(acc)
    for c in range(count):
        x_copy(c).wait_recv()
        lo, hi = spans[c]
        r = hi - lo
        step = next(t for t in (48, 64, 32, 16) if r % t == 0)

        def pulls(i, carry):
            kept = pl.ds(pl.multiple_of(2 * lo + r + i * step, 16), step)
            close = pl.ds(pl.multiple_of(2 * lo + i * step, 16), step)
            rows = pl.ds(pl.multiple_of(lo + i * step, 16), step)
            total = pbuf[kept, :] + cr[close, :].astype(F32) + xr[rows, :].astype(F32)
            unit, inv = norm_stats(tokens[rows, :].astype(F32))
            acc[0:8, :] += fold8(total * unit)
            acc[8:16, :] += fold8(total)
            tgrad[rows, :] = (ghid[rows, :] + norm_pull(total, gain0, unit, inv)).astype(BF)
            return carry

        lax.fori_loop(0, r // step, pulls, 0)
        run("n%d" % c)

    small[...] = jnp.zeros_like(small)
    small[2:10, :] = sums_in[...]
    small[10:11, :] = b1_in[...]
    small[0:1, :] = jnp.sum(acc[0:8, :], axis=0, keepdims=True)
    small[1:2, :] = jnp.sum(acc[8:16, :], axis=0, keepdims=True)
    bias = jnp.sum(gp[...].astype(F32), axis=0, keepdims=True)
    for i in range(2):
        for t in range(2):
            at = (3 * i + 2 * t) * pair
            small[11:12, t * part + i * pair:t * part + (i + 1) * pair] = bias[:, at:at + pair]

    def near_copy(i):
        return pltpu.make_async_remote_copy(
            src_ref=small, dst_ref=near.at[me], send_sem=nsend.at[i], recv_sem=nrecv.at[i], device_id=near_peers[i],
            device_id_type=MESH,
        )

    def far_copy(i):
        return pltpu.make_async_remote_copy(
            src_ref=small_out, dst_ref=far.at[dp], send_sem=fsend.at[i], recv_sem=frecv.at[i], device_id=far_peers[i],
            device_id_type=MESH,
        )

    for i in range(3):
        near_copy(i).start()
    run("near")
    for i in range(3):
        near_copy(i).wait_recv()
    own = lax.broadcasted_iota(jnp.int32, (16, 1), 0) >= 10
    near[me] = small[...]
    small_out[...] = jnp.where(own, small[...], ((near[0] + near[1]) + near[2]) + near[3])
    for i in range(7):
        far_copy(i).start()
    run("far")
    for i in range(7):
        far_copy(i).wait_recv()
    for i in range(7):
        far_copy(i).wait_send()
    far[dp] = small_out[...]
    total = far[0]
    for i in range(1, 8):
        total = total + far[i]
    small_out[...] = total
    run("end")
    for name in ("a", "b"):
        streams[name].arrive(3)
        turn("ab".index(name))

    for name in ("2", "p", "q", "o"):
        streams[name].arrive(streams[name].steps - 1)
    for stream in streams.values():
        stream.drain()
    for i in range(3):
        near_copy(i).wait_send()
    for c in range(count):
        core_copy(c).wait_send()
        x_copy(c).wait_send()


def back(lengths, offset, qkv, o, do, lse, xfull, w3, ghid, tokens, ln_gain, w2q, w1p, w1q, wog, sums, b1_part):
    seq, part = o.shape
    local, width = tokens.shape
    units = w1p.shape[1]
    pair = part // 2
    vmem = pl.BlockSpec(memory_space=pltpu.VMEM)
    shape = jax.ShapeDtypeStruct
    low = lambda *dims: pltpu.VMEM(dims, BF)
    wide = lambda *dims: pltpu.VMEM(dims, F32)
    dma = lambda n: pltpu.SemaphoreType.DMA((n,))
    return pl.pallas_call(
        back_kernel,
        in_specs=[pl.BlockSpec(memory_space=pltpu.SMEM)] * 2 + [pl.BlockSpec(memory_space=pl.ANY)] * 8 + [vmem] * 7,
        out_specs=[vmem] * 6,
        out_shape=[
            shape((local, width), BF), shape((4 * w2q.shape[0], width), BF), shape((width, units), BF),
            shape((part, width), BF), shape((3, width, part), BF), shape((16, width), F32),
        ],
        scratch_shapes=[
            low(seq, 3 * part), low(seq, part), low(seq, part), wide(seq, LANES), low(seq, width),
            wide(local, width), low(local, width), wide(part // HEAD, 8, seq), low(seq, pair), low(seq, pair), wide(pair, seq), wide(8, seq), low(seq, 3 * part), low(width, 3 * part),
            wide(2, 3 * pair, width), low(2, 3 * pair, width), wide(part, width), wide(2 * local, width), low(2 * local, width),
            low(2 * local, width), low(local, width), low(local, width), low(seq // 6 // 16 * 16, 3 * part), wide(16, width),
            low(units // 8, width), low(units // 8, width), low(width // 8, units), low(width // 16, units),
            low(width // 8, units), low(width // 16, units), low(width // 16, units), low(width // 16, units),
            low(part // 2, width), low(part // 2, width), low(part // 2, width), low(3 * part // 8, width),
            low(2, 3 * pair // 2, width), low(2, 3 * pair // 2, width), low(2, 3 * pair // 2, width),
            low(2, 9 * pair // 8, width),
            wide(16, width), wide(4, 16, width), wide(8, 16, width),
            dma(8), dma(8), dma(42), dma(42), dma(3), dma(3), dma(7), dma(7), dma(13),
        ],
        compiler_params=pltpu.CompilerParams(collective_id=1, has_side_effects=True, vmem_limit_bytes=63 << 20),
        cost_estimate=pl.CostEstimate(flops=20 << 30, bytes_accessed=40 << 20, transcendentals=8 << 20),
        name="back",
    )(lengths, offset, qkv, o, do, lse, xfull, w3, ghid, tokens, ln_gain, w2q, w1p, w1q, wog, sums, b1_part)


def finish_kernel(
    w2f, w1f, wof, wqt, small, tgrad_in, mixed_in, w2o, w1o, woo, wqo, gains, shifts, out_bias, b2, b1, qv, tgrad,
    mixed,
):
    tgrad[...] = tgrad_in[...]
    mixed[...] = mixed_in[...]
    w2o[...] = w2f[...].astype(F32)
    w1o[...] = w1f[...].astype(F32)
    woo[...] = wof[...].astype(F32)
    wqo[...] = wqt[...].astype(F32)
    part = qv.shape[1]
    gains[0:1, :] = small[0:1, :]
    gains[1:4, :] = small[2:5, :]
    shifts[0:1, :] = small[1:2, :]
    shifts[1:4, :] = small[5:8, :]
    out_bias[...] = small[8:9, :]
    b2[...] = small[9:10, :]
    b1[...] = small[10:11, :]
    qv[0:1, :] = small[11:12, 0:part]
    qv[1:2, :] = small[11:12, part:2 * part]


def finish(w2f, w1f, wof, wqt, small, tgrad, mixed):
    parts = 4
    shape = jax.ShapeDtypeStruct
    part = wof.shape[0]
    halves = pl.BlockSpec((tgrad.shape[0] // 2, tgrad.shape[1]), lambda i: (i * 2 // parts, 0))
    rows = lambda a: pl.BlockSpec((a.shape[0] // parts, a.shape[1]), lambda i: (i, 0))
    turned = pl.BlockSpec((3, wqt.shape[1] // parts, part), lambda i: (0, i, 0))
    fixed = lambda n, m: pl.BlockSpec((n, m), lambda i: (0, 0))
    width, units = w2f.shape[1], w1f.shape[1]
    return pl.pallas_call(
        finish_kernel,
        grid=(parts,),
        in_specs=[rows(w2f), rows(w1f), rows(wof), turned, fixed(*small.shape), halves, halves],
        out_specs=[
            rows(w2f), rows(w1f), rows(wof), turned, fixed(4, width), fixed(4, width), fixed(1, width),
            fixed(1, width), fixed(1, units), fixed(2, part), halves, halves,
        ],
        out_shape=[
            shape(w2f.shape, F32), shape(w1f.shape, F32), shape(wof.shape, F32), shape(wqt.shape, F32),
            shape((4, width), F32), shape((4, width), F32), shape((1, width), F32), shape((1, width), F32),
            shape((1, units), F32), shape((2, part), F32), shape(tgrad.shape, BF), shape(mixed.shape, BF),
        ],
        compiler_params=pltpu.CompilerParams(vmem_limit_bytes=56 << 20),
        name="finish",
    )(w2f, w1f, wof, wqt, small, tgrad, mixed)


def shards(
    tokens, caption_len, row_offset, wqkv, qv_bias, wout, out_bias, w1, b1, w2, b2, ln_gain, ln_bias, cotangent,
):
    local_rows, width = tokens.shape
    head_part = wqkv.shape[2]
    here = lax.axis_size("dp") == 8 and lax.axis_size("mp") == 4 and head_part == TILE
    if not (here and width == w1.shape[1] == 1024 and local_rows % 32 == 0):
        return shards_by_ops(
            tokens, caption_len, row_offset, wqkv, qv_bias, wout, out_bias, w1, b1, w2, b2, ln_gain, ln_bias,
            cotangent,
        )
    w3 = wqkv.transpose(1, 0, 2)
    (
        xfull, qkv, heads, lse, mixed, grad_hidden, grad_heads, w2_part, w1_first, w1_last, wout_part, sums, b1_part,
    ) = ahead(
        caption_len, row_offset, tokens, cotangent, w3, wout, w1, w2,
        jnp.concatenate([out_bias, b2, b1]).reshape(3, width), ln_gain, ln_bias, qv_bias,
    )
    tokens_grad, w2_grad, w1_grad, wout_grad, wqkv_grad, small = back(
        caption_len, row_offset, qkv, heads, grad_heads, lse.reshape(-1, LANES), xfull, w3, grad_hidden, tokens,
        ln_gain, w2_part, w1_first, w1_last, wout_part, sums, b1_part,
    )
    (
        w2_grad, w1_grad, wout_grad, wqkv_grad, gain_grad, shift_grad, out_bias_grad, b2_grad, b1_grad, qv_grad,
        tokens_grad, mixed,
    ) = finish(w2_grad, w1_grad, wout_grad, wqkv_grad, small, tokens_grad, mixed)
    return (
        mixed, tokens_grad, wqkv_grad.transpose(1, 0, 2), qv_grad, wout_grad, out_bias_grad[0], w1_grad, b1_grad[0],
        w2_grad, b2_grad[0], gain_grad, shift_grad,
    )


def solution(mesh):
    rows = P(("dp", "mp"), None)
    placed = (
        rows, P("dp", None), P("dp"), P(None, None, "mp"), P(None, "mp"), P("mp", None), P(), P(None, "mp"),
        P("mp"), P("mp", None), P(), P(), P(), rows,
    )
    return jax.shard_map(
        shards,
        mesh=mesh,
        in_specs=placed,
        out_specs=(
            rows, rows, P(None, None, "mp"), P(None, "mp"), P("mp", None), P(), P(None, "mp"), P("mp"),
            P("mp", None), P(), P(), P(),
        ),
        check_vma=False,
    )
```

```python
import functools
import jax, jax.numpy as jnp
from jax import lax
from jax.experimental import pallas as pl
from jax.experimental.pallas import tpu as pltpu
from jax.sharding import PartitionSpec as P
HEAD=64; IMG=1024; CAP_MIN=5; LANES=128
F32=jnp.float32; BF=jnp.bfloat16
MESH=pl.DeviceIdType.MESH
NT=(((1,),(1,)),((),()))
TN=(((0,),(0,)),((),()))

def plan(seq):
    least=IMG+CAP_MIN
    slack=seq-2*least
    lo=least//LANES*LANES
    hi=-(-(seq-least)//LANES)*LANES
    head_pad=-(-slack//LANES)*LANES
    tail_pad=(2*least)//LANES*LANES
    def cut(a,b,step):
        out=[]
        while a<b:
            out.append((a,min(a+step,b))); a=min(a+step,b)
        return out
    return lo,hi,head_pad,tail_pad,cut

def free_of_mask(k0,k1,q0,q1,seq):
    lo,hi,head_pad,tail_pad,_=plan(seq)
    if k1>q0: return False
    if q1<=lo: return k0>=head_pad
    if q0>=hi: return k0>=hi and q1<=tail_pad
    return False

def seg_start(pos,b0,b1,b2):
    return jnp.where(pos>=b2,b2,jnp.where(pos>=b1,b1,jnp.where(pos>=b0,b0,0)))

def fwd_kernel(bounds,q_ref,k_ref,v_ref,o_ref,lse_ref):
    seq,width=q_ref.shape
    h=pl.program_id(0)
    b0,b1,b2=bounds[0],bounds[1],bounds[2]
    lo,hi,_,_,cut=plan(seq)
    lane=lax.broadcasted_iota(jnp.int32,(1,width),1)
    mine=(lane//HEAD)==h
    blocks=[(a,b,0) for a,b in cut(0,lo,256)]+[(a,b,0) for a,b in cut(lo,hi,256)]+[(a,b,lo) for a,b in cut(hi,seq,256)]
    for a,b,start in blocks:
        n=b-a
        qm=jnp.where(mine,q_ref[a:b,:].astype(F32)*HEAD**-0.5,0.0).astype(BF)
        qpos=a+lax.broadcasted_iota(jnp.int32,(n,1),0)
        first=seg_start(qpos,b0,b1,b2)
        parts=[]
        top=None
        for c,d in cut(start,b,128):
            s=lax.dot_general(qm,k_ref[c:d,:],NT,preferred_element_type=F32)
            if not free_of_mask(c,d,a,b,seq):
                kpos=c+lax.broadcasted_iota(jnp.int32,(n,d-c),1)
                s=jnp.where((kpos>=first)&(kpos<=qpos),s,-1e9)
            parts.append(s)
            top=s if top is None else jnp.maximum(top,s)
        m=jnp.max(top,axis=1,keepdims=True)
        es=[jnp.exp(s-m) for s in parts]
        tot=es[0]
        for e in es[1:]: tot=tot+e
        l=jnp.sum(tot,axis=1,keepdims=True)
        p=jnp.concatenate([e.astype(BF) for e in es],axis=1)
        o=jnp.dot(p,v_ref[start:b,:],preferred_element_type=F32)/l
        o_ref[a:b,:]=jnp.where(mine,o.astype(BF),o_ref[a:b,:])
        lse=m+jnp.log(l)
        lse_ref[0,:,a:b]=jnp.broadcast_to(lse,(n,128)).T[0:8,:]

def bwd_kernel(bounds,q_ref,k_ref,v_ref,o_ref,do_ref,lse_ref,dq_ref,dk_ref,dv_ref,qm_s,dom_s,dqt_s,delta_s):
    seq,width=q_ref.shape
    h=pl.program_id(0)
    b0,b1,b2=bounds[0],bounds[1],bounds[2]
    lo,hi,_,_,cut=plan(seq)
    lane=lax.broadcasted_iota(jnp.int32,(1,width),1)
    mine=(lane//HEAD)==h
    qm_s[...]=jnp.where(mine,q_ref[...].astype(F32)*HEAD**-0.5,0.0).astype(BF)
    dom_s[...]=jnp.where(mine,do_ref[...],jnp.zeros((),BF))
    ones=jnp.ones((8,width),F32)
    for a,b in cut(0,seq,256):
        prod=dom_s[a:b,:].astype(F32)*o_ref[a:b,:].astype(F32)
        delta_s[:,a:b]=lax.dot_general(ones,prod,NT,preferred_element_type=F32,precision=lax.Precision.HIGHEST)
    dqt_s[...]=jnp.zeros_like(dqt_s)
    blocks=[(a,b,hi) for a,b in cut(0,lo,256)]+[(a,b,seq) for a,b in cut(lo,hi,256)]+[(a,b,seq) for a,b in cut(hi,seq,256)]
    for a,b,stop in blocks:
        n=b-a
        kk=k_ref[a:b,:]; vv=v_ref[a:b,:]
        kpos=a+lax.broadcasted_iota(jnp.int32,(n,1),0)
        kh=jnp.where(mine,kk,jnp.zeros((),BF))
        pts=[];dsts=[]
        for c,d in cut(a,stop,128):
            st=lax.dot_general(kk,qm_s[c:d,:],NT,preferred_element_type=F32)
            pt=jnp.exp(st-lse_ref[0,0:1,c:d])
            if not free_of_mask(a,b,c,d,seq):
                qpos=c+lax.broadcasted_iota(jnp.int32,(1,d-c),1)
                first=seg_start(qpos,b0,b1,b2)
                pt=jnp.where((kpos>=first)&(kpos<=qpos),pt,0.0)
            dpt=lax.dot_general(vv,dom_s[c:d,:],NT,preferred_element_type=F32)
            dst=pt*(dpt-delta_s[0:1,c:d])
            pts.append(pt.astype(BF)); dsts.append(dst.astype(BF))
        pt=jnp.concatenate(pts,axis=1); dst=jnp.concatenate(dsts,axis=1)
        dv=jnp.dot(pt,dom_s[a:stop,:],preferred_element_type=F32)
        dk=jnp.dot(dst,qm_s[a:stop,:],preferred_element_type=F32)
        dv_ref[a:b,:]=jnp.where(mine,dv.astype(BF),dv_ref[a:b,:])
        dk_ref[a:b,:]=jnp.where(mine,dk.astype(BF),dk_ref[a:b,:])
        dqt_s[:,a:stop]+=lax.dot_general(kh,dst,TN,preferred_element_type=F32)
    for a,b in cut(0,seq,128):
        dq=(dqt_s[:,a:b]*HEAD**-0.5).T
        dq_ref[a:b,:]=jnp.where(mine,dq.astype(BF),dq_ref[a:b,:])

def attn_fwd(bounds,q,k,v):
    seq,width=q.shape; H=width//HEAD
    full=pl.BlockSpec((seq,width),lambda h:(0,0))
    return pl.pallas_call(fwd_kernel,grid=(H,),
        in_specs=[pl.BlockSpec(memory_space=pltpu.SMEM),full,full,full],
        out_specs=[full,pl.BlockSpec((1,8,seq),lambda h:(h,0,0))],
        out_shape=[jax.ShapeDtypeStruct((seq,width),BF),jax.ShapeDtypeStruct((H,8,seq),F32)],
        compiler_params=pltpu.CompilerParams(vmem_limit_bytes=56<<20),name="attn_fwd")(bounds,q,k,v)

def attn_bwd(bounds,q,k,v,o,do,lse):
    seq,width=q.shape; H=width//HEAD
    full=pl.BlockSpec((seq,width),lambda h:(0,0))
    sh=jax.ShapeDtypeStruct((seq,width),BF)
    return pl.pallas_call(bwd_kernel,grid=(H,),
        in_specs=[pl.BlockSpec(memory_space=pltpu.SMEM),full,full,full,full,full,pl.BlockSpec((1,8,seq),lambda h:(h,0,0))],
        out_specs=[full,full,full],out_shape=[sh,sh,sh],
        scratch_shapes=[pltpu.VMEM((seq,width),BF),pltpu.VMEM((seq,width),BF),pltpu.VMEM((width,seq),F32),pltpu.VMEM((8,seq),F32)],
        compiler_params=pltpu.CompilerParams(vmem_limit_bytes=56<<20),name="attn_bwd")(bounds,q,k,v,o,do,lse)

eps_norm = 1e-05


def layer_norm(values, gain, shift):
    center = values - jnp.mean(values, axis=-1, keepdims=True)
    spread = jnp.mean(center * center, axis=-1, keepdims=True)
    return center * lax.rsqrt(spread + eps_norm) * gain + shift


def gelu_tanh(values):
    return jax.nn.gelu(values, approximate=True)


def swap(values, axis, mask):
    size = lax.axis_size(axis)
    return lax.ppermute(values, axis, [(i, i ^ mask) for i in range(size)])


def masks_of(axis):
    size = lax.axis_size(axis)
    out = []
    step = size // 2
    while step:
        out.append(step)
        step //= 2
    return out


def gather_rel(block, axis):
    have = {0: block}
    for mask in masks_of(axis):
        have.update({j ^ mask: swap(v, axis, mask) for j, v in list(have.items())})
    return jnp.stack([have[j] for j in range(lax.axis_size(axis))])


def scatter_rel(parts, axis):
    have = {j: parts[j] for j in range(parts.shape[0])}
    for mask in reversed(masks_of(axis)):
        got = {j: swap(have[j].astype(BF), axis, mask) for j in have if j & mask}
        have = {j: have[j] + got[j ^ mask].astype(F32) for j in have if not j & mask}
    return have[0]


def reduce_all(values, axis):
    me = lax.axis_index(axis)
    masks = list(reversed(masks_of(axis)))
    rows = values.shape[0]
    for mask in masks:
        rows //= 2
        bit = (me // mask) % 2
        keep = lax.dynamic_slice_in_dim(values, bit * rows, rows, 0)
        send = lax.dynamic_slice_in_dim(values, (1 - bit) * rows, rows, 0)
        values = keep + swap(send.astype(BF), axis, mask).astype(F32)
    low = values.astype(BF)
    for mask in reversed(masks):
        bit = (me // mask) % 2
        got = swap(low, axis, mask)
        both = jnp.concatenate([low, got], axis=0)
        flipped = jnp.concatenate([got, low], axis=0)
        low = jnp.where(bit == 0, both, flipped)
    return low.astype(F32)


def sum_small(values, axes):
    for axis in axes:
        for mask in masks_of(axis):
            values = values + swap(values, axis, mask)
    return values


def shards_by_ops(
    tokens, caption_len, row_offset, wqkv, qv_bias, wout, out_bias, w1, b1, w2, b2, ln_gain, ln_bias, cotangent,
):
    local_rows, width = tokens.shape
    size = lax.axis_size("mp")
    seq_len = local_rows * size
    head_part = wqkv.shape[2]
    gains = ln_gain.astype(F32)
    shifts = ln_bias.astype(F32)
    me = lax.axis_index("mp")

    def pick(blocks):
        return jnp.concatenate(
            [lax.dynamic_index_in_dim(blocks, me ^ j, 0, keepdims=True) for j in range(size)], axis=0
        )

    first = row_offset[0]
    second = first + caption_len[0, 0] + IMG
    third = second + caption_len[0, 1] + IMG
    bounds = jnp.stack([first, second, third]).astype(jnp.int32)

    def sort(rel):
        return pick(rel).reshape((seq_len,) + rel.shape[2:])

    def rel_of(rows):
        return pick(rows.reshape((size, local_rows) + rows.shape[1:]))

    rows_in = tokens.astype(F32)
    norm_a, pull_a = jax.vjp(layer_norm, rows_in, gains[0], shifts[0])
    attn_full = sort(gather_rel(norm_a.astype(BF), "mp"))
    w_in = wqkv.reshape(width, 3 * head_part)
    projected = jnp.dot(attn_full, w_in, preferred_element_type=F32)
    bias3 = jnp.concatenate([qv_bias[0], jnp.zeros_like(qv_bias[0]), qv_bias[1]]).astype(F32)
    projected = (projected + bias3).astype(BF)
    queries, keys, values = [projected[:, i * head_part:(i + 1) * head_part] for i in range(3)]
    head_low, lse = attn_fwd(bounds, queries, keys, values)
    head_rel = rel_of(head_low)
    grad_out_all = cotangent.astype(F32)
    state = []
    for lo, hi in [(0, local_rows)]:
        rows = hi - lo
        total = size * rows
        attn_out = scatter_rel(
            jnp.dot(head_rel[:, lo:hi], wout, preferred_element_type=F32), "mp"
        ) + out_bias.astype(F32)
        norm_b, pull_b = jax.vjp(layer_norm, attn_out, gains[1], shifts[1])
        hidden_rows = rows_in[lo:hi] + norm_b
        norm_c, pull_c = jax.vjp(layer_norm, hidden_rows, gains[2], shifts[2])
        mlp_full = gather_rel(norm_c.astype(BF), "mp").reshape(total, width)
        pre_act = jnp.dot(mlp_full, w1, preferred_element_type=F32) + b1.astype(F32)
        activated, gelu_pull = jax.vjp(gelu_tanh, pre_act)
        act_low = activated.astype(BF)
        branch = scatter_rel(
            jnp.dot(act_low, w2, preferred_element_type=F32).reshape(size, rows, width), "mp"
        ) + b2.astype(F32)
        norm_d, pull_d = jax.vjp(layer_norm, branch, gains[3], shifts[3])
        mixed = (hidden_rows + norm_d).astype(BF)
        grad_out = grad_out_all[lo:hi]
        grad_branch, gain_d, shift_d = pull_d(grad_out)
        branch_low = grad_branch.astype(BF)
        b2_part = jnp.sum(branch_low.astype(F32), axis=0)
        branch_full = gather_rel(branch_low, "mp").reshape(total, width)
        grad_act = jnp.einsum("td,fd->tf", branch_full, w2, preferred_element_type=F32)
        grad_pre = gelu_pull(grad_act)[0].astype(BF)
        b1_part = jnp.sum(grad_pre.astype(F32), axis=0)
        grad_norm_c = scatter_rel(
            jnp.einsum("tf,df->td", grad_pre, w1, preferred_element_type=F32).reshape(size, rows, width), "mp"
        )
        grad_hidden_c, gain_c, shift_c = pull_c(grad_norm_c)
        grad_hidden = grad_out + grad_hidden_c
        grad_attn, gain_b, shift_b = pull_b(grad_hidden)
        attn_grad_low = grad_attn.astype(BF)
        out_bias_part = jnp.sum(attn_grad_low.astype(F32), axis=0)
        attn_grad_rel = gather_rel(attn_grad_low, "mp")
        state.append(dict(
            mixed=mixed, act=act_low, branch=branch_full, mlp=mlp_full, pre=grad_pre, hidden=grad_hidden,
            attn=attn_grad_rel, heads=head_rel[:, lo:hi].reshape(total, head_part),
            gh=jnp.einsum("jtd,cd->jtc", attn_grad_rel, wout, preferred_element_type=F32).astype(BF),
            sums=jnp.stack([gain_b, gain_c, gain_d, shift_b, shift_c, shift_d, out_bias_part, b2_part]),
            b1=b1_part,
        ))

    def joined(name, axis=0):
        return jnp.concatenate([s[name] for s in state], axis=axis)

    w2_grad = jnp.einsum("tf,td->fd", joined("act"), joined("branch"), preferred_element_type=F32)
    w2_grad = reduce_all(w2_grad, "dp")
    w1_grad = jnp.einsum("td,tf->df", joined("mlp"), joined("pre"), preferred_element_type=F32)
    w1_grad = reduce_all(w1_grad, "dp")
    attn_grad_full = joined("attn", 1).reshape(seq_len, width)
    wout_grad = jnp.einsum(
        "tc,td->cd", head_rel.reshape(seq_len, head_part), attn_grad_full, preferred_element_type=F32
    )
    wout_grad = reduce_all(wout_grad, "dp")
    grad_heads = sort(joined("gh", 1))
    mixed, grad_hidden = joined("mixed"), joined("hidden")
    mid_sums = sum(s["sums"] for s in state)
    b1_grad = sum(s["b1"] for s in state)
    grads = attn_bwd(bounds, queries, keys, values, head_low, grad_heads, lse)
    grad_proj = jnp.concatenate(grads, axis=1)
    part_sums = jnp.sum(grad_proj.astype(F32), axis=0).reshape(3, head_part)
    qv_part = jnp.stack([part_sums[0], part_sums[2]])
    wqkv_grad = jnp.einsum("td,tc->dc", attn_full, grad_proj, preferred_element_type=F32)
    wqkv_grad = reduce_all(wqkv_grad, "dp").reshape(width, 3, head_part)
    grad_rel = rel_of(grad_proj)
    grad_norm_a = scatter_rel(jnp.einsum("jtc,dc->jtd", grad_rel, w_in, preferred_element_type=F32), "mp")
    grad_rows_a, gain_a, shift_a = pull_a(grad_norm_a)
    tokens_grad = (grad_hidden + grad_rows_a).astype(BF)
    own_sums = sum_small(jnp.concatenate([qv_part.reshape(-1), b1_grad]), ("dp",))
    qv_sum = own_sums[: 2 * head_part].reshape(2, head_part)
    b1_sum = own_sums[2 * head_part:]
    stack = jnp.concatenate([gain_a[None], mid_sums[0:3], shift_a[None], mid_sums[3:8]])
    stack = sum_small(stack, ("mp", "dp"))
    return (
        mixed, tokens_grad, wqkv_grad, qv_sum, wout_grad, stack[8], w1_grad, b1_sum, w2_grad, stack[9],
        stack[0:4], stack[4:8],
    )


SLOT = {1: 0, 3: 1, 2: 2, 0: 3}
TILE = 256
AHEAD = 2


def spans_of(rows):
    units = rows // 16
    sizes = [16 * (units // 4 + (1 if i < units % 4 else 0)) for i in range(4)]
    edges = [sum(sizes[:i]) for i in range(5)]
    return [(edges[i], edges[i + 1]) for i in range(4)]


def fold8(values):
    rows, cols = values.shape
    return jnp.sum(values.reshape(rows // 8, 8, cols), axis=0)


def norm_stats(values):
    center = values - jnp.mean(values, axis=-1, keepdims=True)
    inv = lax.rsqrt(jnp.mean(center * center, axis=-1, keepdims=True) + eps_norm)
    return center * inv, inv


def norm_pull(upstream, gain, unit, inv):
    scaled = upstream * gain
    first = jnp.mean(scaled, axis=-1, keepdims=True)
    second = jnp.mean(scaled * unit, axis=-1, keepdims=True)
    return (scaled - first - unit * second) * inv


def dp_place():
    dp, me = lax.axis_index("dp"), lax.axis_index("mp")
    y, low, high = dp % 2, dp // 2 % 2, dp // 4
    return (y, low, high), (
        (dp + 1 - 2 * y, me), (dp + 2 * (1 - 2 * low), me), (dp + 4 * (1 - 2 * high), me)
    )


def by_rows(count, body):
    step = next(t for t in (64, 48, 32, 16) if count % t == 0)

    def trip(i, carry):
        body(pl.multiple_of(i * step, 16), step)
        return carry

    lax.fori_loop(0, count // step, trip, 0)


class Reduction:
    def __init__(self, rows, work, first, held, sbuf, rbuf, full, send, recv, base, order=(0, 1, 2)):
        self.rows, self.work, self.first, self.held, self.full = rows, work, first, held, full
        self.sbuf, self.rbuf, self.send, self.recv, self.base = sbuf, rbuf, send, recv, base
        bits, peers = dp_place()
        self.bits, self.peers = [bits[i] for i in order], [peers[i] for i in order]
        off = [0]
        for k in range(3):
            off.append(off[-1] + self.bits[k] * (rows >> (k + 1)))
        self.off = off
        self.steps = 6

    def copy(self, i):
        if i < 3:
            src, dst, peer = self.sbuf[i], self.rbuf[i], self.peers[i]
        else:
            k = 5 - i
            part = self.full.at[pl.ds(pl.multiple_of(self.off[k + 1], 16), self.rows >> (k + 1))]
            src, dst, peer = part, part, self.peers[k]
        return pltpu.make_async_remote_copy(
            src_ref=src, dst_ref=dst, send_sem=self.send.at[self.base + i], recv_sem=self.recv.at[self.base + i],
            device_id=peer, device_id_type=MESH,
        )

    def copies(self, i):
        return (self.copy(i),)

    def arrive(self, i):
        for copy in self.copies(i):
            copy.wait_recv()

    def leave(self, i):
        for copy in self.copies(i):
            copy.wait_send()

    def depart(self, i):
        for copy in self.copies(i):
            copy.start()

    def at(self, offset, i, step):
        return pl.ds(pl.multiple_of(offset + i - self.off[self.held], 16), step)

    def halve(self, k):
        n = self.rows >> (k + 1)
        bit = self.bits[k]
        give, keep = self.off[k] + (1 - bit) * n, self.off[k] + bit * n
        fresh = k == self.first

        def out(i, step):
            value = self.work[self.at(give, i, step), :]
            if not fresh:
                value = value + self.rbuf[k - 1][pl.ds(pl.multiple_of((1 - bit) * n + i, 16), step), :].astype(F32)
            self.sbuf[k][pl.ds(i, step), :] = value.astype(BF)

        def stay(i, step):
            rows = self.at(keep, i, step)
            self.work[rows, :] += self.rbuf[k - 1][pl.ds(pl.multiple_of(bit * n + i, 16), step), :].astype(F32)

        by_rows(n, out)
        self.depart(k)
        if not fresh:
            by_rows(n, stay)

    def settle(self, dst, at):
        def body(i, step):
            value = self.work[self.at(self.off[3], i, step), :] + self.rbuf[2][pl.ds(i, step), :].astype(F32)
            dst[pl.ds(pl.multiple_of(at + i, 16), step), :] = value.astype(dst.dtype)

        by_rows(self.rows >> 3, body)

    def step(self, i):
        if i > self.first:
            self.arrive(i - 1)
        if i < 3:
            self.halve(i)
        else:
            if i == 3:
                self.settle(self.full, self.off[3])
            self.depart(i)

    def drain(self):
        for i in range(self.first, self.steps):
            self.leave(i)


class Direct(Reduction):
    def __init__(self, rows, work, sbuf, rbuf, full, send, recv, base):
        super().__init__(rows, work, 0, 0, sbuf, rbuf, full, send, recv, base)
        self.steps = 4
        self.z = lax.axis_index("dp") // 2
        self.y = lax.axis_index("dp") % 2

    def copies(self, i):
        me = lax.axis_index("mp")
        n = self.rows >> 3
        half = pl.ds(pl.multiple_of(self.off[1], 16), 4 * n)
        if i in (0, 3):
            part = self.full.at[half]
            pairs = [(self.sbuf[0], self.rbuf[0], self.peers[0])] if i == 0 else [(part, part, self.peers[0])]
        else:
            pairs = []
            own = self.full.at[pl.ds(pl.multiple_of(self.off[1] + self.z * n, 16), n)]
            for j in range(1, 4):
                there = (self.z + j) % 4
                peer = (2 * there + self.y, me)
                if i == 1:
                    src = self.sbuf[1].at[pl.ds(pl.multiple_of(there * n, 16), n)]
                    pairs.append((src, self.rbuf[1].at[pl.ds((j - 1) * n, n)], peer))
                else:
                    pairs.append((own, own, peer))
        first = self.base + (0, 1, 4, 7)[i]
        return [
            pltpu.make_async_remote_copy(
                src_ref=src, dst_ref=dst, send_sem=self.send.at[first + j], recv_sem=self.recv.at[first + j],
                device_id=peer, device_id_type=MESH,
            )
            for j, (src, dst, peer) in enumerate(pairs)
        ]

    def step(self, i):
        n = self.rows >> 3
        if i:
            self.arrive(i - 1)
        if i == 0:
            self.halve(0)
            return
        if i == 1:

            def spread(k, step):
                rows = self.at(self.off[1], k, step)
                value = self.work[rows, :] + self.rbuf[0][pl.ds(k, step), :].astype(F32)
                self.work[rows, :] = value
                self.sbuf[1][pl.ds(k, step), :] = value.astype(BF)

            by_rows(4 * n, spread)
        elif i == 2:

            def body(k, step):
                at = self.off[1] + self.z * n
                value = self.work[self.at(at, k, step), :]
                for j in range(3):
                    value = value + self.rbuf[1][pl.ds(pl.multiple_of(j * n + k, 16), step), :].astype(F32)
                self.full[pl.ds(pl.multiple_of(at + k, 16), step), :] = value.astype(BF)

            by_rows(n, body)
        self.depart(i)


def edges(lengths, offset):
    first = offset[0]
    second = first + lengths[0, 0] + IMG
    return first, second, second + lengths[0, 1] + IMG


def ahead_kernel(
    lengths, offset, tokens, cot, w3, wout, w1, w2, biases, ln_gain, ln_bias, qv_bias,
    xfull, qkv, heads, lse, mixed, ghid, ghead, w2q, w1p, w1q, wog, sums, b1sum,
    vec, b1, mlp, act, dgel, brn, gpre, u1, u2, hid, r1, pbuf, cs, cr, xs, xr, acc, b1acc,
    qkeep, s2y, r2y, r2z, rpy, rqz, rqw, send, recv, dsend, drecv, local_sem,
):
    local, width = tokens.shape
    seq, part = heads.shape
    hidden_units = w1.shape[1]
    spans = spans_of(local)
    count = len(spans)
    dp, me = lax.axis_index("dp"), lax.axis_index("mp")
    mx, mc = me // 2, me % 2
    peer_core = (dp, mx * 2 + 1 - mc)
    peer_x = (dp, (1 - mx) * 2 + mc)
    owner = {0: me, 1: mx * 2 + 1 - mc, 2: (1 - mx) * 2 + mc, 3: (1 - mx) * 2 + 1 - mc}

    barrier = pltpu.get_barrier_semaphore()
    bits, dp_peers = dp_place()
    for peer in (peer_core, peer_x) + dp_peers:
        pl.semaphore_signal(barrier, inc=1, device_id=peer, device_id_type=MESH)
    pl.semaphore_wait(barrier, 5)

    def remote(src, dst, phase, kind, c, device):
        i = (phase * 5 + kind) * count + c
        return pltpu.make_async_remote_copy(
            src_ref=src, dst_ref=dst, send_sem=send.at[i], recv_sem=recv.at[i], device_id=device, device_id_type=MESH
        )

    def core_copy(phase, c):
        lo, hi = spans[c]
        rows = pl.ds(2 * lo, 2 * (hi - lo))
        return remote(cs.at[rows], cr.at[rows], phase, 0, c, peer_core)

    def x_copy(phase, c):
        lo, hi = spans[c]
        rows = pl.ds(lo, hi - lo)
        return remote(xs.at[rows], xr.at[rows], phase, 1, c, peer_x)

    def block(c, j):
        lo, hi = spans[c]
        return pl.ds(4 * lo + SLOT[j] * (hi - lo), hi - lo)

    def gather_copies(full, phase, c):
        own = full.at[block(c, 0)]
        return (
            remote(own, full.at[block(c, 2)], phase, 2, c, peer_x),
            remote(own, full.at[block(c, 1)], phase, 3, c, peer_core),
            remote(full.at[block(c, 2)], full.at[block(c, 3)], phase, 4, c, peer_core),
        )

    def tiles(c):
        lo, hi = spans[c]
        step = next(t for t in (48, 64, 32, 16) if (hi - lo) % t == 0)
        return (hi - lo) // step, step

    def start_gather(full, phase, c):
        first, second, _ = gather_copies(full, phase, c)
        first.start()
        second.start()

    def forward(full, phase, c):
        first, second, third = gather_copies(full, phase, c)
        first.wait_recv()
        third.start()
        second.wait_recv()
        third.wait_recv()

    def partial_products(lhs, rhs, turned, phase, c, half, wide=TILE):
        lo, hi = spans[c]
        r = hi - lo
        rows = pl.ds(4 * lo + half * 2 * r, 2 * r)
        out = pl.ds(2 * lo, 2 * r)

        def body(n, carry):
            cols = pl.ds(pl.multiple_of(n * wide, wide), wide)
            if turned:
                value = lax.dot_general(lhs[rows, :], rhs[cols, :], NT, preferred_element_type=F32)
            else:
                value = jnp.dot(lhs[rows, 0:rhs.shape[0]], rhs[:, cols], preferred_element_type=F32)
            if half == 0:
                cs[out, cols] = value.astype(BF)
            else:
                pbuf[out, cols] = value
            return carry

        lax.fori_loop(0, width // wide, body, 0)

    def pass_on(phase, c):
        lo, hi = spans[c]
        r = hi - lo
        core_copy(phase, c).wait_recv()
        if phase:
            x_copy(phase - 1, c).wait_send()
        xs[lo:hi, :] = (pbuf[2 * lo:2 * lo + r, :] + cr[2 * lo + r:2 * lo + 2 * r, :].astype(F32)).astype(BF)
        x_copy(phase, c).start()

    def own_total(c, i, step):
        lo, hi = spans[c]
        r = hi - lo
        kept = pl.ds(pl.multiple_of(2 * lo + r + i * step, 16), step)
        near = pl.ds(pl.multiple_of(2 * lo + i * step, 16), step)
        far = pl.ds(pl.multiple_of(lo + i * step, 16), step)
        return far, pbuf[kept, :] + cr[near, :].astype(F32) + xr[far, :].astype(F32)

    def row(i):
        return vec[i:i + 1, :]

    wide_biases = biases[...].astype(F32)
    vec[0:2, :] = wide_biases[0:2, :]
    gain, shift = ln_gain[...].astype(F32), ln_bias[...].astype(F32)
    for i in range(4):
        at = 2 * i if i else 8
        vec[at:at + 1, :] = gain[i:i + 1, :]
        vec[at + 1:at + 2, :] = shift[i:i + 1, :]
    b1[...] = wide_biases[2:3, :]
    bias = qv_bias[...].astype(F32)
    acc[...] = jnp.zeros_like(acc)
    b1acc[...] = jnp.zeros_like(b1acc)

    def add(i, values):
        acc[8 * i:8 * i + 8, :] += fold8(values)

    def project(c):
        lo, hi = spans[c]
        for j in (1, 3, 2, 0):
            start = pl.multiple_of(owner[j] * local + lo, 16)
            mlp[block(c, j), 0:part] = heads[pl.ds(start, hi - lo), :]
        partial_products(mlp, wout, False, 0, c, 0)
        core_copy(0, c).start()
        partial_products(mlp, wout, False, 0, c, 1)

    xf = gpre

    def place(j, c):
        lo, hi = spans[c]
        return pl.ds(pl.multiple_of(owner[j] * local + lo, 16), hi - lo)

    def first_copies(c):
        own, across = xf.at[place(0, c)], xf.at[place(2, c)]
        return (
            remote(own, own, 3, 2, c, peer_x),
            remote(own, own, 3, 3, c, peer_core),
            remote(across, across, 3, 4, c, peer_core),
        )

    for c in range(count):
        lo, hi = spans[c]
        trips, step = tiles(c)

        def first_norm(i, carry):
            rows = pl.ds(pl.multiple_of(lo + i * step, 16), step)
            unit, _ = norm_stats(tokens[rows, :].astype(F32))
            dst = pl.ds(pl.multiple_of(me * local + lo + i * step, 16), step)
            xf[dst, :] = (unit * row(8) + row(9)).astype(BF)
            return carry

        lax.fori_loop(0, trips, first_norm, 0)
        for copy in first_copies(c)[:2]:
            copy.start()

    def projections(rows):
        for t in range(3):
            value = jnp.dot(xf[rows, :], w3[t], preferred_element_type=F32)
            if t != 1:
                value = value + bias[t // 2:t // 2 + 1, :]
            act[rows, t * part:(t + 1) * part] = value.astype(BF)

    projections(pl.ds(pl.multiple_of(owner[0] * local, 16), local))
    for c in range(count):
        first_copies(c)[1].wait_recv()
    projections(pl.ds(pl.multiple_of(owner[1] * local, 16), local))
    for c in range(count):
        first_copies(c)[0].wait_recv()
        first_copies(c)[2].start()
        projections(place(2, c))
        if c:
            first_copies(c - 1)[2].wait_recv()
            projections(place(3, c - 1))
    first_copies(count - 1)[2].wait_recv()
    projections(place(3, count - 1))
    keep_x = pltpu.make_async_copy(xf, xfull, local_sem.at[0])
    keep_qkv = pltpu.make_async_copy(act.at[:, 0:3 * part], qkv, local_sem.at[1])
    keep_x.start()
    keep_qkv.start()

    edge0, edge1, edge2 = edges(lengths, offset)
    lo_edge, hi_edge, _, _, cuts = plan(seq)
    pair = 2 * HEAD
    lane = lax.broadcasted_iota(jnp.int32, (1, pair), 1)

    def attend(c):
        lo, hi = spans[c]
        n = hi - lo

        def one_head(h, carry):
            mine = (lane // HEAD) == h % 2
            shift = h // 2 * pair
            qcols, kcols, vcols = (
                pl.ds(pl.multiple_of(t * part + shift, pair), pair) for t in range(3)
            )
            for o in range(4):
                a = o * local + lo
                b = a + n
                start = 0 if a < hi_edge else lo_edge
                stop = -(-b // LANES) * LANES
                qm = jnp.where(mine, act[a:b, qcols].astype(F32) * HEAD**-0.5, 0.0).astype(BF)
                qpos = a + lax.broadcasted_iota(jnp.int32, (n, 1), 0)
                first = seg_start(qpos, edge0, edge1, edge2)
                parts, top = [], None
                for k0, k1 in cuts(start, stop, LANES):
                    s = lax.dot_general(qm, act[k0:k1, kcols], NT, preferred_element_type=F32)
                    if not free_of_mask(k0, k1, a, b, seq):
                        kpos = k0 + lax.broadcasted_iota(jnp.int32, (n, k1 - k0), 1)
                        s = jnp.where((kpos >= first) & (kpos <= qpos), s, -1e9)
                    parts.append(s)
                    top = s if top is None else jnp.maximum(top, s)
                m = jnp.max(top, axis=1, keepdims=True)
                es = [jnp.exp(s - m) for s in parts]
                tot = es[0]
                for e in es[1:]:
                    tot = tot + e
                l = jnp.sum(tot, axis=1, keepdims=True)
                p = jnp.concatenate([e.astype(BF) for e in es], axis=1)
                out = jnp.dot(p, act[start:stop, vcols], preferred_element_type=F32) / l
                hcols = pl.ds(pl.multiple_of(shift, pair), pair)
                heads[a:b, hcols] = jnp.where(mine, out.astype(BF), heads[a:b, hcols])
                log_total = m + jnp.log(l)
                which = lax.broadcasted_iota(jnp.int32, (1, LANES), 1) == h
                at = slice(o * LANES, (o + 1) * LANES)
                ghid[lo:hi, at] = jnp.where(which, log_total, ghid[lo:hi, at])
            return carry

        lax.fori_loop(0, part // HEAD, one_head, 0)

    def two_norms(c):
        x_copy(0, c).wait_recv()
        lo, hi = spans[c]
        trips, step = tiles(c)

        def norms(i, carry):
            rows, total = own_total(c, i, step)
            unit, inv = norm_stats(total + row(0))
            u1[rows, :] = unit
            r1[rows, 0:HEAD] = jnp.broadcast_to(inv, (step, HEAD))
            hidden = tokens[rows, :].astype(F32) + unit * row(2) + row(3)
            hid[rows, :] = hidden
            unit, inv = norm_stats(hidden)
            u2[rows, :] = unit
            r1[rows, HEAD:LANES] = jnp.broadcast_to(inv, (step, HEAD))
            dst = pl.ds(pl.multiple_of(4 * lo + SLOT[0] * (hi - lo) + i * step, 16), step)
            mlp[dst, :] = (unit * row(4) + row(5)).astype(BF)
            return carry

        lax.fori_loop(0, trips, norms, 0)
        start_gather(mlp, 0, c)

    for c in range(count):
        attend(c)
        project(c)
        pass_on(0, c)
        if c >= AHEAD:
            two_norms(c - AHEAD)
    for c in range(count - AHEAD, count):
        two_norms(c)
    keep_lse = [
        pltpu.make_async_copy(ghid.at[:, o * LANES:(o + 1) * LANES], lse.at[o], local_sem.at[2 + o]) for o in range(4)
    ]
    for copy in keep_lse:
        copy.start()
    for copy in [keep_qkv, keep_x] + keep_lse:
        copy.wait()
    for c in range(count):
        for copy in first_copies(c):
            copy.wait_send()

    for c in range(count):
        lo, hi = spans[c]
        r = hi - lo
        forward(mlp, 0, c)
        core_copy(0, c).wait_send()
        for half in range(2):
            rows = pl.ds(4 * lo + half * 2 * r, 2 * r)

            def units(n, carry):
                cols = pl.ds(pl.multiple_of(n * TILE, TILE), TILE)
                pre = jnp.dot(mlp[rows, :], w1[:, cols], preferred_element_type=F32) + b1[:, cols]
                square = pre * pre
                inner = (0.7978845608028654 * pre) * (1.0 + 0.044715 * square)
                tanh = jnp.tanh(inner)
                plus = 0.5 * (1.0 + tanh)
                act[rows, cols] = (pre * plus).astype(BF)
                slope = plus + (0.5 * pre) * (1.0 - tanh * tanh) * (
                    0.7978845608028654 * (1.0 + (3 * 0.044715) * square)
                )
                dgel[rows, cols] = slope.astype(BF)
                return carry

            lax.fori_loop(0, hidden_units // TILE, units, 0)
            partial_products(act, w2, False, 1, c, half)
            if half == 0:
                core_copy(1, c).start()
        pass_on(1, c)

    for c in range(count):
        x_copy(1, c).wait_recv()
        lo, hi = spans[c]
        trips, step = tiles(c)

        def last(i, carry):
            rows, total = own_total(c, i, step)
            unit, inv = norm_stats(total + row(1))
            mixed[rows, :] = (hid[rows, :] + unit * row(6) + row(7)).astype(BF)
            grad = cot[rows, :].astype(F32)
            add(2, grad * unit)
            add(5, grad)
            low = norm_pull(grad, row(6), unit, inv).astype(BF)
            add(7, low.astype(F32))
            dst = pl.ds(pl.multiple_of(4 * lo + SLOT[0] * (hi - lo) + i * step, 16), step)
            brn[dst, :] = low
            return carry

        lax.fori_loop(0, trips, last, 0)
        start_gather(brn, 1, c)

    sum2 = Reduction(hidden_units, hid, 0, 1, (s2y, act.at[512:768]), (r2y, r2z), None, dsend, drecv, 0)
    sump = Reduction(width // 2, w1p, 0, 1, (act.at[0:256],), (rpy,), None, dsend, drecv, 2)
    sumq = Reduction(
        width // 2, qkeep, 0, 1, (act.at[256:512], act.at[768:896]), (rqz, rqw), None, dsend, drecv, 3,
        order=(1, 2, 0),
    )

    def weight_grad(lhs, rhs, first, rows, dst):
        for n in range(rows // TILE):
            cols = pl.ds(pl.multiple_of(first + n * TILE, TILE), TILE)
            value = lax.dot_general(lhs[:, cols], rhs[...], TN, preferred_element_type=F32)
            dst[n * TILE:(n + 1) * TILE, :] = value.astype(dst.dtype)

    half2, half1 = hidden_units // 2, width // 4

    for c in range(count):
        lo, hi = spans[c]
        r = hi - lo
        forward(brn, 1, c)
        if c == count - 1:
            weight_grad(act, brn, (1 - sum2.bits[0]) * half2, half2, s2y)
            sum2.depart(0)
        core_copy(1, c).wait_send()
        for half in range(2):
            rows = pl.ds(4 * lo + half * 2 * r, 2 * r)

            def slopes(n, carry):
                cols = pl.ds(pl.multiple_of(n * TILE, TILE), TILE)
                grad = lax.dot_general(brn[rows, :], w2[cols, :], NT, preferred_element_type=F32)
                low = (grad * dgel[rows, cols].astype(F32)).astype(BF)
                gpre[rows, cols] = low
                b1acc[:, cols] += fold8(low.astype(F32))
                return carry

            lax.fori_loop(0, hidden_units // TILE, slopes, 0)
            partial_products(gpre, w1, True, 2, c, half)
            if half == 0:
                core_copy(2, c).start()
        pass_on(2, c)

    weight_grad(act, brn, sum2.bits[0] * half2, half2, hid)

    for c in range(count):
        x_copy(2, c).wait_recv()
        lo, hi = spans[c]
        trips, step = tiles(c)

        def pulls(i, carry):
            rows, total = own_total(c, i, step)
            unit = u2[rows, :]
            add(1, total * unit)
            add(4, total)
            grad = cot[rows, :].astype(F32) + norm_pull(total, row(4), unit, r1[rows, HEAD:HEAD + 1])
            ghid[rows, :] = grad
            unit = u1[rows, :]
            add(0, grad * unit)
            add(3, grad)
            low = norm_pull(grad, row(2), unit, r1[rows, 0:1]).astype(BF)
            add(6, low.astype(F32))
            dst = pl.ds(pl.multiple_of(4 * lo + SLOT[0] * (hi - lo) + i * step, 16), step)
            dgel[dst, :] = low
            return carry

        lax.fori_loop(0, trips, pulls, 0)
        start_gather(dgel, 2, c)
        if c == 0:
            weight_grad(mlp, gpre, (1 - sump.bits[0]) * half1, half1, act)
            sump.depart(0)
            weight_grad(mlp, gpre, width // 2 + (1 - sumq.bits[0]) * half1, half1, act.at[256:512])
            sumq.depart(0)
        elif c == 2:
            weight_grad(mlp, gpre, width // 2 + sumq.bits[0] * half1, half1, qkeep)

    sum2.step(1)
    weight_grad(mlp, gpre, sump.bits[0] * half1, half1, w1p)
    for c in range(count):
        for copy in gather_copies(brn, 1, c):
            copy.wait_send()
    def finish_sum(stream, last, work, got, dst):
        stream.arrive(last)

        def join(i, step):
            rows = stream.at(stream.off[last + 1], i, step)
            dst[pl.ds(i, step), :] = work[rows, :] + got[pl.ds(i, step), :].astype(F32)

        by_rows(stream.rows >> (last + 1), join)
        for i in range(last + 1):
            stream.leave(i)

    for c in range(count):
        lo, hi = spans[c]
        if c == count - 1:
            finish_sum(sump, 0, w1p, rpy, w1p)
            for i in range(8):
                sums[i:i + 1, :] = jnp.sum(acc[8 * i:8 * i + 8, :], axis=0, keepdims=True)
            b1sum[...] = jnp.sum(b1acc[...], axis=0, keepdims=True)
        forward(dgel, 2, c)
        for j in (1, 3, 2, 0):
            start = pl.multiple_of(owner[j] * local + lo, 16)
            brn[block(c, j), 0:part] = heads[pl.ds(start, hi - lo), :]
            ghead[pl.ds(start, hi - lo), :] = lax.dot_general(
                dgel[block(c, j), :], wout[...], NT, preferred_element_type=F32
            ).astype(BF)
        rows = pl.ds(4 * lo, 4 * (hi - lo))
        share = lax.dot_general(brn[rows, 0:part], dgel[rows, :], TN, preferred_element_type=F32)
        wog[...] = wog[...] + share if c else share
        if c == 0:
            sumq.step(1)
    for stream, last, work, got, dst in ((sum2, 1, hid, r2z, w2q), (sumq, 1, qkeep, rqw, w1q)):
        finish_sum(stream, last, work, got, dst)


    for c in range(count):
        core_copy(2, c).wait_send()
        x_copy(2, c).wait_send()
        for phase, full in ((0, mlp), (2, dgel)):
            for copy in gather_copies(full, phase, c):
                copy.wait_send()


def ahead(lengths, offset, tokens, cot, w3, wout, w1, w2, biases, ln_gain, ln_bias, qv_bias):
    local, width = tokens.shape
    seq = 4 * local
    part = w3.shape[2]
    units = w1.shape[1]
    vmem = pl.BlockSpec(memory_space=pltpu.VMEM)
    any_spec = pl.BlockSpec(memory_space=pl.ANY)
    shape = jax.ShapeDtypeStruct
    copies = 20 * 4
    low = lambda *dims: pltpu.VMEM(dims, BF)
    wide = lambda *dims: pltpu.VMEM(dims, F32)
    dma = lambda n: pltpu.SemaphoreType.DMA((n,))
    return pl.pallas_call(
        ahead_kernel,
        in_specs=[pl.BlockSpec(memory_space=pltpu.SMEM)] * 2 + [vmem] * 10,
        out_specs=[any_spec, any_spec, vmem, any_spec] + [vmem] * 9,
        out_shape=[
            shape((seq, width), BF), shape((seq, 3 * part), BF), shape((seq, part), BF), shape((4, local, LANES), F32),
            shape((local, width), BF), shape((local, width), F32), shape((seq, part), BF),
            shape((units // 4, width), F32), shape((width // 4, units), F32), shape((width // 8, units), F32),
            shape((part, width), F32), shape((8, width), F32), shape((1, units), F32),
        ],
        scratch_shapes=[
            wide(16, width), wide(1, units), low(seq, width), low(seq, units), low(seq, units), low(seq, width), low(seq, units),
            wide(local, width), wide(local, width), wide(local, width), wide(local, LANES),
            wide(2 * local, width), low(2 * local, width), low(2 * local, width), low(local, width),
            low(local, width), wide(64, width), wide(8, units),
            wide(width // 4, units), low(units // 2, width), low(units // 2, width), low(units // 4, width),
            low(width // 4, units), low(width // 4, units), low(width // 8, units),
            dma(copies), dma(copies), dma(5), dma(5), dma(6),
        ],
        compiler_params=pltpu.CompilerParams(collective_id=0, has_side_effects=True, vmem_limit_bytes=63 << 20),
        cost_estimate=pl.CostEstimate(
            flops=16 * seq * width * units, bytes_accessed=50 << 20, transcendentals=2 * seq * units
        ),
        name="ahead",
    )(lengths, offset, tokens, cot, w3, wout, w1, w2, biases, ln_gain, ln_bias, qv_bias)


ORDER = {
    "start": (("o", 0), ("2", 2),),
    3: (("q", 2),),
    4: (("o", 1),),
    5: (("p", 1),),
    6: (("2", 3), ("a", 0),),
    8: (("o", 2),),
    9: (("q", 3), ("p", 2),),
    11: (("2", 4),),
    12: (("q", 4), ("o", 3), ("b", 0),),
    "x0": (("p", 3), ("2", 5),),
    "x1": (("a", 1),),
    "x2": (("p", 4), ("b", 1),),
    "x3": (("a", 2),),
    "n0": (("p", 5),),
    "near": (("b", 2),),
    "far": (("a", 3), ("q", 5),),
    "end": (("b", 3),),
}


def back_kernel(
    lengths, offset, qkv_in, o_in, do_in, lse_in, xfull_in, w3, ghid_in, tokens_in, ln_gain, w2q, w1p, w1q, wog_in, sums_in, b1_in,
    tgrad, w2f, w1f, wof, wqt, small_out,
    qkv, o_ref, do_ref, lse_col, xfull, ghid, tokens, lse_s, qm_s, dom_s, dqt_s, delta_s, gp, w_in, wq, wqf, wog, pbuf, cs, cr, xs, xr, gs, acc,
    s2w, r2w, spz, spw, rpz, rpw, s1q, r1q, soy, soz, roy, roz, say, saz, ray, raz, small, near, far,
    send, recv, dsend, drecv, nsend, nrecv, fsend, frecv, lsem,
):
    local, width = tokens.shape
    seq, part = o_ref.shape
    heads = part // HEAD
    spans = spans_of(local)
    count = len(spans)
    pair = part // 2
    moves = [
        pltpu.make_async_copy(src, dst, lsem.at[i])
        for i, (src, dst) in enumerate(
            (
                (qkv_in, qkv), (do_in, do_ref), (o_in, o_ref), (lse_in, lse_col), (xfull_in, xfull), (ghid_in, ghid),
                (tokens_in, tokens),
            )
        )
    ] + [
        pltpu.make_async_copy(
            w3.at[t, :, i * pair:(i + 1) * pair], w_in.at[:, (3 * i + t) * pair:(3 * i + t + 1) * pair],
            lsem.at[7 + 3 * i + t],
        )
        for i in range(2)
        for t in range(3)
    ]
    for move in moves:
        move.start()
    dp, me = lax.axis_index("dp"), lax.axis_index("mp")
    mx, mc = me // 2, me % 2
    owner = {0: me, 1: mx * 2 + 1 - mc, 2: (1 - mx) * 2 + mc, 3: (1 - mx) * 2 + 1 - mc}
    peer_core, peer_x, peer_far = (dp, owner[1]), (dp, owner[2]), (dp, owner[3])
    near_peers = (peer_core, peer_x, peer_far)
    far_peers = tuple(((dp + i) % 8, me) for i in range(1, 8))
    barrier = pltpu.get_barrier_semaphore()
    for peer in near_peers + far_peers:
        pl.semaphore_signal(barrier, inc=1, device_id=peer, device_id_type=MESH)
    pl.semaphore_wait(barrier, 10)

    half = w1f.shape[0] // 2
    streams = {
        "2": Reduction(w2f.shape[0], w2q, 2, 2, (None, None, s2w), (None, None, r2w), w2f, dsend, drecv, 0),
        "p": Reduction(half, w1p, 1, 1, (None, spz, spw), (None, rpz, rpw), w1f.at[0:half], dsend, drecv, 6),
        "q": Reduction(
            half, w1q, 2, 2, (None, None, s1q), (None, None, r1q), w1f.at[half:2 * half], dsend, drecv, 12,
            order=(1, 2, 0),
        ),
        "o": Direct(part, wog, (soy, soz), (roy, roz), wof, dsend, drecv, 18),
        "a": Direct(3 * pair, wq.at[0], (say.at[0], saz.at[0]), (ray.at[0], raz.at[0]), wqf.at[0], dsend, drecv, 26),
        "b": Direct(3 * pair, wq.at[1], (say.at[1], saz.at[1]), (ray.at[1], raz.at[1]), wqf.at[1], dsend, drecv, 34),
    }

    b0, b1, b2 = edges(lengths, offset)
    gain0 = ln_gain[...].astype(F32)[0:1, :]
    lo_edge, hi_edge, _, _, cut = plan(seq)
    lane = lax.broadcasted_iota(jnp.int32, (1, pair), 1)

    def mask_of(h):
        return (lane // HEAD) == h % 2

    def cols_of(h):
        return pl.ds(pl.multiple_of(h // 2 * pair, pair), pair)

    def grad_cols(h, t):
        return pl.ds(pl.multiple_of(h // 2 * 3 * pair + t * pair, pair), pair)

    def prepare(h):
        mine, cols = mask_of(h), cols_of(h)
        qm_s[...] = jnp.where(mine, qkv[:, cols].astype(F32) * HEAD**-0.5, 0.0).astype(BF)
        dom_s[...] = jnp.where(mine, do_ref[:, cols], jnp.zeros((), BF))
        ones = jnp.ones((8, pair), F32)
        for a, b in cut(0, seq, 256):
            prod = dom_s[a:b, :].astype(F32) * o_ref[a:b, cols].astype(F32)
            delta_s[:, a:b] = lax.dot_general(
                ones, prod, NT, preferred_element_type=F32, precision=lax.Precision.HIGHEST
            )
        dqt_s[...] = jnp.zeros_like(dqt_s)

    def key_blocks(h, blocks):
        mine = mask_of(h)
        key_cols, value_cols = (pl.ds(pl.multiple_of(t * part + h // 2 * pair, pair), pair) for t in (1, 2))
        for a, b, stop in blocks:
            n = b - a
            kk = qkv[a:b, key_cols]
            vv = qkv[a:b, value_cols]
            kpos = a + lax.broadcasted_iota(jnp.int32, (n, 1), 0)
            kh = jnp.where(mine, kk, jnp.zeros((), BF))
            pts, dsts = [], []
            for c, d in cut(a, stop, 128):
                st = lax.dot_general(kk, qm_s[c:d, :], NT, preferred_element_type=F32)
                pt = jnp.exp(st - lse_s[h, 0:1, c:d])
                if not free_of_mask(a, b, c, d, seq):
                    qpos = c + lax.broadcasted_iota(jnp.int32, (1, d - c), 1)
                    first = seg_start(qpos, b0, b1, b2)
                    pt = jnp.where((kpos >= first) & (kpos <= qpos), pt, 0.0)
                dpt = lax.dot_general(vv, dom_s[c:d, :], NT, preferred_element_type=F32)
                pts.append(pt.astype(BF))
                dsts.append((pt * (dpt - delta_s[0:1, c:d])).astype(BF))
            pt = jnp.concatenate(pts, axis=1)
            dst = jnp.concatenate(dsts, axis=1)
            dv = jnp.dot(pt, dom_s[a:stop, :], preferred_element_type=F32)
            dk = jnp.dot(dst, qm_s[a:stop, :], preferred_element_type=F32)
            gv, gk = grad_cols(h, 2), grad_cols(h, 1)
            gp[a:b, gv] = jnp.where(mine, dv.astype(BF), gp[a:b, gv])
            gp[a:b, gk] = jnp.where(mine, dk.astype(BF), gp[a:b, gk])
            dqt_s[:, a:stop] += lax.dot_general(kh, dst, TN, preferred_element_type=F32)

    def finish_queries(h):
        mine, gq = mask_of(h), grad_cols(h, 0)
        for a, b in cut(0, seq, 128):
            dq = (dqt_s[:, a:b] * HEAD**-0.5).T
            gp[a:b, gq] = jnp.where(mine, dq.astype(BF), gp[a:b, gq])

    def input_grad(i):
        wq[i] = lax.dot_general(
            gp[:, i * 3 * pair:(i + 1) * 3 * pair], xfull[...], TN, preferred_element_type=F32
        )

    def turn(i):
        for t in range(3):
            wqt[t, :, i * pair:(i + 1) * pair] = wqf[i, t * pair:(t + 1) * pair, :].T

    def run(point):
        for name, step in ORDER.get(point, ()):
            if step == 0 and name in "ab":
                input_grad("ab".index(name))
            streams[name].step(step)

    wog[...] = wog_in[...]
    run("start")
    gp[...] = jnp.zeros_like(gp)
    for move in moves:
        move.wait()
    for a, b in cut(0, seq, LANES):
        turned = lse_col[a:b, :].T
        for h in range(heads):
            lse_s[h, 0:1, a:b] = turned[h:h + 1, :]

    groups = (
        [(a, b, hi_edge) for a, b in cut(0, lo_edge, 256)][:2],
        [(a, b, hi_edge) for a, b in cut(0, lo_edge, 256)][2:] + [(a, b, seq) for a, b in cut(lo_edge, hi_edge, 256)],
        [(a, b, seq) for a, b in cut(hi_edge, seq, 256)],
    )

    def one_head(h, carry):
        prepare(h)
        for g, blocks in enumerate(groups):
            key_blocks(h, blocks)
            if g == 2:
                finish_queries(h)
            for k in range(heads):
                if (3 * k + g + 1) in ORDER:

                    @pl.when(h == k)
                    def _(k=k, g=g):
                        run(3 * k + g + 1)

        return carry

    lax.fori_loop(0, heads, one_head, 0)

    def remote(src, dst, kind, c, device):
        i = kind * count + c
        return pltpu.make_async_remote_copy(
            src_ref=src, dst_ref=dst, send_sem=send.at[i], recv_sem=recv.at[i], device_id=device, device_id_type=MESH
        )

    def core_copy(c):
        lo, hi = spans[c]
        rows = pl.ds(2 * lo, 2 * (hi - lo))
        return remote(cs.at[rows], cr.at[rows], 0, c, peer_core)

    def x_copy(c):
        lo, hi = spans[c]
        rows = pl.ds(lo, hi - lo)
        return remote(xs.at[rows], xr.at[rows], 1, c, peer_x)

    def project(c):
        lo, hi = spans[c]
        r = hi - lo
        for half in range(2):
            out = pl.ds(2 * lo, 2 * r)
            for s, j in enumerate(((1, 3), (2, 0))[half]):
                src = pl.ds(pl.multiple_of(owner[j] * local + lo, 16), r)
                gs[s * r:(s + 1) * r, :] = gp[src, :]

            def body(n, carry):
                cols = pl.ds(pl.multiple_of(n * TILE, TILE), TILE)
                value = lax.dot_general(gs[0:2 * r, :], w_in[cols, :], NT, preferred_element_type=F32)
                if half == 0:
                    cs[out, cols] = value.astype(BF)
                else:
                    pbuf[out, cols] = value
                return carry

            lax.fori_loop(0, width // TILE, body, 0)
            if half == 0:
                core_copy(c).start()

    def pass_on(c):
        lo, hi = spans[c]
        r = hi - lo
        core_copy(c).wait_recv()
        xs[lo:hi, :] = (pbuf[2 * lo:2 * lo + r, :] + cr[2 * lo + r:2 * lo + 2 * r, :].astype(F32)).astype(BF)
        x_copy(c).start()

    project(0)
    for c in range(count):
        if c + 1 < count:
            project(c + 1)
        pass_on(c)
        run("x%d" % c)

    acc[...] = jnp.zeros_like(acc)
    for c in range(count):
        x_copy(c).wait_recv()
        lo, hi = spans[c]
        r = hi - lo
        step = next(t for t in (48, 64, 32, 16) if r % t == 0)

        def pulls(i, carry):
            kept = pl.ds(pl.multiple_of(2 * lo + r + i * step, 16), step)
            close = pl.ds(pl.multiple_of(2 * lo + i * step, 16), step)
            rows = pl.ds(pl.multiple_of(lo + i * step, 16), step)
            total = pbuf[kept, :] + cr[close, :].astype(F32) + xr[rows, :].astype(F32)
            unit, inv = norm_stats(tokens[rows, :].astype(F32))
            acc[0:8, :] += fold8(total * unit)
            acc[8:16, :] += fold8(total)
            tgrad[rows, :] = (ghid[rows, :] + norm_pull(total, gain0, unit, inv)).astype(BF)
            return carry

        lax.fori_loop(0, r // step, pulls, 0)
        run("n%d" % c)

    small[...] = jnp.zeros_like(small)
    small[2:10, :] = sums_in[...]
    small[10:11, :] = b1_in[...]
    small[0:1, :] = jnp.sum(acc[0:8, :], axis=0, keepdims=True)
    small[1:2, :] = jnp.sum(acc[8:16, :], axis=0, keepdims=True)
    bias = jnp.sum(gp[...].astype(F32), axis=0, keepdims=True)
    for i in range(2):
        for t in range(2):
            at = (3 * i + 2 * t) * pair
            small[11:12, t * part + i * pair:t * part + (i + 1) * pair] = bias[:, at:at + pair]

    def near_copy(i):
        return pltpu.make_async_remote_copy(
            src_ref=small, dst_ref=near.at[me], send_sem=nsend.at[i], recv_sem=nrecv.at[i], device_id=near_peers[i],
            device_id_type=MESH,
        )

    def far_copy(i):
        return pltpu.make_async_remote_copy(
            src_ref=small_out, dst_ref=far.at[dp], send_sem=fsend.at[i], recv_sem=frecv.at[i], device_id=far_peers[i],
            device_id_type=MESH,
        )

    for i in range(3):
        near_copy(i).start()
    run("near")
    for i in range(3):
        near_copy(i).wait_recv()
    own = lax.broadcasted_iota(jnp.int32, (16, 1), 0) >= 10
    near[me] = small[...]
    small_out[...] = jnp.where(own, small[...], ((near[0] + near[1]) + near[2]) + near[3])
    for i in range(7):
        far_copy(i).start()
    run("far")
    for i in range(7):
        far_copy(i).wait_recv()
    for i in range(7):
        far_copy(i).wait_send()
    far[dp] = small_out[...]
    total = far[0]
    for i in range(1, 8):
        total = total + far[i]
    small_out[...] = total
    run("end")
    for name in ("a", "b"):
        streams[name].arrive(3)
        turn("ab".index(name))

    for name in ("2", "p", "q", "o"):
        streams[name].arrive(streams[name].steps - 1)
    for stream in streams.values():
        stream.drain()
    for i in range(3):
        near_copy(i).wait_send()
    for c in range(count):
        core_copy(c).wait_send()
        x_copy(c).wait_send()


def back(lengths, offset, qkv, o, do, lse, xfull, w3, ghid, tokens, ln_gain, w2q, w1p, w1q, wog, sums, b1_part):
    seq, part = o.shape
    local, width = tokens.shape
    units = w1p.shape[1]
    pair = part // 2
    vmem = pl.BlockSpec(memory_space=pltpu.VMEM)
    shape = jax.ShapeDtypeStruct
    low = lambda *dims: pltpu.VMEM(dims, BF)
    wide = lambda *dims: pltpu.VMEM(dims, F32)
    dma = lambda n: pltpu.SemaphoreType.DMA((n,))
    return pl.pallas_call(
        back_kernel,
        in_specs=[pl.BlockSpec(memory_space=pltpu.SMEM)] * 2 + [pl.BlockSpec(memory_space=pl.ANY)] * 8 + [vmem] * 7,
        out_specs=[vmem] * 6,
        out_shape=[
            shape((local, width), BF), shape((4 * w2q.shape[0], width), BF), shape((width, units), BF),
            shape((part, width), BF), shape((3, width, part), BF), shape((16, width), F32),
        ],
        scratch_shapes=[
            low(seq, 3 * part), low(seq, part), low(seq, part), wide(seq, LANES), low(seq, width),
            wide(local, width), low(local, width), wide(part // HEAD, 8, seq), low(seq, pair), low(seq, pair), wide(pair, seq), wide(8, seq), low(seq, 3 * part), low(width, 3 * part),
            wide(2, 3 * pair, width), low(2, 3 * pair, width), wide(part, width), wide(2 * local, width), low(2 * local, width),
            low(2 * local, width), low(local, width), low(local, width), low(seq // 6 // 16 * 16, 3 * part), wide(16, width),
            low(units // 8, width), low(units // 8, width), low(width // 8, units), low(width // 16, units),
            low(width // 8, units), low(width // 16, units), low(width // 16, units), low(width // 16, units),
            low(part // 2, width), low(part // 2, width), low(part // 2, width), low(3 * part // 8, width),
            low(2, 3 * pair // 2, width), low(2, 3 * pair // 2, width), low(2, 3 * pair // 2, width),
            low(2, 9 * pair // 8, width),
            wide(16, width), wide(4, 16, width), wide(8, 16, width),
            dma(8), dma(8), dma(42), dma(42), dma(3), dma(3), dma(7), dma(7), dma(13),
        ],
        compiler_params=pltpu.CompilerParams(collective_id=1, has_side_effects=True, vmem_limit_bytes=63 << 20),
        cost_estimate=pl.CostEstimate(flops=20 << 30, bytes_accessed=40 << 20, transcendentals=8 << 20),
        name="back",
    )(lengths, offset, qkv, o, do, lse, xfull, w3, ghid, tokens, ln_gain, w2q, w1p, w1q, wog, sums, b1_part)


def finish_kernel(
    w2f, w1f, wof, wqt, small, tgrad_in, mixed_in, w2o, w1o, woo, wqo, gains, shifts, out_bias, b2, b1, qv, tgrad,
    mixed,
):
    tgrad[...] = tgrad_in[...]
    mixed[...] = mixed_in[...]
    w2o[...] = w2f[...].astype(F32)
    w1o[...] = w1f[...].astype(F32)
    woo[...] = wof[...].astype(F32)
    wqo[...] = wqt[...].astype(F32)
    part = qv.shape[1]
    gains[0:1, :] = small[0:1, :]
    gains[1:4, :] = small[2:5, :]
    shifts[0:1, :] = small[1:2, :]
    shifts[1:4, :] = small[5:8, :]
    out_bias[...] = small[8:9, :]
    b2[...] = small[9:10, :]
    b1[...] = small[10:11, :]
    qv[0:1, :] = small[11:12, 0:part]
    qv[1:2, :] = small[11:12, part:2 * part]


def finish(w2f, w1f, wof, wqt, small, tgrad, mixed):
    parts = 4
    shape = jax.ShapeDtypeStruct
    part = wof.shape[0]
    halves = pl.BlockSpec((tgrad.shape[0] // 2, tgrad.shape[1]), lambda i: (i * 2 // parts, 0))
    rows = lambda a: pl.BlockSpec((a.shape[0] // parts, a.shape[1]), lambda i: (i, 0))
    turned = pl.BlockSpec((3, wqt.shape[1] // parts, part), lambda i: (0, i, 0))
    fixed = lambda n, m: pl.BlockSpec((n, m), lambda i: (0, 0))
    width, units = w2f.shape[1], w1f.shape[1]
    return pl.pallas_call(
        finish_kernel,
        grid=(parts,),
        in_specs=[rows(w2f), rows(w1f), rows(wof), turned, fixed(*small.shape), halves, halves],
        out_specs=[
            rows(w2f), rows(w1f), rows(wof), turned, fixed(4, width), fixed(4, width), fixed(1, width),
            fixed(1, width), fixed(1, units), fixed(2, part), halves, halves,
        ],
        out_shape=[
            shape(w2f.shape, F32), shape(w1f.shape, F32), shape(wof.shape, F32), shape(wqt.shape, F32),
            shape((4, width), F32), shape((4, width), F32), shape((1, width), F32), shape((1, width), F32),
            shape((1, units), F32), shape((2, part), F32), shape(tgrad.shape, BF), shape(mixed.shape, BF),
        ],
        compiler_params=pltpu.CompilerParams(vmem_limit_bytes=56 << 20),
        name="finish",
    )(w2f, w1f, wof, wqt, small, tgrad, mixed)


def shards(
    tokens, caption_len, row_offset, wqkv, qv_bias, wout, out_bias, w1, b1, w2, b2, ln_gain, ln_bias, cotangent,
):
    local_rows, width = tokens.shape
    head_part = wqkv.shape[2]
    here = lax.axis_size("dp") == 8 and lax.axis_size("mp") == 4 and head_part == TILE
    if not (here and width == w1.shape[1] == 1024 and local_rows % 32 == 0):
        return shards_by_ops(
            tokens, caption_len, row_offset, wqkv, qv_bias, wout, out_bias, w1, b1, w2, b2, ln_gain, ln_bias,
            cotangent,
        )
    w3 = wqkv.transpose(1, 0, 2)
    (
        xfull, qkv, heads, lse, mixed, grad_hidden, grad_heads, w2_part, w1_first, w1_last, wout_part, sums, b1_part,
    ) = ahead(
        caption_len, row_offset, tokens, cotangent, w3, wout, w1, w2,
        jnp.concatenate([out_bias, b2, b1]).reshape(3, width), ln_gain, ln_bias, qv_bias,
    )
    tokens_grad, w2_grad, w1_grad, wout_grad, wqkv_grad, small = back(
        caption_len, row_offset, qkv, heads, grad_heads, lse.reshape(-1, LANES), xfull, w3, grad_hidden, tokens,
        ln_gain, w2_part, w1_first, w1_last, wout_part, sums, b1_part,
    )
    (
        w2_grad, w1_grad, wout_grad, wqkv_grad, gain_grad, shift_grad, out_bias_grad, b2_grad, b1_grad, qv_grad,
        tokens_grad, mixed,
    ) = finish(w2_grad, w1_grad, wout_grad, wqkv_grad, small, tokens_grad, mixed)
    return (
        mixed, tokens_grad, wqkv_grad.transpose(1, 0, 2), qv_grad, wout_grad, out_bias_grad[0], w1_grad, b1_grad[0],
        w2_grad, b2_grad[0], gain_grad, shift_grad,
    )


def solution(mesh):
    rows = P(("dp", "mp"), None)
    placed = (
        rows, P("dp", None), P("dp"), P(None, None, "mp"), P(None, "mp"), P("mp", None), P(), P(None, "mp"),
        P("mp"), P("mp", None), P(), P(), P(), rows,
    )
    return jax.shard_map(
        shards,
        mesh=mesh,
        in_specs=placed,
        out_specs=(
            rows, rows, P(None, None, "mp"), P(None, "mp"), P("mp", None), P(), P(None, "mp"), P("mp"),
            P("mp", None), P(), P(), P(),
        ),
        check_vma=False,
    )
```
